128 devices in a mesh: pipe: 2 (over x_lo), dp: 32 (over x_hi, z, y), tensor: 2 (over core).
Axes of the slice: x: 4 (x_hi: 2, x_lo: 2; x = x_hi * 2 + x_lo), y: 4, z: 4, core: 2. Of those that a mesh axis runs over, the one named last changes fastest.
Arguments:
- inputs: bfloat16 [2, 4096, 896], P(None, ('dp', 'tensor')), may hold values from -16 to 16
- cotangent: bfloat16 [2, 4096, 896], P(None, ('dp', 'tensor')), may hold values from -16 to 16
- lengths: int32 [2, 32, 4], P(None, 'dp'), may hold values from 0 to 128, as said below
- gain_attn: bfloat16 [2, 896], P('pipe'), may hold values from 0.099609375 to 1.8984375
- w_query: bfloat16 [2, 896, 896], P('pipe', None, 'tensor'), may hold values from -0.1875 to 0.1875
- b_query: bfloat16 [2, 896], P('pipe', 'tensor'), may hold values from -3 to 3
- w_keyval: bfloat16 [2, 896, 2, 128], P('pipe', None, 'tensor'), may hold values from -0.1875 to 0.1875
- b_keyval: bfloat16 [2, 2, 128], P('pipe', 'tensor'), may hold values from -3 to 3
- w_out: bfloat16 [2, 896, 896], P('pipe', 'tensor'), may hold values from -0.75 to 0.75
- gain_mlp: bfloat16 [2, 896], P('pipe'), may hold values from 0.099609375 to 1.8984375
- w_gate_up: bfloat16 [2, 896, 2, 4864], P('pipe', None, None, 'tensor'), may hold values from -0.1875 to 0.1875
- w_down: bfloat16 [2, 4864, 896], P('pipe', 'tensor'), may hold values from -0.078125 to 0.078125
Outputs:
- section_out: bfloat16 [2, 2, 4096, 896], P('pipe', None, ('dp', 'tensor'))
- input_grad: float32 [2, 2, 4096, 896], P('pipe', None, ('dp', 'tensor'))
- grad_gain_attn: float32 [2, 896], P('pipe')
- grad_w_query: float32 [2, 896, 896], P('pipe', 'dp', 'tensor')
- grad_b_query: float32 [2, 896], P('pipe')
- grad_w_keyval: float32 [2, 896, 2, 128], P('pipe', 'dp', 'tensor')
- grad_b_keyval: float32 [2, 2, 128], P('pipe')
- grad_w_out: float32 [2, 896, 896], P('pipe', 'tensor', 'dp')
- grad_gain_mlp: float32 [2, 896], P('pipe')
- grad_w_gate_up: float32 [2, 896, 2, 4864], P('pipe', 'dp', None, 'tensor')
- grad_w_down: float32 [2, 4864, 896], P('pipe', 'tensor', 'dp')
The draws below stay inside these ranges and needn't reach their ends.
Inputs may be any that keep to these rules, and one draw needn't show every extreme that they name: In every micro-batch the lengths of one rank sum to more than 64 and at most 128; each rank's first sequence is longer than 64; in every micro-batch some rank holds a single sequence of exactly 128; later lengths may be 0.
All inputs are finite; a program needn't handle non-finite values.
Results may differ from the reference program's by a relative error of at most 0.03.
Values may be sent and summed in bfloat16 or wider, within the bound.
A program may use at most 256 MiB of HBM per device.

```python
import jax
import jax.numpy as jnp
from jax import lax

D = 896
HEADS = 14
KV_HEADS = 2
HEAD = 64
FF = 4864
CAP = 128
SEQS = 4
MICRO = 2
SECTIONS = 2
TOKENS = 4096


def draw_lengths(key, part):
    key = jax.random.fold_in(key, 11)
    rank_count = TOKENS // CAP
    subkeys = jax.random.split(key, 4)
    totals = jax.random.randint(subkeys[0], (MICRO, rank_count), CAP // 2 + 1, CAP + 1)
    chosen = jax.random.randint(subkeys[1], (MICRO, 1), 0, rank_count)
    filled = jnp.arange(rank_count)[None, :] == chosen
    totals = jnp.where(filled, CAP, totals)
    leading = jax.random.randint(subkeys[2], (MICRO, rank_count), CAP // 2 + 1, CAP + 1)
    leading = jnp.where(filled, CAP, jnp.minimum(leading, totals))
    remainder = totals - leading
    cut_points = jax.random.randint(subkeys[3], (MICRO, rank_count, SEQS - 2), 0, CAP + 1)
    cut_points = jnp.sort(cut_points * (remainder[..., None] + 1) // (CAP + 1), axis=-1)
    boundaries = jnp.concatenate([jnp.zeros((MICRO, rank_count, 1), jnp.int32), cut_points.astype(jnp.int32), remainder[..., None].astype(jnp.int32)], axis=-1)
    pieces = boundaries[..., 1:] - boundaries[..., :-1]
    return jnp.concatenate([leading[..., None].astype(jnp.int32), pieces], axis=-1).astype(jnp.int32)


def spiked(entries, rng, source, target, parts, factor):
    owner, partner = [(jnp.arange(entries.shape[dim]) // (entries.shape[dim] // parts)).reshape([-1 if axis == dim else 1 for axis in range(entries.ndim)]) for dim in (source, target)]
    chosen = jax.random.permutation(rng, parts)[partner]
    strong = (owner == chosen) | (owner == (partner + parts // 2) % parts)
    return jnp.where(strong, factor * entries, entries)


def shard_levels(key, shape, cuts, least, high):
    level, own = 1.0, jax.random.fold_in(key, 6)
    for dim, blocks in cuts:
        draws = jnp.exp(jax.random.uniform(jax.random.fold_in(own, dim), (blocks,), jnp.float32, least / len(cuts), high / len(cuts)))
        level = level * jnp.repeat(draws, shape[dim] // blocks).reshape([-1 if axis == dim else 1 for axis in range(len(shape))])
    return level


def bell_draw(stream_key, extent, spread, most, cuts=(), held_as=jnp.bfloat16):
    result = spread * jax.random.normal(stream_key, extent, jnp.float32)
    if cuts:
        result = result * shard_levels(stream_key, extent, cuts, -0.22, 0.18)
    return jnp.clip(result, -most, most).astype(held_as)


def bell_draw_with(rng, shape, scale, most, cuts, heavy, held_as=jnp.bfloat16):
    array = scale * jax.random.normal(rng, shape, jnp.float32)
    if cuts:
        array = array * shard_levels(rng, shape, cuts, -0.22, 0.18)
    return jnp.clip(spiked(array, jax.random.fold_in(rng, 3), *heavy), -most, most).astype(held_as)


def setup_inputs(seed: int = 0) -> dict:
    streams_of = jax.random.split(jax.random.key(seed), 13)
    inputs = bell_draw_with(streams_of[0], (MICRO, TOKENS, D), 1.0, 16.0, ((1, 64),), (1, 2, 64, 4.0))
    cotangent = bell_draw_with(streams_of[1], (MICRO, TOKENS, D), 1.0, 16.0, ((1, 64),), (1, 2, 64, 4.0))
    lengths = draw_lengths(jax.random.fold_in(streams_of[12], 71), 0)
    gain_attn = jnp.clip(1.0 + 0.18 * jax.random.normal(streams_of[3], (SECTIONS, D), jnp.float32), 0.099609375, 1.8984375).astype(jnp.bfloat16)
    w_query = bell_draw(streams_of[4], (SECTIONS, D, HEADS * HEAD), D ** -0.5, 0.1875, ((0, 2), (2, 2)))
    b_query = bell_draw(streams_of[5], (SECTIONS, HEADS * HEAD), 0.5, 3.0, ((0, 2), (1, 2)))
    w_keyval = bell_draw(streams_of[6], (SECTIONS, D, KV_HEADS, 2 * HEAD), D ** -0.5, 0.1875, ((0, 2), (2, 2)))
    b_keyval = bell_draw(streams_of[7], (SECTIONS, KV_HEADS, 2 * HEAD), 0.5, 3.0, ((0, 2), (1, 2)))
    w_out = bell_draw(streams_of[8], (SECTIONS, HEADS * HEAD, D), (HEADS * HEAD // 16) ** -0.5, 0.75, ((0, 2), (1, 2)))
    gain_mlp = jnp.clip(1.0 + 0.18 * jax.random.normal(streams_of[9], (SECTIONS, D), jnp.float32), 0.099609375, 1.8984375).astype(jnp.bfloat16)
    w_gate_up = bell_draw(streams_of[10], (SECTIONS, D, 2, FF), D ** -0.5, 0.1875, ((0, 2), (3, 2)))
    w_down = bell_draw(streams_of[11], (SECTIONS, FF, D), FF ** -0.5, 0.078125, ((0, 2), (1, 2)))
    return {"inputs": inputs, "cotangent": cotangent, "lengths": lengths, "gain_attn": gain_attn, "w_query": w_query, "b_query": b_query, "w_keyval": w_keyval, "b_keyval": b_keyval, "w_out": w_out, "gain_mlp": gain_mlp, "w_gate_up": w_gate_up, "w_down": w_down}


@jax.custom_vjp
def low(v):
    return lax.optimization_barrier(v.astype(jnp.bfloat16)).astype(jnp.float32)

@jax.custom_vjp
def low_back(v):
    return v

def low_keep(v):
    return (low(v), None)

def low_pass(kept, grad):
    return (grad,)

def back_keep(v):
    return (v, None)

def back_low(kept, grad):
    return (low(grad),)
low.defvjp(low_keep, low_pass)
low_back.defvjp(back_keep, back_low)
EPS = 1e-06
THETA = 1000000.0

def matmul(left, right):
    return jnp.dot(left, right, precision=lax.Precision.HIGHEST)

def layout(rank_lengths):
    seq_ends = jnp.cumsum(rank_lengths).astype(jnp.int32)
    seq_starts = (seq_ends - rank_lengths).astype(jnp.int32)
    slot_index = jnp.arange(CAP, dtype=jnp.int32)
    segment = lax.optimization_barrier(jnp.sum((slot_index[:, None] >= seq_ends[None, :]).astype(jnp.int32), axis=1)).astype(jnp.int32)
    starts_all = jnp.concatenate([seq_starts, seq_ends[-1:]]).astype(jnp.int32)
    one_hot = (segment[:, None] == jnp.arange(SEQS + 1, dtype=jnp.int32)[None, :]).astype(jnp.int32)
    slot_start = lax.optimization_barrier(jnp.sum(one_hot * starts_all[None, :], axis=1)).astype(jnp.int32)
    return (segment, (slot_index - slot_start).astype(jnp.int32))

def rotary_angles(position):
    half_width = HEAD // 2
    frequency = THETA ** (-(jnp.arange(half_width, dtype=jnp.float32) * 2.0 / HEAD))
    phases = position.astype(jnp.float32)[:, None] * frequency[None, :]
    phases = jnp.concatenate([phases, phases], axis=1)
    return (jnp.cos(phases)[:, None, :], jnp.sin(phases)[:, None, :])

def rotate(values, cosine_table, sine_table):
    half_width = values.shape[-1] // 2
    turned = jnp.concatenate([-values[..., half_width:], values[..., :half_width]], axis=-1)
    return values * cosine_table + turned * sine_table

def rms_norm(values, gain):
    return values * lax.rsqrt(lax.optimization_barrier(jnp.mean(values * values, axis=-1, keepdims=True)) + EPS) * gain

def attention(queries, key_heads, values, segment):
    slot_index = jnp.arange(CAP, dtype=jnp.int32)
    allowed = (segment[:, None] == segment[None, :]) & (slot_index[None, :] <= slot_index[:, None])
    scores = jnp.einsum('igkd,jgd->gkij', queries, key_heads, precision=lax.Precision.HIGHEST) * HEAD ** (-0.5)
    scores = low_back(jnp.where(allowed, scores, -1e+30))
    soft_weights = low(jax.nn.softmax(scores, axis=-1))
    return jnp.einsum('gkij,jgd->igkd', soft_weights, values, precision=lax.Precision.HIGHEST)

def decoder_layer(stream, params, segment, position):
    gain_attn, w_query, b_query, w_keyval, b_keyval, w_out, gain_mlp, w_gate_up, w_down = params
    per_group = HEADS // KV_HEADS
    cosine_table, sine_table = rotary_angles(position)
    normed = low(rms_norm(stream, gain_attn))
    queries = low_back(matmul(normed, w_query) + b_query).reshape(CAP, HEADS, HEAD)
    keyval = low_back(jnp.einsum('id,dge->ige', normed, w_keyval, precision=lax.Precision.HIGHEST) + b_keyval)
    queries = low(rotate(queries, cosine_table, sine_table)).reshape(CAP, KV_HEADS, per_group, HEAD)
    key_heads = low(rotate(keyval[..., :HEAD], cosine_table, sine_table))
    values = low(keyval[..., HEAD:])
    mixture = jax.checkpoint(attention)(queries, key_heads, values, segment)
    mixture = low_back(low(mixture.reshape(CAP, HEADS * HEAD)))
    middle = stream + low_back(matmul(mixture, w_out))
    normed_two = low(rms_norm(middle, gain_mlp))
    gate_up = low_back(jnp.einsum('id,dgf->igf', normed_two, w_gate_up, precision=lax.Precision.HIGHEST))
    hidden = low(jax.nn.silu(gate_up[:, 0]) * gate_up[:, 1])
    return middle + low_back(matmul(hidden, w_down))

def reference(inputs, cotangent, lengths, gain_attn, w_query, b_query, w_keyval, b_keyval, w_out, gain_mlp, w_gate_up, w_down):
    weights = tuple((w.astype(jnp.float32) for w in (gain_attn, w_query, b_query, w_keyval, b_keyval, w_out, gain_mlp, w_gate_up, w_down)))
    rank_count = TOKENS // CAP
    blocks = inputs.astype(jnp.float32).reshape(MICRO * rank_count, CAP, D)
    upstream = cotangent.astype(jnp.float32).reshape(MICRO * rank_count, CAP, D)
    all_lengths = lengths.reshape(MICRO * rank_count, SEQS)

    def scan_step(totals, scan_item):
        rank_block, grad_block, rank_lengths = scan_item
        segment, position = layout(rank_lengths)
        live_rows = (segment < SEQS).astype(jnp.float32)[:, None]

        def two_sections(stream, probe_zero, params):
            first_section = tuple((w[0] for w in params))
            second_section = tuple((w[1] for w in params))
            middle = low_back(low(decoder_layer(stream, first_section, segment, position))) + probe_zero
            return (middle, decoder_layer(middle, second_section, segment, position))
        (middle, final), pullback = jax.vjp(two_sections, rank_block, jnp.zeros_like(rank_block), weights)
        grad_stream, grad_probe, grad_params = pullback((jnp.zeros_like(middle), grad_block * live_rows))
        totals = jax.tree.map(lambda a, b: a + b, totals, grad_params)
        return (totals, (middle, final, grad_stream, grad_probe))
    zero_grads = tuple((jnp.zeros_like(w) for w in weights))
    totals, (middle, final, grad_stream, grad_probe) = lax.scan(scan_step, zero_grads, (blocks, upstream, all_lengths))
    out_shape = (MICRO, TOKENS, D)
    section_out = jnp.stack([middle.reshape(out_shape), final.reshape(out_shape)]).astype(jnp.bfloat16)
    input_grad = jnp.stack([grad_stream.reshape(out_shape), grad_probe.reshape(out_shape)])
    return (section_out, input_grad, totals[0], totals[1], totals[2], totals[3], totals[4], totals[5], totals[6], totals[7], totals[8])
```

```python
import functools

import jax
import jax.numpy as jnp
import numpy as np
from jax import lax
from jax.experimental import pallas as pl
from jax.experimental.pallas import tpu as pltpu
from jax.sharding import PartitionSpec as P

D = 896
HEADS = 14
HEAD = 64
CAP = 128
SEQS = 4
MICRO = 2
ROWS = MICRO * CAP
OWN = CAP // 2
FH = 2432
QW = 448
EPS = 1e-06
THETA = 1000000.0
MIB = 1024 * 1024

BF = jnp.bfloat16
F32 = jnp.float32
MESH = pl.DeviceIdType.MESH
VMEM = pltpu.VMEM

UP_A = 640
A_UP = FH
A_OUT = FH + UP_A
A_QKV = A_OUT + 512
HALF = A_QKV + 640
B_UP = FH
assert HALF == FH + FH - UP_A
TILES = ((0, 512), (512, 512), (1024, 512), (1536, 512), (2048, 384))
WIDE = ((0, 256), (256, 256), (512, 256), (768, 128))


def nn(a, b):
    return lax.dot_general(a, b, (((1,), (0,)), ((), ())), preferred_element_type=F32)


def nt(a, b):
    return lax.dot_general(a, b, (((1,), (1,)), ((), ())), preferred_element_type=F32)


def tn(a, b):
    return lax.dot_general(a, b, (((0,), (0,)), ((), ())), preferred_element_type=F32)


def rope_table():
    half = HEAD // 2
    frequency = np.power(np.float32(THETA), -(np.arange(half, dtype=np.float32) * np.float32(2.0 / HEAD)))
    phases = (np.arange(CAP, dtype=np.float32)[:, None] * frequency[None, :].astype(np.float32)).astype(np.float32)
    phases = phases.astype(np.float64)
    cosine = np.concatenate([np.cos(phases)] * 4, axis=1).astype(np.float32)
    sine = np.concatenate([-np.sin(phases), np.sin(phases)] * 2, axis=1).astype(np.float32)
    parts = []
    for table in (cosine, sine):
        rest = table
        for _ in range(3):
            piece = rest.astype(jnp.bfloat16)
            parts.append(piece)
            rest = rest - piece.astype(np.float32)
    return np.concatenate(parts, axis=1)


def row_orders():
    index = np.arange(D)
    first, second, x_hi, k = index // 224, index // 56 % 4, index // 28 % 2, index % 28
    orders = []
    for y, z in ((first, second), (second, first)):
        source = (x_hi * 16 + z * 4 + y) * 28 + k
        orders.append((source[:, None] == np.arange(D)[None, :]).astype(jnp.bfloat16))
    return np.stack(orders)


def turn(block, lane):
    low = (lane & 63) < 32
    return jnp.where(low, pltpu.roll(block, 96, 1), pltpu.roll(block, 32, 1))


def layer_kernel(
    len_ref, x_ref, cot_ref, g1_ref, g2_ref, b_ref, tab_ref,
    wq_hbm, wkv_hbm, wo_hbm, wgu_hbm, wd_hbm, perm_hbm,
    so_ref, ig_ref, ga_ref, gb_ref, small_ref,
    wqkv, wo, wgu, wd, perm, xbuf, gbuf, e1s, e1r, e2s, e2r, e3s, e3r, e4s, e4r, pipe_out,
    n1, n2, qb, kb, vb, pmat, mix, middle, gate, up, hidden, dgate, dup, lt, part, gmid, cs, allow,
    gqkv, load_sem, send_sem, recv_sem,
):
    pipe = lax.axis_index("pipe")
    t = lax.axis_index("tensor")
    other = 1 - t

    loads = [
        pltpu.make_async_copy(wq_hbm, wqkv.at[pl.ds(0, QW)], load_sem.at[0]),
        pltpu.make_async_copy(wkv_hbm, wqkv.at[pl.ds(QW, 128)], load_sem.at[1]),
        pltpu.make_async_copy(wo_hbm, wo.at[pl.ds(0, QW)], load_sem.at[2]),
        pltpu.make_async_copy(wgu_hbm, wgu, load_sem.at[3]),
        pltpu.make_async_copy(wd_hbm, wd, load_sem.at[4]),
        pltpu.make_async_copy(perm_hbm, perm, load_sem.at[5]),
    ]
    for c in loads:
        c.start()

    def to_core(src, dst, i):
        return pltpu.make_async_remote_copy(
            src_ref=src, dst_ref=dst, send_sem=send_sem.at[i], recv_sem=recv_sem.at[i],
            device_id={"tensor": other}, device_id_type=MESH)

    def to_pipe(src, dst, i):
        return pltpu.make_async_remote_copy(
            src_ref=src, dst_ref=dst, send_sem=send_sem.at[i], recv_sem=recv_sem.at[i],
            device_id={"pipe": 1 - pipe}, device_id_type=MESH)

    share_x = to_core(xbuf.at[:, t], xbuf.at[:, t], 0)
    share_g = to_core(gbuf.at[:, t], gbuf.at[:, t], 1)
    pass_x = to_pipe(so_ref, xbuf.at[:, t], 2)
    pass_g = to_pipe(pipe_out, gbuf.at[:, t], 3)
    swap_1 = to_core(e1s, e1r, 4)
    swap_2 = to_core(e2s, e2r, 5)
    swap_3 = to_core(e3s, e3r, 6)
    swap_4 = to_core(e4s, e4r, 7)

    barrier = pltpu.get_barrier_semaphore()
    pl.semaphore_signal(barrier, inc=1, device_id={"tensor": other}, device_id_type=MESH)
    pl.semaphore_signal(barrier, inc=1, device_id={"pipe": 1 - pipe}, device_id_type=MESH)
    pl.semaphore_wait(barrier, 2)

    @pl.when(pipe == 0)
    def _():
        xbuf[:, t] = x_ref[...]

    @pl.when(pipe == 1)
    def _():
        gbuf[:, t] = cot_ref[...]
        share_g.start()

    wqkv[pl.ds(QW + 128, 64), :] = jnp.zeros((64, D), BF)
    wo[pl.ds(QW, 64), :] = jnp.zeros((64, D), BF)
    slot = lax.broadcasted_iota(jnp.int32, (CAP, CAP), 0)
    lane = lax.broadcasted_iota(jnp.int32, (CAP, CAP), 1)
    for m in range(MICRO):
        end = 0
        seg_row = jnp.zeros((CAP, CAP), jnp.int32)
        seg_col = jnp.zeros((CAP, CAP), jnp.int32)
        start = jnp.zeros((CAP, CAP), jnp.int32)
        for s in range(SEQS):
            end = end + len_ref[m, s]
            passed = slot >= end
            seg_row = seg_row + passed.astype(jnp.int32)
            seg_col = seg_col + (lane >= end).astype(jnp.int32)
            start = jnp.where(passed, end, start)
        allow[m] = jnp.where((seg_row == seg_col) & (lane <= slot), 1.0, 0.0)
        cs[m, 2] = jnp.where((seg_row < SEQS) | (pipe == 0), 1.0, 0.0)
        one_hot = jnp.where(slot - start == lane, 1.0, 0.0).astype(BF)
        table = nn(one_hot, tab_ref[...])
        cs[m, 0] = table[:, :128] + table[:, 128:256] + table[:, 256:384]
        cs[m, 1] = table[:, 384:512] + table[:, 512:640] + table[:, 640:768]

    @pl.when(pipe == 1)
    def _():
        pass_x.wait_recv()

    share_x.start()
    share_x.wait()
    stream = xbuf[...].astype(F32).reshape(ROWS, D)
    inv = lax.rsqrt(jnp.mean(stream * stream, axis=-1, keepdims=True) + EPS)
    n1[...] = (stream * inv * g1_ref[...]).astype(BF)
    loads[0].wait()
    loads[1].wait()
    half_lane = lax.broadcasted_iota(jnp.int32, (CAP, 128), 1)
    for m in range(MICRO):
        rows = pl.ds(m * CAP, CAP)
        qkv = nt(n1[rows, :], wqkv[...]) + b_ref[...]
        for j in range(4):
            block = qkv[:, j * 128:(j + 1) * 128]
            block = block * cs[m, 0] + turn(block, half_lane) * cs[m, 1]
            qb[m, j] = block.astype(BF)
            if j == 3:
                odd = jnp.where(half_lane >= 64, block, 0.0)
                kb[m, 1] = odd.astype(BF)
                kb[m, 0] = pltpu.roll(odd, 64, 1).astype(BF)
        even = jnp.where(half_lane < 64, qkv[:, 512:640], 0.0)
        vb[m, 0] = even.astype(BF)
        vb[m, 1] = pltpu.roll(even, 64, 1).astype(BF)
    for m in range(MICRO):
        q_even = qb[m].reshape(4 * CAP, 128)
        q_odd = qb[m, :3].reshape(3 * CAP, 128)
        seen = allow[m] > 0.0
        mixed = []
        for parity, queries, count in ((0, q_even, 4), (1, q_odd, 3)):
            scores = nt(queries, kb[m, parity]).reshape(count, CAP, CAP) * HEAD ** (-0.5)
            scores = jnp.where(seen[None], scores, -1e30)
            top = jnp.max(scores, axis=-1, keepdims=True)
            grown = jnp.exp(scores - top)
            p = grown * (1.0 / jnp.sum(grown, axis=-1, keepdims=True))
            pmat[m, pl.ds(4 * parity, count)] = p
            mixed.append(nn(p.reshape(count * CAP, CAP).astype(BF), vb[m, parity]))
        for j in range(4):
            block = mixed[0][j * CAP:(j + 1) * CAP]
            if j < 3:
                block = block + mixed[1][j * CAP:(j + 1) * CAP]
            mix[pl.ds(m * CAP, CAP), j * 128:(j + 1) * 128] = block.astype(BF)
    loads[2].wait()
    for c, w in WIDE:
        e1s[:, c:c + w] = nn(mix[...], wo[:, c:c + w]).astype(BF)
    swap_1.start()
    swap_1.wait()
    mid = stream + (e1s[...].astype(F32) + e1r[...].astype(F32))
    middle[...] = mid.reshape(MICRO, 2, OWN, D)
    inv = lax.rsqrt(jnp.mean(mid * mid, axis=-1, keepdims=True) + EPS)
    n2[...] = (mid * inv * g2_ref[...]).astype(BF)
    loads[3].wait()
    for c, w in TILES:
        g = nn(n2[...], wgu[0, :, c:c + w])
        u = nn(n2[...], wgu[1, :, c:c + w])
        gate[:, c:c + w] = g
        up[:, c:c + w] = u
        hidden[:, c:c + w] = (g * jax.nn.sigmoid(g) * u).astype(BF)
    loads[4].wait()
    for c, w in WIDE:
        part[:, :, :, c:c + w] = nn(hidden[...], wd[:, c:c + w]).reshape(MICRO, 2, OWN, w)
    e2s[...] = part[:, other].astype(BF)
    swap_2.start()
    swap_2.wait()
    so_ref[...] = (middle[:, t] + (part[:, t] + e2r[...].astype(F32))).astype(BF)

    @pl.when(pipe == 0)
    def _():
        pass_x.start()
        pass_g.wait_recv()
        share_g.start()

    loads[5].wait()
    share_g.wait()
    for m in range(MICRO):
        live = cs[m, 2][:, :1].astype(BF).reshape(2, OWN, 1)
        gbuf[m] = gbuf[m] * live
    grad = gbuf[...].reshape(ROWS, D)

    def flip(which, rows):
        return nt(perm[which], rows).astype(BF)

    def put(ref, at, w, value):
        ref[:, :, at:at + w] = value.astype(BF).reshape(4, 224, w)

    lt[...] = flip(0, grad)
    for c, w in TILES:
        put(ga_ref, c, w, nn(lt[...], hidden[:, c:c + w]))
    for c, w in TILES:
        gh = nt(grad, wd[c:c + w, :])
        g = gate[:, c:c + w]
        sig = jax.nn.sigmoid(g)
        dgate[:, c:c + w] = (gh * up[:, c:c + w] * sig * (1.0 + g * (1.0 - sig))).astype(BF)
        dup[:, c:c + w] = (gh * g * sig).astype(BF)
    for c, w in WIDE:
        e3s[:, c:c + w] = (nt(dgate[...], wgu[0, c:c + w, :]) + nt(dup[...], wgu[1, c:c + w, :])).astype(BF)
    swap_3.start()
    lt[...] = flip(1, n2[...])
    for c, w in TILES:
        put(gb_ref, c, w, nn(lt[...], dgate[:, c:c + w]))
    for c, w in ((640, 512), (1152, 512), (1664, 512), (2176, 256)):
        put(gb_ref, B_UP + c - UP_A, w, nn(lt[...], dup[:, c:c + w]))
    lt[...] = flip(0, n2[...])
    put(ga_ref, A_UP, UP_A, nn(lt[...], dup[:, :UP_A]))
    swap_3.wait()

    def norm_back(grads, values, gain):
        inverse = lax.rsqrt(jnp.mean(values * values, axis=-1, keepdims=True) + EPS)
        scaled = values * inverse
        weighted = grads * gain
        back = inverse * (weighted - scaled * jnp.mean(weighted * scaled, axis=-1, keepdims=True))
        return back, grads * scaled

    grads = e3s[...].astype(F32) + e3r[...].astype(F32)
    back, terms = norm_back(grads, middle[...].reshape(ROWS, D), g2_ref[...])
    row = lax.broadcasted_iota(jnp.int32, (ROWS, 1), 0)
    mine = ((row >> 6) & 1) == t
    small_ref[...] = jnp.zeros((8, D), F32)
    small_ref[1:2, :] = jnp.sum(jnp.where(mine, terms, 0.0), axis=0, keepdims=True)
    grad_mid = grad.astype(F32) + back
    gmid[...] = grad_mid.reshape(MICRO, 2, OWN, D)
    mb = grad_mid.astype(BF)
    lt[...] = flip(0, mb)
    put(ga_ref, A_OUT, 512, nn(lt[...], mix[...]))
    gmix = nt(mb, wo[...]).astype(BF)
    for m in range(MICRO):
        blocks = [gmix[m * CAP:(m + 1) * CAP, j * 128:(j + 1) * 128] for j in range(4)]
        q_even = qb[m].reshape(4 * CAP, 128)
        q_odd = qb[m, :3].reshape(3 * CAP, 128)
        out = []
        for parity, queries, count in ((0, q_even, 4), (1, q_odd, 3)):
            gm = jnp.concatenate(blocks[:count], axis=0)
            p = pmat[m, pl.ds(4 * parity, count)].reshape(count * CAP, CAP)
            gp = nt(gm, vb[m, parity])
            ds = (p * (gp - jnp.sum(p * gp, axis=-1, keepdims=True))).astype(BF)
            out.append((nn(ds, kb[m, parity]), tn(ds, queries), tn(p.astype(BF), gm)))
        keys = pltpu.roll(out[0][1], 64, 1) + out[1][1]
        values = out[0][2] + pltpu.roll(out[1][2], 64, 1)
        rows = pl.ds(m * CAP, CAP)
        for j in range(4):
            block = out[0][0][j * CAP:(j + 1) * CAP]
            if j < 3:
                block = block + out[1][0][j * CAP:(j + 1) * CAP]
            else:
                block = jnp.where(half_lane < 64, block, keys)
            block = block * HEAD ** (-0.5)
            block = block * cs[m, 0] - turn(block, half_lane) * cs[m, 1]
            gqkv[rows, j * 128:(j + 1) * 128] = block.astype(BF)
        gqkv[rows, 512:640] = jnp.where(half_lane < 64, values, 0.0).astype(BF)
    for c, w in WIDE:
        part[:, :, :, c:c + w] = nn(gqkv[...], wqkv[:, c:c + w]).reshape(MICRO, 2, OWN, w)
    e4s[...] = part[:, other].astype(BF)
    swap_4.start()
    swap_4.wait()
    grads = (part[:, t] + e4r[...].astype(F32)).reshape(MICRO * OWN, D)
    back, terms = norm_back(grads, xbuf[:, t].astype(F32).reshape(MICRO * OWN, D), g1_ref[...])
    total = gmid[:, t] + back.reshape(MICRO, OWN, D)
    ig_ref[...] = total
    pipe_out[...] = total.astype(BF)

    @pl.when(pipe == 1)
    def _():
        pass_g.start()

    small_ref[0:1, :] = jnp.sum(terms, axis=0, keepdims=True)
    bias = jnp.sum(gqkv[...].astype(F32), axis=0, keepdims=True)
    for c in range(2):
        small_ref[2 + c:3 + c, :640] = jnp.where(t == c, bias, 0.0)
    lt[...] = flip(0, n1[...])
    put(ga_ref, A_QKV, 640, nn(lt[...], gqkv[...]))

    @pl.when(pipe == 0)
    def _():
        pass_x.wait_send()

    @pl.when(pipe == 1)
    def _():
        pass_g.wait_send()


def run_layers(lens, x, cot, g1, g2, bias, wq, wkv, wo, wgu, wd):
    vmem = pl.BlockSpec(memory_space=VMEM)
    hbm = pl.BlockSpec(memory_space=pl.ANY)
    return pl.pallas_call(
        layer_kernel,
        out_shape=(
            jax.ShapeDtypeStruct((MICRO, OWN, D), BF),
            jax.ShapeDtypeStruct((MICRO, OWN, D), F32),
            jax.ShapeDtypeStruct((4, 224, HALF), BF),
            jax.ShapeDtypeStruct((4, 224, HALF), BF),
            jax.ShapeDtypeStruct((8, D), F32),
        ),
        in_specs=[pl.BlockSpec(memory_space=pltpu.SMEM)] + [vmem] * 6 + [hbm] * 6,
        out_specs=(vmem,) * 5,
        scratch_shapes=[
            VMEM((640, D), BF), VMEM((512, D), BF), VMEM((2, D, FH), BF), VMEM((FH, D), BF), VMEM((2, D, D), BF),
            VMEM((MICRO, 2, OWN, D), BF), VMEM((MICRO, 2, OWN, D), BF),
            VMEM((ROWS, D), BF), VMEM((ROWS, D), BF),
            VMEM((MICRO, OWN, D), BF), VMEM((MICRO, OWN, D), BF),
            VMEM((ROWS, D), BF), VMEM((ROWS, D), BF),
            VMEM((MICRO, OWN, D), BF), VMEM((MICRO, OWN, D), BF), VMEM((MICRO, OWN, D), BF),
            VMEM((ROWS, D), BF), VMEM((ROWS, D), BF),
            VMEM((MICRO, 4, CAP, 128), BF), VMEM((MICRO, 2, CAP, 128), BF), VMEM((MICRO, 2, CAP, 128), BF),
            VMEM((MICRO, 7, CAP, CAP), F32), VMEM((ROWS, 512), BF), VMEM((MICRO, 2, OWN, D), F32),
            VMEM((ROWS, FH), F32), VMEM((ROWS, FH), F32), VMEM((ROWS, FH), BF), VMEM((ROWS, FH), BF), VMEM((ROWS, FH), BF),
            VMEM((D, ROWS), BF), VMEM((MICRO, 2, OWN, D), F32), VMEM((MICRO, 2, OWN, D), F32),
            VMEM((MICRO, 3, CAP, 128), F32), VMEM((MICRO, CAP, CAP), F32), VMEM((ROWS, 640), BF),
            pltpu.SemaphoreType.DMA((6,)), pltpu.SemaphoreType.DMA((8,)), pltpu.SemaphoreType.DMA((8,)),
        ],
        compiler_params=pltpu.CompilerParams(collective_id=0, has_side_effects=True, vmem_limit_bytes=60 * MIB),
        name="layers",
    )(lens, x, cot, g1, g2, bias, jnp.asarray(rope_table()), wq, wkv, wo, wgu, wd, jnp.asarray(row_orders()))


PIECES = ((0, 1408), (1408, 1408), (2816, 1408))


def sum_kernel(
    g0_hbm, g1_hbm, small_ref, o0_ref, o1_ref, so_ref,
    grads, r1, r2, h2, q1, q2, h3, q3, small_in, load_sem, send_sem, recv_sem, small_send, small_recv,
):
    rank = lax.axis_index("dp")
    t = lax.axis_index("tensor")
    x_hi, z, y = rank // 16, (rank // 4) % 4, rank % 4

    def at(yy, zz, xx):
        return {"dp": xx * 16 + zz * 4 + yy}

    def along(axis, step):
        if axis == 0:
            return at((y + step) % 4, z, x_hi)
        return at(y, (z + step) % 4, x_hi)

    x_peer = at(y, z, 1 - x_hi)
    pos = (y, z)
    loads = []
    for h, src in ((0, g0_hbm), (1, g1_hbm)):
        for i, (c, w) in enumerate(PIECES):
            loads.append(pltpu.make_async_copy(src.at[:, :, pl.ds(c, w)], grads.at[h, :, :, pl.ds(c, w)], load_sem.at[h, i]))
    for i in range(len(PIECES)):
        for h in range(2):
            loads[h * len(PIECES) + i].start()

    barrier = pltpu.get_barrier_semaphore()
    peers = [along(0, 1), along(0, 3), along(1, 1), along(1, 3), x_peer, {"tensor": 1 - t}]
    for peer in peers:
        pl.semaphore_signal(barrier, inc=1, device_id=peer, device_id_type=MESH)
    pl.semaphore_wait(barrier, len(peers))

    def remote(src, dst, peer, *sem):
        return pltpu.make_async_remote_copy(
            src_ref=src, dst_ref=dst, send_sem=send_sem.at[sem], recv_sem=recv_sem.at[sem],
            device_id=peer, device_id_type=MESH)

    copies = {}

    def ring_copies(h, i, stage):
        c, w = PIECES[i]
        cols = pl.ds(c, w)
        axis = h if stage == 0 else 1 - h
        f = pos[axis]
        ahead, behind = along(axis, 1), along(axis, 3)
        if stage == 0:
            n, src, first, last = 112, grads.at[h], r1.at[h], r2.at[h]
        else:
            n, src, first, last = 32, h2.at[h], q1.at[h], q2.at[h]
        top, low = pl.ds(0, n), pl.ds(n, n)
        base = 6 * stage
        cp = [
            remote(src.at[(f + 2) % 4, top, cols], first.at[0, :, cols], ahead, h, i, base),
            remote(src.at[(f + 2) % 4, low, cols], first.at[1, :, cols], behind, h, i, base + 1),
            remote(src.at[(f + 1) % 4, low, cols], last.at[0, 1, :, cols], ahead, h, i, base + 2),
            remote(src.at[(f + 3) % 4, top, cols], last.at[1, 0, :, cols], behind, h, i, base + 3),
            remote(first.at[0, :, cols], last.at[0, 0, :, cols], ahead, h, i, base + 4),
            remote(first.at[1, :, cols], last.at[1, 1, :, cols], behind, h, i, base + 5),
        ]
        return cp, f, src, first, last, n, cols

    def ring_begin(h, i, stage):
        cp = ring_copies(h, i, stage)[0]
        copies[h, i, stage] = cp
        for k in range(4):
            cp[k].start()

    def ring_middle(h, i, stage):
        cp, f, src, first, last, n, cols = ring_copies(h, i, stage)
        for k, (chunk, part) in enumerate((((f + 1) % 4, 0), ((f + 3) % 4, 1))):
            cp[k].wait_recv()
            own = src[chunk, part * n:(part + 1) * n, cols]
            first[k, :, cols] = (own.astype(F32) + first[k, :, cols].astype(F32)).astype(BF)
            cp[4 + k].start()

    def ring_total(h, i, stage):
        cp, f, src, first, last, n, cols = ring_copies(h, i, stage)
        for k in range(2, 6):
            cp[k].wait_recv()
        sums = []
        for part in range(2):
            own = src[f, part * n:(part + 1) * n, cols]
            sums.append(own.astype(F32) + last[0, part, :, cols].astype(F32) + last[1, part, :, cols].astype(F32))
        return sums

    def second_begin(h, i):
        c, w = PIECES[i]
        top, low = ring_total(h, i, 0)
        for k in range(4):
            src = (top, low)[k // 2][(k % 2) * 56:(k % 2 + 1) * 56]
            h2[h, k, :56, c:c + w] = src.astype(BF)
            h2[h, k, 56:, c:c + w] = jnp.zeros((8, w), BF)
        ring_begin(h, i, 1)

    def third(h, i):
        c, w = PIECES[i]
        return remote(h3.at[h, :, pl.ds(c, w)], q3.at[h, :, pl.ds(c, w)], x_peer, h, i, 12)

    def third_begin(h, i):
        c, w = PIECES[i]
        top, low = ring_total(h, i, 1)
        both = jnp.concatenate([top, low], axis=0)
        first, last = both[:32], both[28:60]
        upper = x_hi == 1
        h3[h, :, c:c + w] = jnp.where(upper, first, last).astype(BF)
        (o0_ref, o1_ref)[h][:, c:c + w] = jnp.where(upper, last, first)[:28]
        third(h, i).start()

    def third_end(h, i):
        c, w = PIECES[i]
        third(h, i).wait_recv()
        out = (o0_ref, o1_ref)[h]
        out[:, c:c + w] = out[:, c:c + w] + q3[h, :, c:c + w].astype(F32)[:28]

    small_peers = [
        along(0, 1 + 2 * (y % 2)), along(0, 3 - 2 * (y % 2)),
        along(1, 1 + 2 * (z % 2)), along(1, 3 - 2 * (z % 2)), x_peer, {"tensor": 1 - t},
    ]

    def small_copy(k):
        return pltpu.make_async_remote_copy(
            src_ref=small_in.at[0, k], dst_ref=small_in.at[1, k], send_sem=small_send.at[k], recv_sem=small_recv.at[k],
            device_id=small_peers[k], device_id_type=MESH)

    def small_step(k):
        if k > 0:
            small_copy(k - 1).wait_recv()
            total = small_in[0, k - 1] + small_in[1, k - 1]
        else:
            total = small_ref[...]
        if k < 6:
            small_in[0, k] = total
            small_copy(k).start()
        else:
            so_ref[...] = total

    def begin(i):
        for h in range(2):
            loads[h * len(PIECES) + i].wait()
            ring_begin(h, i, 0)

    def both(f, *a):
        for h in range(2):
            f(h, *a)

    small_step(0)
    begin(0)
    begin(1)
    both(ring_middle, 0, 0)
    small_step(1)
    begin(2)
    both(ring_middle, 1, 0)
    small_step(2)
    both(second_begin, 0)
    both(ring_middle, 2, 0)
    small_step(3)
    both(ring_middle, 0, 1)
    both(second_begin, 1)
    small_step(4)
    both(third_begin, 0)
    both(ring_middle, 1, 1)
    both(second_begin, 2)
    small_step(5)
    both(third_begin, 1)
    both(ring_middle, 2, 1)
    both(third_end, 0)
    both(third_end, 1)
    both(third_begin, 2)
    small_step(6)
    both(third_end, 2)
    for i in range(len(PIECES)):
        for h in range(2):
            for stage in range(2):
                for cp in ring_copies(h, i, stage)[0]:
                    cp.wait_send()
            third(h, i).wait_send()
    for k in range(6):
        small_copy(k).wait_send()


def run_sums(ga, gb, small):
    vmem = pl.BlockSpec(memory_space=VMEM)
    hbm = pl.BlockSpec(memory_space=pl.ANY)
    count = len(PIECES)
    return pl.pallas_call(
        sum_kernel,
        out_shape=(
            jax.ShapeDtypeStruct((28, HALF), F32), jax.ShapeDtypeStruct((28, HALF), F32),
            jax.ShapeDtypeStruct((8, D), F32),
        ),
        in_specs=[hbm, hbm, vmem],
        out_specs=(vmem,) * 3,
        scratch_shapes=[
            VMEM((2, 4, 224, HALF), BF), VMEM((2, 2, 112, HALF), BF), VMEM((2, 2, 2, 112, HALF), BF),
            VMEM((2, 4, 64, HALF), BF), VMEM((2, 2, 32, HALF), BF), VMEM((2, 2, 2, 32, HALF), BF),
            VMEM((2, 32, HALF), BF), VMEM((2, 32, HALF), BF), VMEM((2, 6, 8, D), F32),
            pltpu.SemaphoreType.DMA((2, count)), pltpu.SemaphoreType.DMA((2, count, 13)), pltpu.SemaphoreType.DMA((2, count, 13)),
            pltpu.SemaphoreType.DMA((6,)), pltpu.SemaphoreType.DMA((6,)),
        ],
        compiler_params=pltpu.CompilerParams(collective_id=1, has_side_effects=True, vmem_limit_bytes=56 * MIB),
        name="sums",
    )(ga, gb, small)


def body(
    inputs, cotangent, lengths, gain_attn, w_query, b_query, w_keyval, b_keyval, w_out, gain_mlp, w_gate_up, w_down,
):
    bias = jnp.concatenate([b_query[0], b_keyval[0, 0], jnp.zeros((64,), BF)]).astype(F32)[None]
    outs = run_layers(
        lengths[:, 0], inputs, cotangent, gain_attn.astype(F32), gain_mlp.astype(F32), bias,
        jnp.swapaxes(w_query[0], 0, 1), jnp.swapaxes(w_keyval[0, :, 0], 0, 1), w_out[0],
        jnp.swapaxes(w_gate_up[0], 0, 1), w_down[0],
    )
    section_out, input_grad, ga, gb, small = outs
    sa, sb, total = run_sums(ga, gb, small)
    g_up = jnp.concatenate([sa[:, A_UP:A_UP + UP_A], sb[:, B_UP:]], axis=1)
    g_gate_up = jnp.stack([sb[:, :FH], g_up], axis=1)
    g_query = sa[:, A_QKV:A_QKV + QW]
    g_keyval = sa[:, A_QKV + QW:A_QKV + QW + 128]
    return (
        section_out[None],
        input_grad[None],
        total[0:1],
        g_query[None],
        total[2:4, :QW].reshape(1, HEADS * HEAD),
        g_keyval[None, :, None, :],
        total[2:4, QW:QW + 128][None],
        jnp.swapaxes(sa[:, A_OUT:A_OUT + QW], 0, 1)[None],
        total[1:2],
        g_gate_up[None],
        jnp.swapaxes(sa[:, :FH], 0, 1)[None],
    )


def solution(mesh):
    placed = (
        P(None, ("dp", "tensor"), None),
        P(None, ("dp", "tensor"), None),
        P(None, "dp", None),
        P("pipe", None),
        P("pipe", None, "tensor"),
        P("pipe", "tensor"),
        P("pipe", None, "tensor", None),
        P("pipe", "tensor", None),
        P("pipe", "tensor", None),
        P("pipe", None),
        P("pipe", None, None, "tensor"),
        P("pipe", "tensor", None),
    )
    return jax.shard_map(
        body,
        mesh=mesh,
        in_specs=placed,
        out_specs=(
            P("pipe", None, ("dp", "tensor"), None),
            P("pipe", None, ("dp", "tensor"), None),
            P("pipe", None),
            P("pipe", "dp", "tensor"),
            P("pipe", None),
            P("pipe", "dp", "tensor", None),
            P("pipe", None, None),
            P("pipe", "tensor", "dp"),
            P("pipe", None),
            P("pipe", "dp", None, "tensor"),
            P("pipe", "tensor", "dp"),
        ),
        check_vma=False,
    )
```

```python
import functools

import jax
import jax.numpy as jnp
import numpy as np
from jax import lax
from jax.experimental import pallas as pl
from jax.experimental.pallas import tpu as pltpu
from jax.sharding import PartitionSpec as P

D = 896
HEADS = 14
HEAD = 64
CAP = 128
SEQS = 4
MICRO = 2
ROWS = MICRO * CAP
OWN = CAP // 2
FH = 2432
QW = 448
EPS = 1e-06
THETA = 1000000.0
MIB = 1024 * 1024

BF = jnp.bfloat16
F32 = jnp.float32
MESH = pl.DeviceIdType.MESH
VMEM = pltpu.VMEM

UP_A = 640
A_UP = FH
A_OUT = FH + UP_A
A_Q = A_OUT + 512
A_KV = A_Q + 512
HALF = A_KV + 128
B_UP = FH
assert HALF == FH + FH - UP_A
TILES = ((0, 512), (512, 512), (1024, 512), (1536, 512), (2048, 384))
UP_TILES = ((640, 512), (1152, 512), (1664, 512), (2176, 256))
WIDE = ((0, 256), (256, 256), (512, 256), (768, 128))
PIECES = (
    (("down", 0, 1280, 0), ("down", 1280, 1152, 1280), ("up", 0, 640, A_UP), ("rest", 0, 1152, A_OUT)),
    (("gate", 0, 1280, 0), ("gate", 1280, 1152, 1280), ("up", 640, 896, B_UP), ("up", 1536, 896, B_UP + 896)),
)
COUNT = 4


def nn(a, b):
    return lax.dot_general(a, b, (((1,), (0,)), ((), ())), preferred_element_type=F32)


def nt(a, b):
    return lax.dot_general(a, b, (((1,), (1,)), ((), ())), preferred_element_type=F32)


def tn(a, b):
    return lax.dot_general(a, b, (((0,), (0,)), ((), ())), preferred_element_type=F32)


def rope_table():
    half = HEAD // 2
    frequency = np.power(np.float32(THETA), -(np.arange(half, dtype=np.float32) * np.float32(2.0 / HEAD)))
    phases = (np.arange(CAP, dtype=np.float32)[:, None] * frequency[None, :].astype(np.float32)).astype(np.float32)
    phases = phases.astype(np.float64)
    cosine = np.concatenate([np.cos(phases)] * 4, axis=1).astype(np.float32)
    sine = np.concatenate([-np.sin(phases), np.sin(phases)] * 2, axis=1).astype(np.float32)
    parts = []
    for table in (cosine, sine):
        rest = table
        for _ in range(3):
            piece = rest.astype(jnp.bfloat16)
            parts.append(piece)
            rest = rest - piece.astype(np.float32)
    return np.concatenate(parts, axis=1)


def row_order():
    index = np.arange(D)
    y, z, x_hi, k = index // 224, index // 56 % 4, index // 28 % 2, index % 28
    source = (x_hi * 16 + z * 4 + y) * 28 + k
    return (source[:, None] == np.arange(D)[None, :]).astype(jnp.bfloat16)


def turn(block, lane):
    low = (lane & 63) < 32
    return jnp.where(low, pltpu.roll(block, 96, 1), pltpu.roll(block, 32, 1))


def train_kernel(
    len_ref, x_ref, cot_ref, g1_ref, g2_ref, bq_ref, bkv_ref, tab_ref,
    wq_hbm, wkv_hbm, wo_hbm, wgu_hbm, wd_hbm, perm_hbm,
    so_ref, ig_ref, o0_ref, o1_ref, total_ref,
    wq, wkv, wo, wgu, wd, perm, xbuf, gbuf, e1s, e1r, e2s, e2r, pipe_out,
    n1, n2, qb, kb, vb, pmat, mix, middle, dgate, dup, hidden, lt, part, gmid, cs, allow, gqkv,
    mb_ref, gdown, grest, r1, r2, h2, q1, q2, h3, q3, small_in,
    load_sem, send_sem, recv_sem, sum_send, sum_recv, small_send, small_recv,
):
    pipe = lax.axis_index("pipe")
    t = lax.axis_index("tensor")
    rank = lax.axis_index("dp")
    other = 1 - t
    x_hi, z, y = rank // 16, (rank // 4) % 4, rank % 4
    pos = (y, z)

    loads = [
        pltpu.make_async_copy(wq_hbm, wq.at[pl.ds(0, QW)], load_sem.at[0]),
        pltpu.make_async_copy(wkv_hbm, wkv, load_sem.at[1]),
        pltpu.make_async_copy(wo_hbm, wo.at[pl.ds(0, QW)], load_sem.at[2]),
        pltpu.make_async_copy(wgu_hbm, wgu, load_sem.at[3]),
        pltpu.make_async_copy(wd_hbm, wd, load_sem.at[4]),
        pltpu.make_async_copy(perm_hbm, perm, load_sem.at[5]),
    ]
    for c in loads:
        c.start()

    def to_core(src, dst, i):
        return pltpu.make_async_remote_copy(
            src_ref=src, dst_ref=dst, send_sem=send_sem.at[i], recv_sem=recv_sem.at[i],
            device_id={"tensor": other}, device_id_type=MESH)

    def to_pipe(src, dst, i):
        return pltpu.make_async_remote_copy(
            src_ref=src, dst_ref=dst, send_sem=send_sem.at[i], recv_sem=recv_sem.at[i],
            device_id={"pipe": 1 - pipe}, device_id_type=MESH)

    share_x = to_core(xbuf.at[:, t], xbuf.at[:, t], 0)
    share_g = to_core(gbuf.at[:, t], gbuf.at[:, t], 1)
    pass_x = to_pipe(so_ref, xbuf.at[:, t], 2)
    pass_g = to_pipe(pipe_out, gbuf.at[:, t], 3)
    swap_1 = to_core(e1s, e1r, 4)
    swap_2 = to_core(e2s, e2r, 5)
    swap_3 = to_core(e1s, e1r, 6)
    swap_4 = to_core(e2s, e2r, 7)

    def at(yy, zz, xx):
        return {"dp": xx * 16 + zz * 4 + yy}

    def along(axis, step):
        if axis == 0:
            return at((y + step) % 4, z, x_hi)
        return at(y, (z + step) % 4, x_hi)

    x_peer = at(y, z, 1 - x_hi)
    peers = [along(0, 1), along(0, 3), along(1, 1), along(1, 3), x_peer, {"tensor": other}, {"pipe": 1 - pipe}]
    barrier = pltpu.get_barrier_semaphore()
    for peer in peers:
        pl.semaphore_signal(barrier, inc=1, device_id=peer, device_id_type=MESH)
    pl.semaphore_wait(barrier, len(peers))

    def remote(src, dst, peer, *sem):
        return pltpu.make_async_remote_copy(
            src_ref=src, dst_ref=dst, send_sem=sum_send.at[sem], recv_sem=sum_recv.at[sem],
            device_id=peer, device_id_type=MESH)

    def source(h, i, stage, q, half):
        name, c, w, at_col = PIECES[h][i]
        if stage == 1:
            return h2.at[h, q, pl.ds(32 * half, 32), pl.ds(at_col, w)]
        rows, cols = pl.ds(pl.multiple_of(q * 224 + 112 * half, 16), 112), pl.ds(c, w)
        if name == "down":
            return gdown.at[rows, cols]
        if name == "rest":
            return grest.at[rows, cols]
        return wgu.at[("gate", "up").index(name), rows, cols]

    def landing(h, i, stage):
        _, _, w, at_col = PIECES[h][i]
        cols = pl.ds(at_col, w)
        first, last = (r1, r2) if stage == 0 else (q1, q2)
        return (lambda k: first.at[h, k, :, cols]), (lambda k, half: last.at[h, k, half, :, cols])

    def ring_copy(h, i, stage, k):
        axis = h if stage == 0 else 1 - h
        f = pos[axis]
        first, last = landing(h, i, stage)
        ahead, behind = along(axis, 1), along(axis, 3)
        src, dst, peer = (
            lambda: (source(h, i, stage, (f + 2) % 4, 0), first(0), ahead),
            lambda: (source(h, i, stage, (f + 2) % 4, 1), first(1), behind),
            lambda: (source(h, i, stage, (f + 1) % 4, 1), last(0, 1), ahead),
            lambda: (source(h, i, stage, (f + 3) % 4, 0), last(1, 0), behind),
            lambda: (first(0), last(0, 0), ahead),
            lambda: (first(1), last(1, 1), behind),
        )[k]()
        return remote(src, dst, peer, h, i, 6 * stage + k)

    def begin(h, i, stage=0):
        for k in range(4):
            ring_copy(h, i, stage, k).start()

    def middle_of(h, i, stage):
        f = pos[h if stage == 0 else 1 - h]
        first, _ = landing(h, i, stage)
        for k, q in enumerate(((f + 1) % 4, (f + 3) % 4)):
            ring_copy(h, i, stage, k).wait_recv()
            own = source(h, i, stage, q, k)[...]
            slot = first(k)
            slot[...] = (own.astype(F32) + slot[...].astype(F32)).astype(BF)
            ring_copy(h, i, stage, 4 + k).start()

    def ring_total(h, i, stage):
        f = pos[h if stage == 0 else 1 - h]
        for k in range(2, 6):
            ring_copy(h, i, stage, k).wait_recv()
        _, last = landing(h, i, stage)
        sums = []
        for half in range(2):
            own = source(h, i, stage, f, half)[...]
            sums.append(own.astype(F32) + last(0, half)[...].astype(F32) + last(1, half)[...].astype(F32))
        return sums

    def second(h, i):
        _, _, w, c = PIECES[h][i]
        sums = ring_total(h, i, 0)
        for k in range(4):
            block = sums[k // 2][(k % 2) * 56:(k % 2 + 1) * 56]
            block = jnp.concatenate([block, jnp.zeros((8, w), F32)], axis=0)
            h2[h, k, :, c:c + w] = block.astype(BF)
        begin(h, i, 1)

    def third_copy(h, i):
        _, _, w, c = PIECES[h][i]
        return remote(h3.at[h, :, pl.ds(c, w)], q3.at[h, :, pl.ds(c, w)], x_peer, h, i, 12)

    def third(h, i):
        _, _, w, c = PIECES[h][i]
        both = jnp.concatenate(ring_total(h, i, 1), axis=0)
        first, last = both[:32], both[28:60]
        upper = x_hi == 1
        h3[h, :, c:c + w] = jnp.where(upper, first, last).astype(BF)
        (o0_ref, o1_ref)[h][:, c:c + w] = jnp.where(upper, last, first)[:28]
        third_copy(h, i).start()

    def third_end(h, i):
        _, _, w, c = PIECES[h][i]
        third_copy(h, i).wait_recv()
        out = (o0_ref, o1_ref)[h]
        out[:, c:c + w] = out[:, c:c + w] + q3[h, :, c:c + w].astype(F32)[:28]

    small_peers = [
        along(0, 1 + 2 * (y % 2)), along(0, 3 - 2 * (y % 2)),
        along(1, 1 + 2 * (z % 2)), along(1, 3 - 2 * (z % 2)), x_peer, {"tensor": other},
    ]

    def small_copy(k):
        return pltpu.make_async_remote_copy(
            src_ref=small_in.at[0, k], dst_ref=small_in.at[1, k], send_sem=small_send.at[k], recv_sem=small_recv.at[k],
            device_id=small_peers[k], device_id_type=MESH)

    def small_step(k):
        if k > 0:
            small_copy(k - 1).wait_recv()
            total = small_in[0, k - 1] + small_in[1, k - 1]
            if k < 6:
                small_in[0, k] = total
            else:
                total_ref[...] = total
        if k < 6:
            small_copy(k).start()

    @pl.when(pipe == 0)
    def _():
        xbuf[:, t] = x_ref[...]

    @pl.when(pipe == 1)
    def _():
        gbuf[:, t] = cot_ref[...]
        share_g.start()

    wq[pl.ds(QW, 64), :] = jnp.zeros((64, D), BF)
    wo[pl.ds(QW, 64), :] = jnp.zeros((64, D), BF)
    slot = lax.broadcasted_iota(jnp.int32, (CAP, CAP), 0)
    lane = lax.broadcasted_iota(jnp.int32, (CAP, CAP), 1)
    for m in range(MICRO):
        end = 0
        seg_row = jnp.zeros((CAP, CAP), jnp.int32)
        seg_col = jnp.zeros((CAP, CAP), jnp.int32)
        start = jnp.zeros((CAP, CAP), jnp.int32)
        for s in range(SEQS):
            end = end + len_ref[m, s]
            passed = slot >= end
            seg_row = seg_row + passed.astype(jnp.int32)
            seg_col = seg_col + (lane >= end).astype(jnp.int32)
            start = jnp.where(passed, end, start)
        allow[m] = jnp.where((seg_row == seg_col) & (lane <= slot), 1.0, 0.0)
        cs[m, 2] = jnp.where((seg_row < SEQS) | (pipe == 0), 1.0, 0.0)
        one_hot = jnp.where(slot - start == lane, 1.0, 0.0).astype(BF)
        table = nn(one_hot, tab_ref[...])
        cs[m, 0] = table[:, :128] + table[:, 128:256] + table[:, 256:384]
        cs[m, 1] = table[:, 384:512] + table[:, 512:640] + table[:, 640:768]
    bias_q = jnp.concatenate([bq_ref[...].astype(F32), jnp.zeros((1, 64), F32)], axis=1)
    bias_kv = bkv_ref[...].astype(F32)
    gain_1 = g1_ref[...].astype(F32)
    gain_2 = g2_ref[...].astype(F32)

    @pl.when(pipe == 1)
    def _():
        pass_x.wait_recv()

    share_x.start()
    share_x.wait()
    stream = xbuf[...].astype(F32).reshape(ROWS, D)
    inv = lax.rsqrt(jnp.mean(stream * stream, axis=-1, keepdims=True) + EPS)
    n1[...] = (stream * inv * gain_1).astype(BF)
    loads[0].wait()
    loads[1].wait()
    half_lane = lax.broadcasted_iota(jnp.int32, (CAP, 128), 1)
    for m in range(MICRO):
        rows = pl.ds(m * CAP, CAP)
        qs = nt(n1[rows, :], wq[...]) + bias_q
        vk = pltpu.roll(nn(n1[rows, :], wkv[...]) + bias_kv, 64, 1)
        for j in range(4):
            block = qs[:, j * 128:(j + 1) * 128]
            if j == 3:
                block = jnp.where(half_lane < 64, block, vk)
            block = block * cs[m, 0] + turn(block, half_lane) * cs[m, 1]
            qb[m, j] = block.astype(BF)
            if j == 3:
                odd = jnp.where(half_lane >= 64, block, 0.0)
                kb[m, 1] = odd.astype(BF)
                kb[m, 0] = pltpu.roll(odd, 64, 1).astype(BF)
        even = jnp.where(half_lane < 64, vk, 0.0)
        vb[m, 0] = even.astype(BF)
        vb[m, 1] = pltpu.roll(even, 64, 1).astype(BF)
    for m in range(MICRO):
        q_even = qb[m].reshape(4 * CAP, 128)
        q_odd = qb[m, :3].reshape(3 * CAP, 128)
        seen = allow[m] > 0.0
        mixed = []
        for parity, queries, count in ((0, q_even, 4), (1, q_odd, 3)):
            scores = nt(queries, kb[m, parity]).reshape(count, CAP, CAP) * HEAD ** (-0.5)
            scores = jnp.where(seen[None], scores, -1e30)
            top = jnp.max(scores, axis=-1, keepdims=True)
            grown = jnp.exp(scores - top)
            p = grown * (1.0 / jnp.sum(grown, axis=-1, keepdims=True))
            pmat[m, pl.ds(4 * parity, count)] = p
            mixed.append(nn(p.reshape(count * CAP, CAP).astype(BF), vb[m, parity]))
        for j in range(4):
            block = mixed[0][j * CAP:(j + 1) * CAP]
            if j < 3:
                block = block + mixed[1][j * CAP:(j + 1) * CAP]
            mix[pl.ds(m * CAP, CAP), j * 128:(j + 1) * 128] = block.astype(BF)
    loads[2].wait()
    for c, w in WIDE:
        e1s[:, c:c + w] = nn(mix[...], wo[:, c:c + w]).astype(BF)
    swap_1.start()
    swap_1.wait()
    mid = stream + (e1s[...].astype(F32) + e1r[...].astype(F32))
    middle[...] = mid.reshape(MICRO, 2, OWN, D)
    inv = lax.rsqrt(jnp.mean(mid * mid, axis=-1, keepdims=True) + EPS)
    n2[...] = (mid * inv * gain_2).astype(BF)
    loads[3].wait()
    for c, w in TILES:
        g = nn(n2[...], wgu[0, :, c:c + w])
        u = nn(n2[...], wgu[1, :, c:c + w])
        sig = jax.nn.sigmoid(g)
        silu = g * sig
        hidden[:, c:c + w] = (silu * u).astype(BF)
        dup[:, c:c + w] = silu.astype(BF)
        dgate[:, c:c + w] = (u * sig * (1.0 + g * (1.0 - sig))).astype(BF)
    loads[4].wait()
    for c, w in WIDE:
        part[:, :, :, c:c + w] = nn(hidden[...], wd[:, c:c + w]).reshape(MICRO, 2, OWN, w)
    e2s[...] = part[:, other].astype(BF)
    swap_2.start()
    swap_2.wait()
    so_ref[...] = (middle[:, t] + (part[:, t] + e2r[...].astype(F32))).astype(BF)

    @pl.when(pipe == 0)
    def _():
        pass_x.start()
        pass_g.wait_recv()
        share_g.start()

    loads[5].wait()
    share_g.wait()
    for m in range(MICRO):
        live = cs[m, 2][:, :1].astype(BF).reshape(2, OWN, 1)
        gbuf[m] = gbuf[m] * live

    def weights_down():
        lt[0] = nt(perm[...], gbuf[...].reshape(ROWS, D)).astype(BF)
        for i, tiles in enumerate((((0, 512), (512, 768)), ((1280, 512), (1792, 640)))):
            for c, w in tiles:
                gdown[:, c:c + w] = nn(lt[0], hidden[:, c:c + w]).astype(BF)
            begin(0, i)

    def weights_gate_up():
        turned = nt(perm[...], n2[...])
        lt[0] = turned.astype(BF)
        lt[1] = jnp.concatenate(
            [turned[(4 * b + a) * 56:(4 * b + a + 1) * 56] for a in range(4) for b in range(4)], axis=0).astype(BF)
        for i, tiles in enumerate((((0, 512), (512, 768)), ((1280, 512), (1792, 640)))):
            for c, w in tiles:
                wgu[0, :, c:c + w] = nn(lt[1], dgate[:, c:c + w]).astype(BF)
            begin(1, i)
        wgu[1, :, :UP_A] = nn(lt[0], dup[:, :UP_A]).astype(BF)
        begin(0, 2)
        for i, c in ((2, 640), (3, 1536)):
            wgu[1, :, c:c + 896] = nn(lt[1], dup[:, c:c + 896]).astype(BF)
            begin(1, i)

    @pl.when(pipe == 0)
    def _():
        weights_down()

    grad = gbuf[...].reshape(ROWS, D)
    for c, w in TILES:
        gh = nt(grad, wd[c:c + w, :])
        dgate[:, c:c + w] = (gh * dgate[:, c:c + w].astype(F32)).astype(BF)
        dup[:, c:c + w] = (gh * dup[:, c:c + w].astype(F32)).astype(BF)
    for c, w in WIDE:
        e1s[:, c:c + w] = (nt(dgate[...], wgu[0, c:c + w, :]) + nt(dup[...], wgu[1, c:c + w, :])).astype(BF)
    swap_3.start()

    @pl.when(pipe == 0)
    def _():
        weights_gate_up()

    swap_3.wait()

    def norm_back(grads, values, gain):
        inverse = lax.rsqrt(jnp.mean(values * values, axis=-1, keepdims=True) + EPS)
        scaled = values * inverse
        weighted = grads * gain
        back = inverse * (weighted - scaled * jnp.mean(weighted * scaled, axis=-1, keepdims=True))
        return back, grads * scaled

    grads = e1s[...].astype(F32) + e1r[...].astype(F32)
    back, terms = norm_back(grads, middle[...].reshape(ROWS, D), gain_2)
    row = lax.broadcasted_iota(jnp.int32, (ROWS, 1), 0)
    mine = ((row >> 6) & 1) == t
    small_in[0, 0] = jnp.zeros((8, D), F32)
    small_in[0, 0, 1:2, :] = jnp.sum(jnp.where(mine, terms, 0.0), axis=0, keepdims=True)
    grad_mid = gbuf[...].reshape(ROWS, D).astype(F32) + back
    gmid[...] = grad_mid.reshape(MICRO, 2, OWN, D)
    mb_ref[...] = grad_mid.astype(BF)
    gmix = nt(mb_ref[...], wo[...]).astype(BF)
    for m in range(MICRO):
        blocks = [gmix[m * CAP:(m + 1) * CAP, j * 128:(j + 1) * 128] for j in range(4)]
        q_even = qb[m].reshape(4 * CAP, 128)
        q_odd = qb[m, :3].reshape(3 * CAP, 128)
        out = []
        for parity, queries, count in ((0, q_even, 4), (1, q_odd, 3)):
            gm = jnp.concatenate(blocks[:count], axis=0)
            p = pmat[m, pl.ds(4 * parity, count)].reshape(count * CAP, CAP)
            gp = nt(gm, vb[m, parity])
            ds = (p * (gp - jnp.sum(p * gp, axis=-1, keepdims=True))).astype(BF)
            out.append((nn(ds, kb[m, parity]), tn(ds, queries), tn(p.astype(BF), gm)))
        keys = pltpu.roll(out[0][1], 64, 1) + out[1][1]
        values = out[0][2] + pltpu.roll(out[1][2], 64, 1)
        rows = pl.ds(m * CAP, CAP)
        for j in range(4):
            block = out[0][0][j * CAP:(j + 1) * CAP]
            if j < 3:
                block = block + out[1][0][j * CAP:(j + 1) * CAP]
            else:
                block = jnp.where(half_lane < 64, block, keys)
            block = block * HEAD ** (-0.5)
            block = block * cs[m, 0] - turn(block, half_lane) * cs[m, 1]
            if j == 3:
                gqkv[rows, 512:640] = pltpu.roll(jnp.where(half_lane < 64, values, block), 64, 1).astype(BF)
                block = jnp.where(half_lane < 64, block, 0.0)
            gqkv[rows, j * 128:(j + 1) * 128] = block.astype(BF)
    for c, w in WIDE:
        part[:, :, :, c:c + w] = (
            nn(gqkv[:, :512], wq[:, c:c + w]) + nt(gqkv[:, 512:], wkv[c:c + w, :])).reshape(MICRO, 2, OWN, w)
    e2s[...] = part[:, other].astype(BF)
    swap_4.start()
    swap_4.wait()
    grads = (part[:, t] + e2r[...].astype(F32)).reshape(MICRO * OWN, D)
    back, terms = norm_back(grads, xbuf[:, t].astype(F32).reshape(MICRO * OWN, D), gain_1)
    total = gmid[:, t] + back.reshape(MICRO, OWN, D)
    ig_ref[...] = total
    pipe_out[...] = total.astype(BF)

    @pl.when(pipe == 1)
    def _():
        pass_g.start()

    @pl.when(pipe == 1)
    def _():
        weights_down()
        weights_gate_up()

    lt[0] = nt(perm[...], mb_ref[...]).astype(BF)
    lt[1] = nt(perm[...], n1[...]).astype(BF)
    grest[:, :512] = nn(lt[0], mix[...]).astype(BF)
    grest[:, 512:] = nn(lt[1], gqkv[...]).astype(BF)
    begin(0, 3)
    small_in[0, 0, 0:1, :] = jnp.sum(terms, axis=0, keepdims=True)
    bias = jnp.sum(gqkv[...].astype(F32), axis=0, keepdims=True)
    wide = jnp.concatenate([bias[:, :512], jnp.zeros((1, D - 512), F32)], axis=1)
    small_in[0, 0, 2:3, :] = jnp.where(t == 0, wide, pltpu.roll(wide, QW, 1))
    for c in range(2):
        small_in[0, 0, 3 + c:4 + c, :128] = jnp.where(t == c, bias[:, 512:], 0.0)

    def both(f, *a):
        for h in range(2):
            f(h, *a)

    small_step(0)
    both(middle_of, 0, 0)
    small_step(1)
    both(middle_of, 1, 0)
    small_step(2)
    both(middle_of, 2, 0)
    small_step(3)
    both(middle_of, 3, 0)
    small_step(4)
    both(second, 0)
    small_step(5)
    both(second, 1)
    small_step(6)
    both(middle_of, 0, 1)
    both(second, 2)
    both(middle_of, 1, 1)
    both(third, 0)
    both(second, 3)
    both(middle_of, 2, 1)
    both(third, 1)
    both(middle_of, 3, 1)
    both(third, 2)
    both(third_end, 0)
    both(third_end, 1)
    both(third, 3)
    both(third_end, 2)
    both(third_end, 3)
    for i in range(COUNT):
        for h in range(2):
            for stage in range(2):
                for k in range(6):
                    ring_copy(h, i, stage, k).wait_send()
            third_copy(h, i).wait_send()
    for k in range(6):
        small_copy(k).wait_send()

    @pl.when(pipe == 0)
    def _():
        pass_x.wait_send()

    @pl.when(pipe == 1)
    def _():
        pass_g.wait_send()


def run_train(lens, x, cot, g1, g2, bq, bkv, wq, wkv, wo, wgu, wd):
    vmem = pl.BlockSpec(memory_space=VMEM)
    hbm = pl.BlockSpec(memory_space=pl.ANY)
    dma = pltpu.SemaphoreType.DMA
    return pl.pallas_call(
        train_kernel,
        out_shape=(
            jax.ShapeDtypeStruct((MICRO, OWN, D), BF),
            jax.ShapeDtypeStruct((MICRO, OWN, D), F32),
            jax.ShapeDtypeStruct((28, HALF), F32),
            jax.ShapeDtypeStruct((28, HALF), F32),
            jax.ShapeDtypeStruct((8, D), F32),
        ),
        in_specs=[pl.BlockSpec(memory_space=pltpu.SMEM)] + [vmem] * 7 + [hbm] * 6,
        out_specs=(vmem,) * 5,
        scratch_shapes=[
            VMEM((512, D), BF), VMEM((D, 128), BF), VMEM((512, D), BF), VMEM((2, D, FH), BF), VMEM((FH, D), BF), VMEM((D, D), BF),
            VMEM((MICRO, 2, OWN, D), BF), VMEM((MICRO, 2, OWN, D), BF),
            VMEM((ROWS, D), BF), VMEM((ROWS, D), BF),
            VMEM((MICRO, OWN, D), BF), VMEM((MICRO, OWN, D), BF), VMEM((MICRO, OWN, D), BF),
            VMEM((ROWS, D), BF), VMEM((ROWS, D), BF),
            VMEM((MICRO, 4, CAP, 128), BF), VMEM((MICRO, 2, CAP, 128), BF), VMEM((MICRO, 2, CAP, 128), BF),
            VMEM((MICRO, 7, CAP, CAP), F32), VMEM((ROWS, 512), BF), VMEM((MICRO, 2, OWN, D), F32),
            VMEM((ROWS, FH), BF), VMEM((ROWS, FH), BF), VMEM((ROWS, FH), BF),
            VMEM((2, D, ROWS), BF), VMEM((MICRO, 2, OWN, D), F32), VMEM((MICRO, 2, OWN, D), F32),
            VMEM((MICRO, 3, CAP, 128), F32), VMEM((MICRO, CAP, CAP), F32), VMEM((ROWS, 640), BF),
            VMEM((ROWS, D), BF), VMEM((D, FH), BF), VMEM((D, 1152), BF),
            VMEM((2, 2, 112, HALF), BF), VMEM((2, 2, 2, 112, HALF), BF),
            VMEM((2, 4, 64, HALF), BF), VMEM((2, 2, 32, HALF), BF), VMEM((2, 2, 2, 32, HALF), BF),
            VMEM((2, 32, HALF), BF), VMEM((2, 32, HALF), BF), VMEM((2, 6, 8, D), F32),
            dma((6,)), dma((8,)), dma((8,)), dma((2, COUNT, 13)), dma((2, COUNT, 13)), dma((6,)), dma((6,)),
        ],
        compiler_params=pltpu.CompilerParams(collective_id=0, has_side_effects=True, vmem_limit_bytes=63 * MIB),
        name="train",
    )(lens, x, cot, g1, g2, bq, bkv, jnp.asarray(rope_table()), wq, wkv, wo, wgu, wd, jnp.asarray(row_order()))


def place_kernel(
    so_in, ig_in, sa_ref, sb_ref, small_ref,
    so_ref, ig_ref, gain1_ref, gq_ref, bq_ref, gkv_ref, bkv_ref, go_ref, gain2_ref, ggu_ref, gd_ref,
):
    so_ref[...] = so_in[...]
    ig_ref[...] = ig_in[...]
    gain1_ref[...] = small_ref[0:1, :]
    gain2_ref[...] = small_ref[1:2, :]
    bq_ref[...] = small_ref[2:3, :]
    bkv_ref[...] = small_ref[3:5, :128]
    gq_ref[:, 0, :] = sa_ref[:, A_Q:A_Q + QW]
    gkv_ref[:, 0, :] = sa_ref[:, A_KV:]
    go_ref[:, 0, :] = sa_ref[:, A_OUT:A_OUT + QW]
    gd_ref[:, 0, :] = sa_ref[:, :FH]
    ggu_ref[:, 0, :] = sb_ref[:, :FH]
    ggu_ref[:, 1, :UP_A] = sa_ref[:, A_UP:A_OUT]
    ggu_ref[:, 1, UP_A:] = sb_ref[:, B_UP:]


def run_place(*arrays):
    vmem = pl.BlockSpec(memory_space=VMEM)
    shapes = (
        (MICRO, OWN, D), (MICRO, OWN, D), (1, D), (28, 1, QW), (1, D), (28, 1, 128), (2, 128),
        (28, 1, QW), (1, D), (28, 2, FH), (28, 1, FH),
    )
    return pl.pallas_call(
        place_kernel,
        out_shape=tuple(jax.ShapeDtypeStruct(s, F32 if i else BF) for i, s in enumerate(shapes)),
        in_specs=[vmem] * 5,
        out_specs=(vmem,) * 11,
        compiler_params=pltpu.CompilerParams(vmem_limit_bytes=32 * MIB),
        name="place",
    )(*arrays)


def body(
    inputs, cotangent, lengths, gain_attn, w_query, b_query, w_keyval, b_keyval, w_out, gain_mlp, w_gate_up, w_down,
):
    outs = run_train(
        lengths[:, 0], inputs, cotangent, gain_attn, gain_mlp, b_query, b_keyval[0],
        jnp.swapaxes(w_query[0], 0, 1), w_keyval[0, :, 0], w_out[0],
        jnp.swapaxes(w_gate_up[0], 0, 1), w_down[0],
    )
    so, ig, gain1, gq, bq, gkv, bkv, go, gain2, ggu, gd = run_place(*outs)
    return (
        so[None], ig[None], gain1, jnp.swapaxes(gq, 0, 1), bq, gkv[None], bkv[None],
        jnp.transpose(go, (1, 2, 0)), gain2, ggu[None], jnp.transpose(gd, (1, 2, 0)),
    )


def solution(mesh):
    placed = (
        P(None, ("dp", "tensor"), None),
        P(None, ("dp", "tensor"), None),
        P(None, "dp", None),
        P("pipe", None),
        P("pipe", None, "tensor"),
        P("pipe", "tensor"),
        P("pipe", None, "tensor", None),
        P("pipe", "tensor", None),
        P("pipe", "tensor", None),
        P("pipe", None),
        P("pipe", None, None, "tensor"),
        P("pipe", "tensor", None),
    )
    return jax.shard_map(
        body,
        mesh=mesh,
        in_specs=placed,
        out_specs=(
            P("pipe", None, ("dp", "tensor"), None),
            P("pipe", None, ("dp", "tensor"), None),
            P("pipe", None),
            P("pipe", "dp", "tensor"),
            P("pipe", None),
            P("pipe", "dp", "tensor", None),
            P("pipe", None, None),
            P("pipe", "tensor", "dp"),
            P("pipe", None),
            P("pipe", "dp", None, "tensor"),
            P("pipe", "tensor", "dp"),
        ),
        check_vma=False,
    )
```

```python
import functools

import jax
import jax.numpy as jnp
import numpy as np
from jax import lax
from jax.experimental import pallas as pl
from jax.experimental.pallas import tpu as pltpu
from jax.sharding import PartitionSpec as P

D = 896
HEADS = 14
HEAD = 64
CAP = 128
SEQS = 4
MICRO = 2
ROWS = MICRO * CAP
OWN = CAP // 2
FH = 2432
QW = 448
EPS = 1e-06
THETA = 1000000.0
MIB = 1024 * 1024

BF = jnp.bfloat16
F32 = jnp.float32
MESH = pl.DeviceIdType.MESH
VMEM = pltpu.VMEM

PIECES = {
    "a0": ("down", 0, 640, 0), "a1": ("gate", 0, 896, 640), "a2": ("gate", 896, 896, 1536),
    "a3": ("out", 0, 512, 2432), "a4": ("qkv", 0, 640, 2944),
    "b0": ("down", 640, 640, 3584), "b1": ("up", 0, 896, 4224), "b2": ("up", 896, 896, 5120),
    "c0": ("down", 1280, 512, 0), "c1": ("down", 1792, 640, 512), "c2": ("gate", 1792, 640, 1152), "c3": ("up", 1792, 640, 1792),
}
NAMES = tuple(PIECES)
COLS_AB = 6016
COLS_C = 2432
SPLIT = {"c0": 256, "c1": 384, "c2": 256, "c3": 384}
SERVICE = (
    "m0:a0 m0:b0 cx:c0 m0:a1",
    "m0:b1 m0:a2 m0:b2 cx:c1",
    "m0:a3 s:b0 m0:c0 m0:a4",
    "cx:c2 s:b1 s:a0 s:b2",
    "m0:c1 s:a1 s:c0 m0:c2",
    "s:a2 cx:c3 m1:a0 s:a3",
    "m1:b0 s:c1 m1:a1 s:a4",
    "s:c2 m1:b1 m1:a2 m1:b2",
    "m0:c3 m1:c0 t:b0 m1:c1",
    "t:a0 m1:c2 m1:a3 t:b1",
    "e:b0 t:a1 t:b2 e:a0",
    "t:c0 m1:a4 t:c1 t:c2",
    "e:b1 t:a2 e:a1 s:c3",
    "t:a3 e:b2 t:a4 e:a2",
    "m1:c3 e:a3 e:a4 t:c3",
)
SERVICE = tuple(event for line in SERVICE for event in line.split())
TILES = ((0, 512), (512, 512), (1024, 512), (1536, 512), (2048, 384))
WIDE = ((0, 256), (256, 256), (512, 256), (768, 128))


def nn(a, b):
    return lax.dot_general(a, b, (((1,), (0,)), ((), ())), preferred_element_type=F32)


def nt(a, b):
    return lax.dot_general(a, b, (((1,), (1,)), ((), ())), preferred_element_type=F32)


def tn(a, b):
    return lax.dot_general(a, b, (((0,), (0,)), ((), ())), preferred_element_type=F32)


def rope_table():
    half = HEAD // 2
    frequency = np.power(np.float32(THETA), -(np.arange(half, dtype=np.float32) * np.float32(2.0 / HEAD)))
    phases = (np.arange(CAP, dtype=np.float32)[:, None] * frequency[None, :].astype(np.float32)).astype(np.float32)
    phases = phases.astype(np.float64)
    cosine = np.concatenate([np.cos(phases)] * 4, axis=1).astype(np.float32)
    sine = np.concatenate([-np.sin(phases), np.sin(phases)] * 2, axis=1).astype(np.float32)
    parts = []
    for table in (cosine, sine):
        rest = table
        for _ in range(3):
            piece = rest.astype(jnp.bfloat16)
            parts.append(piece)
            rest = rest - piece.astype(np.float32)
    return np.concatenate(parts, axis=1)


def row_order():
    index = np.arange(D)
    y, z, x_hi, k = index // 224, index // 56 % 4, index // 28 % 2, index % 28
    source = (x_hi * 16 + z * 4 + y) * 28 + k
    return (source[:, None] == np.arange(D)[None, :]).astype(jnp.bfloat16)


def turn(block, lane):
    low = (lane & 63) < 32
    return jnp.where(low, pltpu.roll(block, 96, 1), pltpu.roll(block, 32, 1))


def train_kernel(
    len_ref, x_ref, cot_ref, g1_ref, g2_ref, bq_ref, bkv_ref, tab_ref,
    wq_hbm, wkv_hbm, wo_hbm, wgu_hbm, wd_hbm, perm_hbm,
    so_ref, ig_ref, oab_ref, oc_ref, total_ref,
    wq, wkv, wo, wgu, wd, perm, xbuf, gbuf, e1s, e1r, e2s, e2r, pipe_out,
    n1, n2, qb, kb, vb, pmat, mix, middle, dgate, dup, hidden, lt, part, gmid, cs, allow, gqkv,
    lt_n, mb_ref, gdown, gout, gqkv_w,
    r1, r2, h2, q1, q2, h3, q3, cx, c1, c2, hc, d1, d2, small_in,
    load_sem, send_sem, recv_sem, sum_send, sum_recv, small_send, small_recv,
):
    pipe = lax.axis_index("pipe")
    t = lax.axis_index("tensor")
    rank = lax.axis_index("dp")
    other = 1 - t
    x_hi, z, y = rank // 16, (rank // 4) % 4, rank % 4
    pos = (y, z)

    loads = [
        pltpu.make_async_copy(wq_hbm, wq.at[pl.ds(0, QW)], load_sem.at[0]),
        pltpu.make_async_copy(wkv_hbm, wkv, load_sem.at[1]),
        pltpu.make_async_copy(wo_hbm, wo.at[pl.ds(0, QW)], load_sem.at[2]),
        pltpu.make_async_copy(wgu_hbm, wgu, load_sem.at[3]),
        pltpu.make_async_copy(wd_hbm, wd, load_sem.at[4]),
        pltpu.make_async_copy(perm_hbm, perm, load_sem.at[5]),
    ]
    for c in loads:
        c.start()

    def to_core(src, dst, i):
        return pltpu.make_async_remote_copy(
            src_ref=src, dst_ref=dst, send_sem=send_sem.at[i], recv_sem=recv_sem.at[i],
            device_id={"tensor": other}, device_id_type=MESH)

    def to_pipe(src, dst, i):
        return pltpu.make_async_remote_copy(
            src_ref=src, dst_ref=dst, send_sem=send_sem.at[i], recv_sem=recv_sem.at[i],
            device_id={"pipe": 1 - pipe}, device_id_type=MESH)

    share_x = to_core(xbuf.at[:, t], xbuf.at[:, t], 0)
    share_g = to_core(gbuf.at[:, t], gbuf.at[:, t], 1)
    pass_x = to_pipe(so_ref, xbuf.at[:, t], 2)
    pass_g = to_pipe(pipe_out, gbuf.at[:, t], 3)
    swap_1 = to_core(e1s, e1r, 4)
    swap_2 = to_core(e2s, e2r, 5)
    swap_3 = to_core(e1s, e1r, 6)
    swap_4 = to_core(e2s, e2r, 7)

    def at(yy, zz, xx):
        return {"dp": xx * 16 + zz * 4 + yy}

    def along(axis, step):
        if axis == 0:
            return at((y + step) % 4, z, x_hi)
        return at(y, (z + step) % 4, x_hi)

    x_peer = at(y, z, 1 - x_hi)
    peers = [along(0, 1), along(0, 3), along(1, 1), along(1, 3), x_peer, {"tensor": other}, {"pipe": 1 - pipe}]
    barrier = pltpu.get_barrier_semaphore()
    for peer in peers:
        pl.semaphore_signal(barrier, inc=1, device_id=peer, device_id_type=MESH)
    pl.semaphore_wait(barrier, len(peers))

    def remote(src, dst, peer, *sem):
        return pltpu.make_async_remote_copy(
            src_ref=src, dst_ref=dst, send_sem=sum_send.at[sem], recv_sem=sum_recv.at[sem],
            device_id=peer, device_id_type=MESH)

    bufs = {"down": gdown, "gate": wgu.at[0], "up": wgu.at[1], "out": gout, "qkv": gqkv_w}

    def columns(name, half=None):
        _, _, w, c = PIECES[name]
        if half is None:
            return pl.ds(c, w)
        cutoff = SPLIT[name]
        return pl.ds(c, cutoff) if half == 0 else pl.ds(c + cutoff, w - cutoff)

    def held(name, start, count):
        buf, c, w, _ = PIECES[name]
        return bufs[buf].at[pl.ds(pl.multiple_of(start, 16), count), pl.ds(c, w)]

    def ring(name, stage):
        if name[0] == "c":
            here = lambda half: columns(name, half)
            if stage == 0:
                return (1, lambda q, half: cx.at[pl.ds(pl.multiple_of(q * 112, 16), 112), here(half)],
                        lambda half: c1.at[:, here(half)], lambda k, half: c2.at[k, :, here(half)])
            return (0, lambda q, half: hc.at[q, :, here(half)],
                    lambda half: d1.at[:, here(half)], lambda k, half: d2.at[k, :, here(half)])
        axis = "ab".index(name[0])
        cols = columns(name)
        if stage == 0:
            return (axis, lambda q, half: held(name, q * 224 + 112 * half, 112),
                    lambda half: r1.at[half, :, cols], lambda k, half: r2.at[k, half, :, cols])
        return (1 - axis, lambda q, half: h2.at[q, pl.ds(32 * half, 32), cols],
                lambda half: q1.at[half, :, cols], lambda k, half: q2.at[k, half, :, cols])

    def ring_copy(name, stage, k):
        axis, block, first, last = ring(name, stage)
        f = pos[axis]
        ahead, behind = along(axis, 1), along(axis, 3)
        src, dst, peer = (
            lambda: (block((f + 2) % 4, 0), first(0), ahead),
            lambda: (block((f + 2) % 4, 1), first(1), behind),
            lambda: (block((f + 1) % 4, 1), last(0, 1), ahead),
            lambda: (block((f + 3) % 4, 0), last(1, 0), behind),
            lambda: (first(0), last(0, 0), ahead),
            lambda: (first(1), last(1, 1), behind),
        )[k]()
        return remote(src, dst, peer, NAMES.index(name), 6 * stage + k)

    def ring_begin(name, stage):
        for k in range(4):
            ring_copy(name, stage, k).start()

    def ring_middle(name, stage):
        axis, block, first, _ = ring(name, stage)
        f = pos[axis]
        for k, q in enumerate(((f + 1) % 4, (f + 3) % 4)):
            ring_copy(name, stage, k).wait_recv()
            own = block(q, k)[...]
            slot = first(k)
            slot[...] = (own.astype(F32) + slot[...].astype(F32)).astype(BF)
            ring_copy(name, stage, 4 + k).start()

    def ring_total(name, stage):
        axis, block, _, last = ring(name, stage)
        for k in range(2, 6):
            ring_copy(name, stage, k).wait_recv()
        return [
            block(pos[axis], half)[...].astype(F32) + last(0, half)[...].astype(F32) + last(1, half)[...].astype(F32)
            for half in range(2)]

    def x_copy(name):
        if name[0] == "c":
            return remote(held(name, (1 - x_hi) * 448, 448), cx.at[:, columns(name)], x_peer, NAMES.index(name), 12)
        cols = columns(name)
        return remote(h3.at[:, cols], q3.at[:, cols], x_peer, NAMES.index(name), 12)

    def begin(name):
        if name[0] == "c":
            x_copy(name).start()
        else:
            ring_begin(name, 0)

    def serve(event, name):
        cols = columns(name)
        if event == "cx":
            x_copy(name).wait_recv()
            own = held(name, x_hi * 448, 448)[...]
            cx[:, cols] = (own.astype(F32) + cx[:, cols].astype(F32)).astype(BF)
            ring_begin(name, 0)
        elif event == "m0":
            ring_middle(name, 0)
        elif event == "s":
            sums = ring_total(name, 0)
            for k in range(4):
                if name[0] == "c":
                    for half in range(2):
                        block = sums[half][28 * k:28 * k + 28]
                        zeros = jnp.zeros((4, block.shape[1]), F32)
                        hc[k, :, columns(name, half)] = jnp.concatenate([block, zeros], axis=0).astype(BF)
                else:
                    block = sums[k // 2][(k % 2) * 56:(k % 2 + 1) * 56]
                    zeros = jnp.zeros((8, block.shape[1]), F32)
                    h2[k, :, cols] = jnp.concatenate([block, zeros], axis=0).astype(BF)
            ring_begin(name, 1)
        elif event == "m1":
            ring_middle(name, 1)
        elif event == "t":
            sums = ring_total(name, 1)
            if name[0] == "c":
                for half in range(2):
                    oc_ref[:, columns(name, half)] = sums[half][:28]
            else:
                whole = jnp.concatenate(sums, axis=0)
                first, last = whole[:32], whole[28:60]
                upper = x_hi == 1
                h3[:, cols] = jnp.where(upper, first, last).astype(BF)
                oab_ref[:, cols] = jnp.where(upper, last, first)[:28]
                x_copy(name).start()
        else:
            x_copy(name).wait_recv()
            oab_ref[:, cols] = oab_ref[:, cols] + q3[:, cols].astype(F32)[:28]

    small_peers = [
        along(0, 1 + 2 * (y % 2)), along(0, 3 - 2 * (y % 2)),
        along(1, 1 + 2 * (z % 2)), along(1, 3 - 2 * (z % 2)), x_peer, {"tensor": other},
    ]

    def small_copy(k):
        return pltpu.make_async_remote_copy(
            src_ref=small_in.at[0, k], dst_ref=small_in.at[1, k], send_sem=small_send.at[k], recv_sem=small_recv.at[k],
            device_id=small_peers[k], device_id_type=MESH)

    def small_step(k):
        if k > 0:
            small_copy(k - 1).wait_recv()
            total = small_in[0, k - 1] + small_in[1, k - 1]
            if k < 6:
                small_in[0, k] = total
            else:
                total_ref[...] = total
        if k < 6:
            small_copy(k).start()

    @pl.when(pipe == 0)
    def _():
        xbuf[:, t] = x_ref[...]

    @pl.when(pipe == 1)
    def _():
        gbuf[:, t] = cot_ref[...]
        share_g.start()

    wq[pl.ds(QW, 64), :] = jnp.zeros((64, D), BF)
    wo[pl.ds(QW, 64), :] = jnp.zeros((64, D), BF)
    slot = lax.broadcasted_iota(jnp.int32, (CAP, CAP), 0)
    lane = lax.broadcasted_iota(jnp.int32, (CAP, CAP), 1)
    for m in range(MICRO):
        end = 0
        seg_row = jnp.zeros((CAP, CAP), jnp.int32)
        seg_col = jnp.zeros((CAP, CAP), jnp.int32)
        start = jnp.zeros((CAP, CAP), jnp.int32)
        for s in range(SEQS):
            end = end + len_ref[m, s]
            passed = slot >= end
            seg_row = seg_row + passed.astype(jnp.int32)
            seg_col = seg_col + (lane >= end).astype(jnp.int32)
            start = jnp.where(passed, end, start)
        allow[m] = jnp.where((seg_row == seg_col) & (lane <= slot), 1.0, 0.0)
        cs[m, 2] = jnp.where((seg_row < SEQS) | (pipe == 0), 1.0, 0.0)
        one_hot = jnp.where(slot - start == lane, 1.0, 0.0).astype(BF)
        table = nn(one_hot, tab_ref[...])
        cs[m, 0] = table[:, :128] + table[:, 128:256] + table[:, 256:384]
        cs[m, 1] = table[:, 384:512] + table[:, 512:640] + table[:, 640:768]
    bias_q = jnp.concatenate([bq_ref[...].astype(F32), jnp.zeros((1, 64), F32)], axis=1)
    bias_kv = bkv_ref[...].astype(F32)
    gain_1 = g1_ref[...].astype(F32)
    gain_2 = g2_ref[...].astype(F32)

    @pl.when(pipe == 1)
    def _():
        pass_x.wait_recv()

    share_x.start()
    share_x.wait()
    stream = xbuf[...].astype(F32).reshape(ROWS, D)
    inv = lax.rsqrt(jnp.mean(stream * stream, axis=-1, keepdims=True) + EPS)
    n1[...] = (stream * inv * gain_1).astype(BF)
    loads[0].wait()
    loads[1].wait()
    half_lane = lax.broadcasted_iota(jnp.int32, (CAP, 128), 1)
    for m in range(MICRO):
        rows = pl.ds(m * CAP, CAP)
        qs = nt(n1[rows, :], wq[...]) + bias_q
        vk = pltpu.roll(nn(n1[rows, :], wkv[...]) + bias_kv, 64, 1)
        for j in range(4):
            block = qs[:, j * 128:(j + 1) * 128]
            if j == 3:
                block = jnp.where(half_lane < 64, block, vk)
            block = block * cs[m, 0] + turn(block, half_lane) * cs[m, 1]
            qb[m, j] = block.astype(BF)
            if j == 3:
                odd = jnp.where(half_lane >= 64, block, 0.0)
                kb[m, 1] = odd.astype(BF)
                kb[m, 0] = pltpu.roll(odd, 64, 1).astype(BF)
        even = jnp.where(half_lane < 64, vk, 0.0)
        vb[m, 0] = even.astype(BF)
        vb[m, 1] = pltpu.roll(even, 64, 1).astype(BF)
    for m in range(MICRO):
        q_even = qb[m].reshape(4 * CAP, 128)
        q_odd = qb[m, :3].reshape(3 * CAP, 128)
        seen = allow[m] > 0.0
        mixed = []
        for parity, queries, count in ((0, q_even, 4), (1, q_odd, 3)):
            scores = nt(queries, kb[m, parity]).reshape(count, CAP, CAP) * HEAD ** (-0.5)
            scores = jnp.where(seen[None], scores, -1e30)
            top = jnp.max(scores, axis=-1, keepdims=True)
            grown = jnp.exp(scores - top)
            p = grown * (1.0 / jnp.sum(grown, axis=-1, keepdims=True))
            pmat[m, pl.ds(4 * parity, count)] = p
            mixed.append(nn(p.reshape(count * CAP, CAP).astype(BF), vb[m, parity]))
        for j in range(4):
            block = mixed[0][j * CAP:(j + 1) * CAP]
            if j < 3:
                block = block + mixed[1][j * CAP:(j + 1) * CAP]
            mix[pl.ds(m * CAP, CAP), j * 128:(j + 1) * 128] = block.astype(BF)
    loads[2].wait()
    for c, w in WIDE:
        e1s[:, c:c + w] = nn(mix[...], wo[:, c:c + w]).astype(BF)
    swap_1.start()
    swap_1.wait()
    mid = stream + (e1s[...].astype(F32) + e1r[...].astype(F32))
    middle[...] = mid.reshape(MICRO, 2, OWN, D)
    inv = lax.rsqrt(jnp.mean(mid * mid, axis=-1, keepdims=True) + EPS)
    n2[...] = (mid * inv * gain_2).astype(BF)
    loads[3].wait()
    for c, w in TILES:
        g = nn(n2[...], wgu[0, :, c:c + w])
        u = nn(n2[...], wgu[1, :, c:c + w])
        sig = jax.nn.sigmoid(g)
        silu = g * sig
        hidden[:, c:c + w] = (silu * u).astype(BF)
        dup[:, c:c + w] = silu.astype(BF)
        dgate[:, c:c + w] = (u * sig * (1.0 + g * (1.0 - sig))).astype(BF)
    loads[4].wait()
    for c, w in WIDE:
        part[:, :, :, c:c + w] = nn(hidden[...], wd[:, c:c + w]).reshape(MICRO, 2, OWN, w)
    e2s[...] = part[:, other].astype(BF)
    swap_2.start()
    swap_2.wait()
    so_ref[...] = (middle[:, t] + (part[:, t] + e2r[...].astype(F32))).astype(BF)

    def flips(rows, out):
        turned = nt(perm[...], rows)
        out[0] = turned.astype(BF)
        out[1] = jnp.concatenate(
            [turned[(4 * b + a) * 56:(4 * b + a + 1) * 56] for a in range(4) for b in range(4)], axis=0).astype(BF)
        out[2] = rows.astype(F32).T.astype(BF)

    loads[5].wait()

    @pl.when(pipe == 0)
    def _():
        pass_x.start()
        flips(n2[...], lt_n)
        pass_g.wait_recv()
        share_g.start()

    share_g.wait()
    for m in range(MICRO):
        live = cs[m, 2][:, :1].astype(BF).reshape(2, OWN, 1)
        gbuf[m] = gbuf[m] * live

    def weights_down():
        flips(gbuf[...].reshape(ROWS, D), lt)
        for name, order in (("c0", 2), ("a0", 0), ("b0", 1), ("c1", 2)):
            _, c, w, _ = PIECES[name]
            gdown[:, c:c + w] = nn(lt[order], hidden[:, c:c + w]).astype(BF)
            begin(name)

    def weights_gate_up():
        for name, order in (("a1", 0), ("b1", 1), ("c2", 2), ("a2", 0), ("b2", 1), ("c3", 2)):
            buf, c, w, _ = PIECES[name]
            which, rhs = ((0, dgate), (1, dup))[buf == "up"]
            wgu[which, :, c:c + w] = nn(lt_n[order], rhs[:, c:c + w]).astype(BF)
            begin(name)

    def weights_out():
        lt[0] = nt(perm[...], mb_ref[...]).astype(BF)
        gout[...] = nn(lt[0], mix[...]).astype(BF)
        begin("a3")

    @pl.when(pipe == 0)
    def _():
        weights_down()

    grad = gbuf[...].reshape(ROWS, D)
    for c, w in TILES:
        gh = nt(grad, wd[c:c + w, :])
        dgate[:, c:c + w] = (gh * dgate[:, c:c + w].astype(F32)).astype(BF)
        dup[:, c:c + w] = (gh * dup[:, c:c + w].astype(F32)).astype(BF)
    for c, w in WIDE:
        e1s[:, c:c + w] = (nt(dgate[...], wgu[0, c:c + w, :]) + nt(dup[...], wgu[1, c:c + w, :])).astype(BF)
    swap_3.start()

    @pl.when(pipe == 0)
    def _():
        weights_gate_up()

    swap_3.wait()

    def norm_back(grads, values, gain):
        inverse = lax.rsqrt(jnp.mean(values * values, axis=-1, keepdims=True) + EPS)
        scaled = values * inverse
        weighted = grads * gain
        back = inverse * (weighted - scaled * jnp.mean(weighted * scaled, axis=-1, keepdims=True))
        return back, grads * scaled

    grads = e1s[...].astype(F32) + e1r[...].astype(F32)
    back, terms = norm_back(grads, middle[...].reshape(ROWS, D), gain_2)
    row = lax.broadcasted_iota(jnp.int32, (ROWS, 1), 0)
    mine = ((row >> 6) & 1) == t
    small_in[0, 0] = jnp.zeros((8, D), F32)
    small_in[0, 0, 1:2, :] = jnp.sum(jnp.where(mine, terms, 0.0), axis=0, keepdims=True)
    grad_mid = gbuf[...].reshape(ROWS, D).astype(F32) + back
    gmid[...] = grad_mid.reshape(MICRO, 2, OWN, D)
    mb_ref[...] = grad_mid.astype(BF)

    @pl.when(pipe == 0)
    def _():
        weights_out()

    gmix = nt(mb_ref[...], wo[...]).astype(BF)
    for m in range(MICRO):
        blocks = [gmix[m * CAP:(m + 1) * CAP, j * 128:(j + 1) * 128] for j in range(4)]
        q_even = qb[m].reshape(4 * CAP, 128)
        q_odd = qb[m, :3].reshape(3 * CAP, 128)
        out = []
        for parity, queries, count in ((0, q_even, 4), (1, q_odd, 3)):
            gm = jnp.concatenate(blocks[:count], axis=0)
            p = pmat[m, pl.ds(4 * parity, count)].reshape(count * CAP, CAP)
            gp = nt(gm, vb[m, parity])
            ds = (p * (gp - jnp.sum(p * gp, axis=-1, keepdims=True))).astype(BF)
            out.append((nn(ds, kb[m, parity]), tn(ds, queries), tn(p.astype(BF), gm)))
        keys = pltpu.roll(out[0][1], 64, 1) + out[1][1]
        values = out[0][2] + pltpu.roll(out[1][2], 64, 1)
        rows = pl.ds(m * CAP, CAP)
        for j in range(4):
            block = out[0][0][j * CAP:(j + 1) * CAP]
            if j < 3:
                block = block + out[1][0][j * CAP:(j + 1) * CAP]
            else:
                block = jnp.where(half_lane < 64, block, keys)
            block = block * HEAD ** (-0.5)
            block = block * cs[m, 0] - turn(block, half_lane) * cs[m, 1]
            if j == 3:
                gqkv[rows, 512:640] = pltpu.roll(jnp.where(half_lane < 64, values, block), 64, 1).astype(BF)
                block = jnp.where(half_lane < 64, block, 0.0)
            gqkv[rows, j * 128:(j + 1) * 128] = block.astype(BF)
    for c, w in WIDE:
        part[:, :, :, c:c + w] = (
            nn(gqkv[:, :512], wq[:, c:c + w]) + nt(gqkv[:, 512:], wkv[c:c + w, :])).reshape(MICRO, 2, OWN, w)
    e2s[...] = part[:, other].astype(BF)
    swap_4.start()
    swap_4.wait()
    grads = (part[:, t] + e2r[...].astype(F32)).reshape(MICRO * OWN, D)
    back, terms = norm_back(grads, xbuf[:, t].astype(F32).reshape(MICRO * OWN, D), gain_1)
    total = gmid[:, t] + back.reshape(MICRO, OWN, D)
    ig_ref[...] = total
    pipe_out[...] = total.astype(BF)

    @pl.when(pipe == 1)
    def _():
        pass_g.start()

    @pl.when(pipe == 1)
    def _():
        weights_down()
        flips(n2[...], lt_n)
        weights_gate_up()
        weights_out()

    lt[1] = nt(perm[...], n1[...]).astype(BF)
    gqkv_w[...] = nn(lt[1], gqkv[...]).astype(BF)
    begin("a4")
    small_in[0, 0, 0:1, :] = jnp.sum(terms, axis=0, keepdims=True)
    bias = jnp.sum(gqkv[...].astype(F32), axis=0, keepdims=True)
    wide = jnp.concatenate([bias[:, :512], jnp.zeros((1, D - 512), F32)], axis=1)
    small_in[0, 0, 2:3, :] = jnp.where(t == 0, wide, pltpu.roll(wide, QW, 1))
    for c in range(2):
        small_in[0, 0, 3 + c:4 + c, :128] = jnp.where(t == c, bias[:, 512:], 0.0)

    for step, event in enumerate(SERVICE):
        if step % 4 == 0 and step < 28:
            small_step(step // 4)
        serve(*event.split(":"))
    for name in NAMES:
        for stage in range(2):
            for k in range(6):
                ring_copy(name, stage, k).wait_send()
        x_copy(name).wait_send()
    for k in range(6):
        small_copy(k).wait_send()

    @pl.when(pipe == 0)
    def _():
        pass_x.wait_send()

    @pl.when(pipe == 1)
    def _():
        pass_g.wait_send()


def run_train(lens, x, cot, g1, g2, bq, bkv, wq, wkv, wo, wgu, wd):
    vmem = pl.BlockSpec(memory_space=VMEM)
    hbm = pl.BlockSpec(memory_space=pl.ANY)
    dma = pltpu.SemaphoreType.DMA
    return pl.pallas_call(
        train_kernel,
        out_shape=(
            jax.ShapeDtypeStruct((MICRO, OWN, D), BF),
            jax.ShapeDtypeStruct((MICRO, OWN, D), F32),
            jax.ShapeDtypeStruct((28, COLS_AB), F32),
            jax.ShapeDtypeStruct((28, COLS_C), F32),
            jax.ShapeDtypeStruct((8, D), F32),
        ),
        in_specs=[pl.BlockSpec(memory_space=pltpu.SMEM)] + [vmem] * 7 + [hbm] * 6,
        out_specs=(vmem,) * 5,
        scratch_shapes=[
            VMEM((512, D), BF), VMEM((D, 128), BF), VMEM((512, D), BF), VMEM((2, D, FH), BF), VMEM((FH, D), BF), VMEM((D, D), BF),
            VMEM((MICRO, 2, OWN, D), BF), VMEM((MICRO, 2, OWN, D), BF),
            VMEM((ROWS, D), BF), VMEM((ROWS, D), BF),
            VMEM((MICRO, OWN, D), BF), VMEM((MICRO, OWN, D), BF), VMEM((MICRO, OWN, D), BF),
            VMEM((ROWS, D), BF), VMEM((ROWS, D), BF),
            VMEM((MICRO, 4, CAP, 128), BF), VMEM((MICRO, 2, CAP, 128), BF), VMEM((MICRO, 2, CAP, 128), BF),
            VMEM((MICRO, 7, CAP, CAP), F32), VMEM((ROWS, 512), BF), VMEM((MICRO, 2, OWN, D), F32),
            VMEM((ROWS, FH), BF), VMEM((ROWS, FH), BF), VMEM((ROWS, FH), BF),
            VMEM((3, D, ROWS), BF), VMEM((MICRO, 2, OWN, D), F32), VMEM((MICRO, 2, OWN, D), F32),
            VMEM((MICRO, 3, CAP, 128), F32), VMEM((MICRO, CAP, CAP), F32), VMEM((ROWS, 640), BF),
            VMEM((3, D, ROWS), BF), VMEM((ROWS, D), BF), VMEM((D, FH), BF), VMEM((D, 512), BF), VMEM((D, 640), BF),
            VMEM((2, 112, COLS_AB), BF), VMEM((2, 2, 112, COLS_AB), BF),
            VMEM((4, 64, COLS_AB), BF), VMEM((2, 32, COLS_AB), BF), VMEM((2, 2, 32, COLS_AB), BF),
            VMEM((32, COLS_AB), BF), VMEM((32, COLS_AB), BF),
            VMEM((448, COLS_C), BF), VMEM((112, COLS_C), BF), VMEM((2, 112, COLS_C), BF),
            VMEM((4, 32, COLS_C), BF), VMEM((32, COLS_C), BF), VMEM((2, 32, COLS_C), BF),
            VMEM((2, 6, 8, D), F32),
            dma((6,)), dma((8,)), dma((8,)), dma((len(NAMES), 13)), dma((len(NAMES), 13)), dma((6,)), dma((6,)),
        ],
        compiler_params=pltpu.CompilerParams(collective_id=0, has_side_effects=True, vmem_limit_bytes=63 * MIB),
        name="train",
    )(lens, x, cot, g1, g2, bq, bkv, jnp.asarray(rope_table()), wq, wkv, wo, wgu, wd, jnp.asarray(row_order()))


def place_kernel(
    so_in, ig_in, sab_ref, sc_ref, small_ref,
    so_ref, ig_ref, gain1_ref, gq_ref, bq_ref, gkv_ref, bkv_ref, go_ref, gain2_ref, ggu_ref, gd_ref,
):
    so_ref[...] = so_in[...]
    ig_ref[...] = ig_in[...]
    gain1_ref[...] = small_ref[0:1, :]
    gain2_ref[...] = small_ref[1:2, :]
    bq_ref[...] = small_ref[2:3, :]
    bkv_ref[...] = small_ref[3:5, :128]
    gq_ref[:, 0, :] = sab_ref[:, 2944:2944 + QW]
    gkv_ref[:, 0, :] = sab_ref[:, 3456:3584]
    go_ref[:, 0, :] = sab_ref[:, 2432:2432 + QW]
    gd_ref[:, 0, :640] = sab_ref[:, :640]
    gd_ref[:, 0, 640:1280] = sab_ref[:, 3584:4224]
    gd_ref[:, 0, 1280:] = sc_ref[:, :1152]
    ggu_ref[:, 0, :1792] = sab_ref[:, 640:2432]
    ggu_ref[:, 0, 1792:] = sc_ref[:, 1152:1792]
    ggu_ref[:, 1, :1792] = sab_ref[:, 4224:6016]
    ggu_ref[:, 1, 1792:] = sc_ref[:, 1792:]


def run_place(*arrays):
    vmem = pl.BlockSpec(memory_space=VMEM)
    shapes = (
        (MICRO, OWN, D), (MICRO, OWN, D), (1, D), (28, 1, QW), (1, D), (28, 1, 128), (2, 128),
        (28, 1, QW), (1, D), (28, 2, FH), (28, 1, FH),
    )
    return pl.pallas_call(
        place_kernel,
        out_shape=tuple(jax.ShapeDtypeStruct(s, F32 if i else BF) for i, s in enumerate(shapes)),
        in_specs=[vmem] * 5,
        out_specs=(vmem,) * 11,
        compiler_params=pltpu.CompilerParams(vmem_limit_bytes=60 * MIB),
        name="place",
    )(*arrays)


def body(
    inputs, cotangent, lengths, gain_attn, w_query, b_query, w_keyval, b_keyval, w_out, gain_mlp, w_gate_up, w_down,
):
    outs = run_train(
        lengths[:, 0], inputs, cotangent, gain_attn, gain_mlp, b_query, b_keyval[0],
        jnp.swapaxes(w_query[0], 0, 1), w_keyval[0, :, 0], w_out[0],
        jnp.swapaxes(w_gate_up[0], 0, 1), w_down[0],
    )
    so, ig, gain1, gq, bq, gkv, bkv, go, gain2, ggu, gd = run_place(*outs)
    return (
        so[None], ig[None], gain1, jnp.swapaxes(gq, 0, 1), bq, gkv[None], bkv[None],
        jnp.transpose(go, (1, 2, 0)), gain2, ggu[None], jnp.transpose(gd, (1, 2, 0)),
    )


def solution(mesh):
    placed = (
        P(None, ("dp", "tensor"), None),
        P(None, ("dp", "tensor"), None),
        P(None, "dp", None),
        P("pipe", None),
        P("pipe", None, "tensor"),
        P("pipe", "tensor"),
        P("pipe", None, "tensor", None),
        P("pipe", "tensor", None),
        P("pipe", "tensor", None),
        P("pipe", None),
        P("pipe", None, None, "tensor"),
        P("pipe", "tensor", None),
    )
    return jax.shard_map(
        body,
        mesh=mesh,
        in_specs=placed,
        out_specs=(
            P("pipe", None, ("dp", "tensor"), None),
            P("pipe", None, ("dp", "tensor"), None),
            P("pipe", None),
            P("pipe", "dp", "tensor"),
            P("pipe", None),
            P("pipe", "dp", "tensor", None),
            P("pipe", None, None),
            P("pipe", "tensor", "dp"),
            P("pipe", None),
            P("pipe", "dp", None, "tensor"),
            P("pipe", "tensor", "dp"),
        ),
        check_vma=False,
    )
```

```python
import functools

import jax
import jax.numpy as jnp
import numpy as np
from jax import lax
from jax.experimental import pallas as pl
from jax.experimental.pallas import tpu as pltpu
from jax.sharding import PartitionSpec as P

D = 896
HEADS = 14
HEAD = 64
CAP = 128
SEQS = 4
MICRO = 2
ROWS = MICRO * CAP
OWN = CAP // 2
FH = 2432
QW = 448
EPS = 1e-06
THETA = 1000000.0
MIB = 1024 * 1024

BF = jnp.bfloat16
F32 = jnp.float32
MESH = pl.DeviceIdType.MESH
VMEM = pltpu.VMEM

PIECES = {
    "a0": ("down", 0, 640, 0), "a1": ("gate", 0, 896, 640), "a2": ("gate", 896, 1152, 1536),
    "a3": ("out", 0, 512, 2688), "a4": ("qkv", 0, 640, 3200),
    "b0": ("down", 640, 640, 3840), "b1": ("up", 0, 896, 4480), "b2": ("up", 896, 1280, 5376),
    "c0": ("down", 1280, 512, 0), "c1": ("down", 1792, 640, 512), "c2": ("gate", 2048, 384, 1152), "c3": ("up", 2176, 256, 1536),
}
NAMES = tuple(PIECES)
COLS_AB = 6656
COLS_C = 1792
SPLIT = {"c0": 256, "c1": 256, "c2": 256, "c3": 128}
SERVICE = (
    "cx:c0 m0:a0 m0:a1 m0:b0",
    "m0:b1 m0:a2 m0:b2 m0:a3",
    "m0:c0 cx:c1 s:b0 m0:a4",
    "s:b1 cx:c2 s:a0 s:b2",
    "s:a1 s:c0 cx:c3 m0:c1",
    "m0:c2 s:a2 m1:a0 s:a3",
    "m1:a1 m1:b0 m0:c3 s:c1",
    "s:a4 s:c2 m1:b1 m1:a2",
    "m1:b2 t:a0 m1:a3 m1:c0",
    "t:a1 t:b0 e:a0 s:c3",
    "m1:c1 m1:a4 m1:c2 t:b1",
    "e:a1 t:a2 t:a3 e:b0",
    "t:b2 t:c0 m1:c3 t:a4",
    "t:c1 t:c2 e:b1 t:c3",
    "e:a2 e:a3 e:b2 e:a4",
)
SERVICE = tuple(event for line in SERVICE for event in line.split())
TILES = ((0, 512), (512, 512), (1024, 512), (1536, 512), (2048, 384))
WIDE = ((0, 256), (256, 256), (512, 256), (768, 128))


def nn(a, b):
    return lax.dot_general(a, b, (((1,), (0,)), ((), ())), preferred_element_type=F32)


def nt(a, b):
    return lax.dot_general(a, b, (((1,), (1,)), ((), ())), preferred_element_type=F32)


def tn(a, b):
    return lax.dot_general(a, b, (((0,), (0,)), ((), ())), preferred_element_type=F32)


def rope_table():
    half = HEAD // 2
    frequency = np.power(np.float32(THETA), -(np.arange(half, dtype=np.float32) * np.float32(2.0 / HEAD)))
    phases = (np.arange(CAP, dtype=np.float32)[:, None] * frequency[None, :].astype(np.float32)).astype(np.float32)
    phases = phases.astype(np.float64)
    cosine = np.concatenate([np.cos(phases)] * 4, axis=1).astype(np.float32)
    sine = np.concatenate([-np.sin(phases), np.sin(phases)] * 2, axis=1).astype(np.float32)
    parts = []
    for table in (cosine, sine):
        rest = table
        for _ in range(3):
            piece = rest.astype(jnp.bfloat16)
            parts.append(piece)
            rest = rest - piece.astype(np.float32)
    return np.concatenate(parts, axis=1)


def row_order():
    index = np.arange(D)
    y, z, x_hi, k = index // 224, index // 56 % 4, index // 28 % 2, index % 28
    source = (x_hi * 16 + z * 4 + y) * 28 + k
    return (source[:, None] == np.arange(D)[None, :]).astype(jnp.bfloat16)


def turn(block, lane):
    low = (lane & 63) < 32
    return jnp.where(low, pltpu.roll(block, 96, 1), pltpu.roll(block, 32, 1))


def train_kernel(
    len_ref, x_ref, cot_ref, g1_ref, g2_ref, bq_ref, bkv_ref, tab_ref,
    wq_hbm, wkv_hbm, wo_hbm, wgu_hbm, wd_hbm, perm_hbm,
    sums_ref, rows_ref,
    wq, wkv, wo, wgu, wd, perm, xbuf, gbuf, e1s, e1r, e2s, e2r, pipe_out,
    n1, n2, qb, kb, vb, pmat, mix, middle, dgate, dup, hidden, lt, part, gmid, cs, allow, gqkv,
    lt_n, mb_ref, gdown, gout, gqkv_w,
    r1, r2, h2, q1, q2, h3, q3, cx, c1, c2, hc, d1, d2, small_in,
    load_sem, send_sem, recv_sem, sum_send, sum_recv, small_send, small_recv,
):
    pipe = lax.axis_index("pipe")
    t = lax.axis_index("tensor")
    rank = lax.axis_index("dp")
    other = 1 - t
    x_hi, z, y = rank // 16, (rank // 4) % 4, rank % 4
    pos = (y, z)

    loads = [
        pltpu.make_async_copy(wq_hbm, wq.at[pl.ds(0, QW)], load_sem.at[0]),
        pltpu.make_async_copy(wkv_hbm, wkv, load_sem.at[1]),
        pltpu.make_async_copy(wo_hbm, wo.at[pl.ds(0, QW)], load_sem.at[2]),
        pltpu.make_async_copy(wgu_hbm, wgu, load_sem.at[3]),
        pltpu.make_async_copy(wd_hbm, wd, load_sem.at[4]),
        pltpu.make_async_copy(perm_hbm, perm, load_sem.at[5]),
    ]
    for c in loads:
        c.start()

    def to_core(src, dst, i):
        return pltpu.make_async_remote_copy(
            src_ref=src, dst_ref=dst, send_sem=send_sem.at[i], recv_sem=recv_sem.at[i],
            device_id={"tensor": other}, device_id_type=MESH)

    def to_pipe(src, dst, i):
        return pltpu.make_async_remote_copy(
            src_ref=src, dst_ref=dst, send_sem=send_sem.at[i], recv_sem=recv_sem.at[i],
            device_id={"pipe": 1 - pipe}, device_id_type=MESH)

    share_x = to_core(xbuf.at[:, t], xbuf.at[:, t], 0)
    share_g = to_core(gbuf.at[:, t], gbuf.at[:, t], 1)
    pass_x = to_pipe(pipe_out, xbuf.at[:, t], 2)
    pass_g = to_pipe(pipe_out, gbuf.at[:, t], 3)
    swap_1 = to_core(e1s, e1r, 4)
    swap_2 = to_core(e2s, e2r, 5)
    swap_3 = to_core(e1s, e1r, 6)
    swap_4 = to_core(e2s, e2r, 7)

    def at(yy, zz, xx):
        return {"dp": xx * 16 + zz * 4 + yy}

    def along(axis, step):
        if axis == 0:
            return at((y + step) % 4, z, x_hi)
        return at(y, (z + step) % 4, x_hi)

    x_peer = at(y, z, 1 - x_hi)
    peers = [along(0, 1), along(0, 3), along(1, 1), along(1, 3), x_peer, {"tensor": other}, {"pipe": 1 - pipe}]
    barrier = pltpu.get_barrier_semaphore()
    for peer in peers:
        pl.semaphore_signal(barrier, inc=1, device_id=peer, device_id_type=MESH)
    pl.semaphore_wait(barrier, len(peers))

    def remote(src, dst, peer, *sem):
        return pltpu.make_async_remote_copy(
            src_ref=src, dst_ref=dst, send_sem=sum_send.at[sem], recv_sem=sum_recv.at[sem],
            device_id=peer, device_id_type=MESH)

    bufs = {"down": gdown, "gate": wgu.at[0], "up": wgu.at[1], "out": gout, "qkv": gqkv_w}

    def columns(name, half=None):
        _, _, w, c = PIECES[name]
        if half is None:
            return pl.ds(c, w)
        cutoff = SPLIT[name]
        return pl.ds(c, cutoff) if half == 0 else pl.ds(c + cutoff, w - cutoff)

    def held(name, start, count):
        buf, c, w, _ = PIECES[name]
        return bufs[buf].at[pl.ds(pl.multiple_of(start, 16), count), pl.ds(c, w)]

    def ring(name, stage):
        if name[0] == "c":
            here = lambda half: columns(name, half)
            if stage == 0:
                return (1, lambda q, half: cx.at[pl.ds(pl.multiple_of(q * 112, 16), 112), here(half)],
                        lambda half: c1.at[:, here(half)], lambda k, half: c2.at[k, :, here(half)])
            return (0, lambda q, half: hc.at[q, :, here(half)],
                    lambda half: d1.at[:, here(half)], lambda k, half: d2.at[k, :, here(half)])
        axis = "ab".index(name[0])
        cols = columns(name)
        if stage == 0:
            return (axis, lambda q, half: held(name, q * 224 + 112 * half, 112),
                    lambda half: r1.at[half, :, cols], lambda k, half: r2.at[k, half, :, cols])
        return (1 - axis, lambda q, half: h2.at[q, pl.ds(32 * half, 32), cols],
                lambda half: q1.at[half, :, cols], lambda k, half: q2.at[k, half, :, cols])

    def ring_copy(name, stage, k):
        axis, block, first, last = ring(name, stage)
        f = pos[axis]
        ahead, behind = along(axis, 1), along(axis, 3)
        src, dst, peer = (
            lambda: (block((f + 2) % 4, 0), first(0), ahead),
            lambda: (block((f + 2) % 4, 1), first(1), behind),
            lambda: (block((f + 1) % 4, 1), last(0, 1), ahead),
            lambda: (block((f + 3) % 4, 0), last(1, 0), behind),
            lambda: (first(0), last(0, 0), ahead),
            lambda: (first(1), last(1, 1), behind),
        )[k]()
        return remote(src, dst, peer, NAMES.index(name), 6 * stage + k)

    def ring_begin(name, stage):
        for k in range(4):
            ring_copy(name, stage, k).start()

    def ring_middle(name, stage):
        axis, block, first, _ = ring(name, stage)
        f = pos[axis]
        for k, q in enumerate(((f + 1) % 4, (f + 3) % 4)):
            ring_copy(name, stage, k).wait_recv()
            own = block(q, k)[...]
            slot = first(k)
            slot[...] = (own.astype(F32) + slot[...].astype(F32)).astype(BF)
            ring_copy(name, stage, 4 + k).start()

    def ring_total(name, stage):
        axis, block, _, last = ring(name, stage)
        for k in range(2, 6):
            ring_copy(name, stage, k).wait_recv()
        return [
            block(pos[axis], half)[...].astype(F32) + last(0, half)[...].astype(F32) + last(1, half)[...].astype(F32)
            for half in range(2)]

    def x_copy(name):
        if name[0] == "c":
            return remote(held(name, (1 - x_hi) * 448, 448), cx.at[:, columns(name)], x_peer, NAMES.index(name), 12)
        cols = columns(name)
        return remote(h3.at[:, cols], q3.at[:, cols], x_peer, NAMES.index(name), 12)

    def begin(name):
        if name[0] == "c":
            x_copy(name).start()
        else:
            ring_begin(name, 0)

    def serve(event, name):
        cols = columns(name)
        if event == "cx":
            x_copy(name).wait_recv()
            own = held(name, x_hi * 448, 448)[...]
            cx[:, cols] = (own.astype(F32) + cx[:, cols].astype(F32)).astype(BF)
            ring_begin(name, 0)
        elif event == "m0":
            ring_middle(name, 0)
        elif event == "s":
            sums = ring_total(name, 0)
            for k in range(4):
                if name[0] == "c":
                    for half in range(2):
                        block = sums[half][28 * k:28 * k + 28]
                        zeros = jnp.zeros((4, block.shape[1]), F32)
                        hc[k, :, columns(name, half)] = jnp.concatenate([block, zeros], axis=0).astype(BF)
                else:
                    block = sums[k // 2][(k % 2) * 56:(k % 2 + 1) * 56]
                    zeros = jnp.zeros((8, block.shape[1]), F32)
                    h2[k, :, cols] = jnp.concatenate([block, zeros], axis=0).astype(BF)
            ring_begin(name, 1)
        elif event == "m1":
            ring_middle(name, 1)
        elif event == "t":
            sums = ring_total(name, 1)
            if name[0] == "c":
                for half in range(2):
                    at = columns(name, half)
                    sums_ref[:28, pl.ds(COLS_AB + at.start, at.size)] = sums[half][:28]
            else:
                whole = jnp.concatenate(sums, axis=0)
                first, last = whole[:32], whole[28:60]
                upper = x_hi == 1
                h3[:, cols] = jnp.where(upper, first, last).astype(BF)
                sums_ref[:28, cols] = jnp.where(upper, last, first)[:28]
                x_copy(name).start()
        else:
            x_copy(name).wait_recv()
            sums_ref[:28, cols] = sums_ref[:28, cols] + q3[:, cols].astype(F32)[:28]

    small_peers = [
        along(0, 1 + 2 * (y % 2)), along(0, 3 - 2 * (y % 2)),
        along(1, 1 + 2 * (z % 2)), along(1, 3 - 2 * (z % 2)), x_peer, {"tensor": other},
    ]

    def small_copy(k):
        return pltpu.make_async_remote_copy(
            src_ref=small_in.at[0, k], dst_ref=small_in.at[1, k], send_sem=small_send.at[k], recv_sem=small_recv.at[k],
            device_id=small_peers[k], device_id_type=MESH)

    def small_step(k):
        if k > 0:
            small_copy(k - 1).wait_recv()
            total = small_in[0, k - 1] + small_in[1, k - 1]
            if k < 6:
                small_in[0, k] = total
            else:
                sums_ref[32:40, :D] = total
        if k < 6:
            small_copy(k).start()

    @pl.when(pipe == 0)
    def _():
        xbuf[:, t] = x_ref[...]

    @pl.when(pipe == 1)
    def _():
        gbuf[:, t] = cot_ref[...]
        share_g.start()

    wq[pl.ds(QW, 64), :] = jnp.zeros((64, D), BF)
    wo[pl.ds(QW, 64), :] = jnp.zeros((64, D), BF)
    slot = lax.broadcasted_iota(jnp.int32, (CAP, CAP), 0)
    lane = lax.broadcasted_iota(jnp.int32, (CAP, CAP), 1)
    for m in range(MICRO):
        end = 0
        seg_row = jnp.zeros((CAP, CAP), jnp.int32)
        seg_col = jnp.zeros((CAP, CAP), jnp.int32)
        start = jnp.zeros((CAP, CAP), jnp.int32)
        for s in range(SEQS):
            end = end + len_ref[m, s]
            passed = slot >= end
            seg_row = seg_row + passed.astype(jnp.int32)
            seg_col = seg_col + (lane >= end).astype(jnp.int32)
            start = jnp.where(passed, end, start)
        allow[m] = jnp.where((seg_row == seg_col) & (lane <= slot), 1.0, 0.0)
        cs[m, 2] = jnp.where((seg_row < SEQS) | (pipe == 0), 1.0, 0.0)
        one_hot = jnp.where(slot - start == lane, 1.0, 0.0).astype(BF)
        table = nn(one_hot, tab_ref[...])
        cs[m, 0] = table[:, :128] + table[:, 128:256] + table[:, 256:384]
        cs[m, 1] = table[:, 384:512] + table[:, 512:640] + table[:, 640:768]
    bias_q = jnp.concatenate([bq_ref[...].astype(F32), jnp.zeros((1, 64), F32)], axis=1)
    bias_kv = bkv_ref[...].astype(F32)
    gain_1 = g1_ref[...].astype(F32)
    gain_2 = g2_ref[...].astype(F32)

    @pl.when(pipe == 1)
    def _():
        pass_x.wait_recv()

    share_x.start()
    share_x.wait()
    stream = xbuf[...].astype(F32).reshape(ROWS, D)
    inv = lax.rsqrt(jnp.mean(stream * stream, axis=-1, keepdims=True) + EPS)
    n1[...] = (stream * inv * gain_1).astype(BF)
    loads[0].wait()
    loads[1].wait()
    half_lane = lax.broadcasted_iota(jnp.int32, (CAP, 128), 1)
    for m in range(MICRO):
        rows = pl.ds(m * CAP, CAP)
        qs = nt(n1[rows, :], wq[...]) + bias_q
        vk = pltpu.roll(nn(n1[rows, :], wkv[...]) + bias_kv, 64, 1)
        for j in range(4):
            block = qs[:, j * 128:(j + 1) * 128]
            if j == 3:
                block = jnp.where(half_lane < 64, block, vk)
            block = block * cs[m, 0] + turn(block, half_lane) * cs[m, 1]
            qb[m, j] = block.astype(BF)
            if j == 3:
                odd = jnp.where(half_lane >= 64, block, 0.0)
                kb[m, 1] = odd.astype(BF)
                kb[m, 0] = pltpu.roll(odd, 64, 1).astype(BF)
        even = jnp.where(half_lane < 64, vk, 0.0)
        vb[m, 0] = even.astype(BF)
        vb[m, 1] = pltpu.roll(even, 64, 1).astype(BF)
    for m in range(MICRO):
        q_even = qb[m].reshape(4 * CAP, 128)
        q_odd = qb[m, :3].reshape(3 * CAP, 128)
        seen = allow[m] > 0.0
        mixed = []
        for parity, queries, count in ((0, q_even, 4), (1, q_odd, 3)):
            scores = nt(queries, kb[m, parity]).reshape(count, CAP, CAP) * HEAD ** (-0.5)
            scores = jnp.where(seen[None], scores, -1e30)
            top = jnp.max(scores, axis=-1, keepdims=True)
            grown = jnp.exp(scores - top)
            p = grown * (1.0 / jnp.sum(grown, axis=-1, keepdims=True))
            pmat[m, pl.ds(4 * parity, count)] = p
            mixed.append(nn(p.reshape(count * CAP, CAP).astype(BF), vb[m, parity]))
        for j in range(4):
            block = mixed[0][j * CAP:(j + 1) * CAP]
            if j < 3:
                block = block + mixed[1][j * CAP:(j + 1) * CAP]
            mix[pl.ds(m * CAP, CAP), j * 128:(j + 1) * 128] = block.astype(BF)
    loads[2].wait()
    for c, w in WIDE:
        e1s[:, c:c + w] = nn(mix[...], wo[:, c:c + w]).astype(BF)
    swap_1.start()
    swap_1.wait()
    mid = stream + (e1s[...].astype(F32) + e1r[...].astype(F32))
    middle[...] = mid.reshape(MICRO, 2, OWN, D)
    inv = lax.rsqrt(jnp.mean(mid * mid, axis=-1, keepdims=True) + EPS)
    n2[...] = (mid * inv * gain_2).astype(BF)
    loads[3].wait()
    for c, w in TILES:
        g = nn(n2[...], wgu[0, :, c:c + w])
        u = nn(n2[...], wgu[1, :, c:c + w])
        sig = jax.nn.sigmoid(g)
        silu = g * sig
        hidden[:, c:c + w] = (silu * u).astype(BF)
        dup[:, c:c + w] = silu.astype(BF)
        dgate[:, c:c + w] = (u * sig * (1.0 + g * (1.0 - sig))).astype(BF)
    loads[4].wait()
    for c, w in WIDE:
        part[:, :, :, c:c + w] = nn(hidden[...], wd[:, c:c + w]).reshape(MICRO, 2, OWN, w)
    e2s[...] = part[:, other].astype(BF)
    swap_2.start()
    swap_2.wait()
    pipe_out[...] = (middle[:, t] + (part[:, t] + e2r[...].astype(F32))).astype(BF)
    rows_ref[0] = pipe_out[...].astype(F32)

    def flips(rows, out):
        turned = nt(perm[...], rows)
        out[0] = turned.astype(BF)
        out[1] = jnp.concatenate(
            [turned[(4 * b + a) * 56:(4 * b + a + 1) * 56] for a in range(4) for b in range(4)], axis=0).astype(BF)
        out[2] = rows.astype(F32).T.astype(BF)

    loads[5].wait()

    @pl.when(pipe == 0)
    def _():
        pass_x.start()
        flips(n2[...], lt_n)
        pass_g.wait_recv()
        share_g.start()

    share_g.wait()
    for m in range(MICRO):
        live = cs[m, 2][:, :1].astype(BF).reshape(2, OWN, 1)
        gbuf[m] = gbuf[m] * live

    def weights_down():
        flips(gbuf[...].reshape(ROWS, D), lt)
        for name, order in (("c0", 2), ("a0", 0), ("b0", 1), ("c1", 2)):
            _, c, w, _ = PIECES[name]
            gdown[:, c:c + w] = nn(lt[order], hidden[:, c:c + w]).astype(BF)
            begin(name)

    def weights_gate_up():
        for name, order in (("a1", 0), ("b1", 1), ("c2", 2), ("a2", 0), ("b2", 1), ("c3", 2)):
            buf, c, w, _ = PIECES[name]
            which, rhs = ((0, dgate), (1, dup))[buf == "up"]
            wgu[which, :, c:c + w] = nn(lt_n[order], rhs[:, c:c + w]).astype(BF)
            begin(name)

    def weights_out():
        lt[0] = nt(perm[...], mb_ref[...]).astype(BF)
        gout[...] = nn(lt[0], mix[...]).astype(BF)
        begin("a3")

    @pl.when(pipe == 0)
    def _():
        weights_down()

    grad = gbuf[...].reshape(ROWS, D)
    for c, w in TILES:
        gh = nt(grad, wd[c:c + w, :])
        dgate[:, c:c + w] = (gh * dgate[:, c:c + w].astype(F32)).astype(BF)
        dup[:, c:c + w] = (gh * dup[:, c:c + w].astype(F32)).astype(BF)
    for c, w in WIDE:
        e1s[:, c:c + w] = (nt(dgate[...], wgu[0, c:c + w, :]) + nt(dup[...], wgu[1, c:c + w, :])).astype(BF)
    swap_3.start()

    @pl.when(pipe == 0)
    def _():
        weights_gate_up()

    swap_3.wait()

    def norm_back(grads, values, gain):
        inverse = lax.rsqrt(jnp.mean(values * values, axis=-1, keepdims=True) + EPS)
        scaled = values * inverse
        weighted = grads * gain
        back = inverse * (weighted - scaled * jnp.mean(weighted * scaled, axis=-1, keepdims=True))
        return back, grads * scaled

    grads = e1s[...].astype(F32) + e1r[...].astype(F32)
    back, terms = norm_back(grads, middle[...].reshape(ROWS, D), gain_2)
    row = lax.broadcasted_iota(jnp.int32, (ROWS, 1), 0)
    mine = ((row >> 6) & 1) == t
    small_in[0, 0] = jnp.zeros((8, D), F32)
    small_in[0, 0, 1:2, :] = jnp.sum(jnp.where(mine, terms, 0.0), axis=0, keepdims=True)
    grad_mid = gbuf[...].reshape(ROWS, D).astype(F32) + back
    gmid[...] = grad_mid.reshape(MICRO, 2, OWN, D)
    mb_ref[...] = grad_mid.astype(BF)

    @pl.when(pipe == 0)
    def _():
        weights_out()

    gmix = nt(mb_ref[...], wo[...]).astype(BF)
    for m in range(MICRO):
        blocks = [gmix[m * CAP:(m + 1) * CAP, j * 128:(j + 1) * 128] for j in range(4)]
        q_even = qb[m].reshape(4 * CAP, 128)
        q_odd = qb[m, :3].reshape(3 * CAP, 128)
        out = []
        for parity, queries, count in ((0, q_even, 4), (1, q_odd, 3)):
            gm = jnp.concatenate(blocks[:count], axis=0)
            p = pmat[m, pl.ds(4 * parity, count)].reshape(count * CAP, CAP)
            gp = nt(gm, vb[m, parity])
            ds = (p * (gp - jnp.sum(p * gp, axis=-1, keepdims=True))).astype(BF)
            out.append((nn(ds, kb[m, parity]), tn(ds, queries), tn(p.astype(BF), gm)))
        keys = pltpu.roll(out[0][1], 64, 1) + out[1][1]
        values = out[0][2] + pltpu.roll(out[1][2], 64, 1)
        rows = pl.ds(m * CAP, CAP)
        for j in range(4):
            block = out[0][0][j * CAP:(j + 1) * CAP]
            if j < 3:
                block = block + out[1][0][j * CAP:(j + 1) * CAP]
            else:
                block = jnp.where(half_lane < 64, block, keys)
            block = block * HEAD ** (-0.5)
            block = block * cs[m, 0] - turn(block, half_lane) * cs[m, 1]
            if j == 3:
                gqkv[rows, 512:640] = pltpu.roll(jnp.where(half_lane < 64, values, block), 64, 1).astype(BF)
                block = jnp.where(half_lane < 64, block, 0.0)
            gqkv[rows, j * 128:(j + 1) * 128] = block.astype(BF)
    for c, w in WIDE:
        part[:, :, :, c:c + w] = (
            nn(gqkv[:, :512], wq[:, c:c + w]) + nt(gqkv[:, 512:], wkv[c:c + w, :])).reshape(MICRO, 2, OWN, w)
    e2s[...] = part[:, other].astype(BF)
    swap_4.start()
    swap_4.wait()
    grads = (part[:, t] + e2r[...].astype(F32)).reshape(MICRO * OWN, D)
    back, terms = norm_back(grads, xbuf[:, t].astype(F32).reshape(MICRO * OWN, D), gain_1)
    total = gmid[:, t] + back.reshape(MICRO, OWN, D)
    rows_ref[1] = total

    @pl.when(pipe == 0)
    def _():
        pass_x.wait_send()

    pipe_out[...] = total.astype(BF)

    @pl.when(pipe == 1)
    def _():
        pass_g.start()

    @pl.when(pipe == 1)
    def _():
        weights_down()
        flips(n2[...], lt_n)
        weights_gate_up()
        weights_out()

    lt[1] = nt(perm[...], n1[...]).astype(BF)
    gqkv_w[...] = nn(lt[1], gqkv[...]).astype(BF)
    begin("a4")
    small_in[0, 0, 0:1, :] = jnp.sum(terms, axis=0, keepdims=True)
    bias = jnp.sum(gqkv[...].astype(F32), axis=0, keepdims=True)
    wide = jnp.concatenate([bias[:, :512], jnp.zeros((1, D - 512), F32)], axis=1)
    small_in[0, 0, 2:3, :] = jnp.where(t == 0, wide, pltpu.roll(wide, QW, 1))
    for c in range(2):
        small_in[0, 0, 3 + c:4 + c, :128] = jnp.where(t == c, bias[:, 512:], 0.0)

    for step, event in enumerate(SERVICE):
        if step % 4 == 0 and step < 28:
            small_step(step // 4)
        serve(*event.split(":"))
    for name in NAMES:
        for stage in range(2):
            for k in range(6):
                ring_copy(name, stage, k).wait_send()
        x_copy(name).wait_send()
    for k in range(6):
        small_copy(k).wait_send()

    @pl.when(pipe == 1)
    def _():
        pass_g.wait_send()


def run_train(lens, x, cot, g1, g2, bq, bkv, wq, wkv, wo, wgu, wd):
    vmem = pl.BlockSpec(memory_space=VMEM)
    hbm = pl.BlockSpec(memory_space=pl.ANY)
    dma = pltpu.SemaphoreType.DMA
    return pl.pallas_call(
        train_kernel,
        out_shape=(
            jax.ShapeDtypeStruct((40, COLS_AB + COLS_C), F32),
            jax.ShapeDtypeStruct((2, MICRO, OWN, D), F32),
        ),
        in_specs=[pl.BlockSpec(memory_space=pltpu.SMEM)] + [vmem] * 7 + [hbm] * 6,
        out_specs=(vmem,) * 2,
        scratch_shapes=[
            VMEM((512, D), BF), VMEM((D, 128), BF), VMEM((512, D), BF), VMEM((2, D, FH), BF), VMEM((FH, D), BF), VMEM((D, D), BF),
            VMEM((MICRO, 2, OWN, D), BF), VMEM((MICRO, 2, OWN, D), BF),
            VMEM((ROWS, D), BF), VMEM((ROWS, D), BF),
            VMEM((MICRO, OWN, D), BF), VMEM((MICRO, OWN, D), BF), VMEM((MICRO, OWN, D), BF),
            VMEM((ROWS, D), BF), VMEM((ROWS, D), BF),
            VMEM((MICRO, 4, CAP, 128), BF), VMEM((MICRO, 2, CAP, 128), BF), VMEM((MICRO, 2, CAP, 128), BF),
            VMEM((MICRO, 7, CAP, CAP), F32), VMEM((ROWS, 512), BF), VMEM((MICRO, 2, OWN, D), F32),
            VMEM((ROWS, FH), BF), VMEM((ROWS, FH), BF), VMEM((ROWS, FH), BF),
            VMEM((3, D, ROWS), BF), VMEM((MICRO, 2, OWN, D), F32), VMEM((MICRO, 2, OWN, D), F32),
            VMEM((MICRO, 3, CAP, 128), F32), VMEM((MICRO, CAP, CAP), F32), VMEM((ROWS, 640), BF),
            VMEM((3, D, ROWS), BF), VMEM((ROWS, D), BF), VMEM((D, FH), BF), VMEM((D, 512), BF), VMEM((D, 640), BF),
            VMEM((2, 112, COLS_AB), BF), VMEM((2, 2, 112, COLS_AB), BF),
            VMEM((4, 64, COLS_AB), BF), VMEM((2, 32, COLS_AB), BF), VMEM((2, 2, 32, COLS_AB), BF),
            VMEM((32, COLS_AB), BF), VMEM((32, COLS_AB), BF),
            VMEM((448, COLS_C), BF), VMEM((112, COLS_C), BF), VMEM((2, 112, COLS_C), BF),
            VMEM((4, 32, COLS_C), BF), VMEM((32, COLS_C), BF), VMEM((2, 32, COLS_C), BF),
            VMEM((2, 6, 8, D), F32),
            dma((6,)), dma((8,)), dma((8,)), dma((len(NAMES), 13)), dma((len(NAMES), 13)), dma((6,)), dma((6,)),
        ],
        compiler_params=pltpu.CompilerParams(collective_id=0, has_side_effects=True, vmem_limit_bytes=63 * MIB),
        name="train",
    )(lens, x, cot, g1, g2, bq, bkv, jnp.asarray(rope_table()), wq, wkv, wo, wgu, wd, jnp.asarray(row_order()))


def place_kernel(
    sums_ref, rows_ref,
    so_ref, ig_ref, gain1_ref, gq_ref, bq_ref, gkv_ref, bkv_ref, go_ref, gain2_ref, ggu_ref, gd_ref,
):
    so_ref[...] = rows_ref[0].astype(BF)
    ig_ref[...] = rows_ref[1]
    gain1_ref[...] = sums_ref[32:33, :D]
    gain2_ref[...] = sums_ref[33:34, :D]
    bq_ref[...] = sums_ref[34:35, :D]
    bkv_ref[...] = sums_ref[35:37, :128]
    gq_ref[:, 0, :] = sums_ref[:28, 3200:3200 + QW]
    gkv_ref[:, 0, :] = sums_ref[:28, 3712:3840]
    go_ref[:, 0, :] = sums_ref[:28, 2688:2688 + QW]
    for ref, names in ((gd_ref.at[:, 0], "a0 b0 c0 c1"), (ggu_ref.at[:, 0], "a1 a2 c2"), (ggu_ref.at[:, 1], "b1 b2 c3")):
        for name in names.split():
            _, c, w, at = PIECES[name]
            at = at + COLS_AB * (name[0] == "c")
            ref[:, c:c + w] = sums_ref[:28, at:at + w]


def run_place(*arrays):
    vmem = pl.BlockSpec(memory_space=VMEM)
    shapes = (
        (MICRO, OWN, D), (MICRO, OWN, D), (1, D), (28, 1, QW), (1, D), (28, 1, 128), (2, 128),
        (28, 1, QW), (1, D), (28, 2, FH), (28, 1, FH),
    )
    return pl.pallas_call(
        place_kernel,
        out_shape=tuple(jax.ShapeDtypeStruct(s, F32 if i else BF) for i, s in enumerate(shapes)),
        in_specs=[vmem] * 2,
        out_specs=(vmem,) * 11,
        compiler_params=pltpu.CompilerParams(vmem_limit_bytes=32 * MIB),
        name="place",
    )(*arrays)


def body(
    inputs, cotangent, lengths, gain_attn, w_query, b_query, w_keyval, b_keyval, w_out, gain_mlp, w_gate_up, w_down,
):
    outs = run_train(
        lengths[:, 0], inputs, cotangent, gain_attn, gain_mlp, b_query, b_keyval[0],
        jnp.swapaxes(w_query[0], 0, 1), w_keyval[0, :, 0], w_out[0],
        jnp.swapaxes(w_gate_up[0], 0, 1), w_down[0],
    )
    so, ig, gain1, gq, bq, gkv, bkv, go, gain2, ggu, gd = run_place(*outs)
    return (
        so[None], ig[None], gain1, jnp.swapaxes(gq, 0, 1), bq, gkv[None], bkv[None],
        jnp.transpose(go, (1, 2, 0)), gain2, ggu[None], jnp.transpose(gd, (1, 2, 0)),
    )


def solution(mesh):
    placed = (
        P(None, ("dp", "tensor"), None),
        P(None, ("dp", "tensor"), None),
        P(None, "dp", None),
        P("pipe", None),
        P("pipe", None, "tensor"),
        P("pipe", "tensor"),
        P("pipe", None, "tensor", None),
        P("pipe", "tensor", None),
        P("pipe", "tensor", None),
        P("pipe", None),
        P("pipe", None, None, "tensor"),
        P("pipe", "tensor", None),
    )
    return jax.shard_map(
        body,
        mesh=mesh,
        in_specs=placed,
        out_specs=(
            P("pipe", None, ("dp", "tensor"), None),
            P("pipe", None, ("dp", "tensor"), None),
            P("pipe", None),
            P("pipe", "dp", "tensor"),
            P("pipe", None),
            P("pipe", "dp", "tensor", None),
            P("pipe", None, None),
            P("pipe", "tensor", "dp"),
            P("pipe", None),
            P("pipe", "dp", None, "tensor"),
            P("pipe", "tensor", "dp"),
        ),
        check_vma=False,
    )
```

```python
import functools

import jax
import jax.numpy as jnp
import numpy as np
from jax import lax
from jax.experimental import pallas as pl
from jax.experimental.pallas import tpu as pltpu
from jax.sharding import PartitionSpec as P

D = 896
HEADS = 14
HEAD = 64
CAP = 128
SEQS = 4
MICRO = 2
ROWS = MICRO * CAP
OWN = CAP // 2
FH = 2432
QW = 448
EPS = 1e-06
THETA = 1000000.0
MIB = 1024 * 1024

BF = jnp.bfloat16
F32 = jnp.float32
MESH = pl.DeviceIdType.MESH
VMEM = pltpu.VMEM

PIECES = {
    "a0": ("down", 0, 640, 0), "a1": ("gate", 0, 896, 640), "a2": ("gate", 896, 1152, 1536),
    "a3": ("out", 0, 512, 2688), "a4": ("qkv", 0, 640, 3200),
    "b0": ("down", 640, 640, 3840), "b1": ("up", 0, 896, 4480), "b2": ("up", 896, 1280, 5376),
    "c0": ("down", 1280, 512, 0), "c1": ("down", 1792, 640, 512), "c2": ("gate", 2048, 384, 1152), "c3": ("up", 2176, 256, 1536),
}
NAMES = tuple(PIECES)
COLS_AB = 6656
COLS_C = 1792
SPLIT = {"c0": 256, "c1": 256, "c2": 256, "c3": 128}
SERVICE = (
    "cx:c0 m0:a0 m0:a1 m0:b0",
    "m0:b1 m0:a2 m0:b2 m0:a3",
    "m0:c0 cx:c1 s:b0 m0:a4",
    "s:b1 cx:c2 s:a0 s:b2",
    "s:a1 s:c0 cx:c3 m0:c1",
    "m0:c2 s:a2 m1:a0 s:a3",
    "m1:a1 m1:b0 m0:c3 s:c1",
    "s:a4 s:c2 m1:b1 m1:a2",
    "m1:b2 t:a0 m1:a3 m1:c0",
    "t:a1 t:b0 e:a0 s:c3",
    "m1:c1 m1:a4 m1:c2 t:b1",
    "e:a1 t:a2 t:a3 e:b0",
    "t:b2 t:c0 m1:c3 t:a4",
    "t:c1 t:c2 e:b1 t:c3",
    "e:a2 e:a3 e:b2 e:a4",
)
SERVICE = tuple(event for line in SERVICE for event in line.split())
TILES = ((0, 512), (512, 512), (1024, 512), (1536, 512), (2048, 384))
WIDE = ((0, 256), (256, 256), (512, 256), (768, 128))


def nn(a, b):
    return lax.dot_general(a, b, (((1,), (0,)), ((), ())), preferred_element_type=F32)


def nt(a, b):
    return lax.dot_general(a, b, (((1,), (1,)), ((), ())), preferred_element_type=F32)


def tn(a, b):
    return lax.dot_general(a, b, (((0,), (0,)), ((), ())), preferred_element_type=F32)


def rope_table():
    half = HEAD // 2
    frequency = np.power(np.float32(THETA), -(np.arange(half, dtype=np.float32) * np.float32(2.0 / HEAD)))
    phases = (np.arange(CAP, dtype=np.float32)[:, None] * frequency[None, :].astype(np.float32)).astype(np.float32)
    phases = phases.astype(np.float64)
    cosine = np.concatenate([np.cos(phases)] * 4, axis=1).astype(np.float32)
    sine = np.concatenate([-np.sin(phases), np.sin(phases)] * 2, axis=1).astype(np.float32)
    parts = []
    for table in (cosine, sine):
        rest = table
        for _ in range(3):
            piece = rest.astype(jnp.bfloat16)
            parts.append(piece)
            rest = rest - piece.astype(np.float32)
    return np.concatenate(parts, axis=1)


def row_order():
    index = np.arange(D)
    y, z, x_hi, k = index // 224, index // 56 % 4, index // 28 % 2, index % 28
    source = (x_hi * 16 + z * 4 + y) * 28 + k
    return (source[:, None] == np.arange(D)[None, :]).astype(jnp.bfloat16)


def turn(block, lane):
    low = (lane & 63) < 32
    return jnp.where(low, pltpu.roll(block, 96, 1), pltpu.roll(block, 32, 1))


def train_kernel(
    len_ref, x_ref, cot_ref, g1_ref, g2_ref, bq_ref, bkv_ref, tab_ref,
    wq_hbm, wkv_hbm, wo_hbm, wgu_hbm, wd_hbm, perm_hbm,
    sums_ref, rows_ref,
    wq, wkv, wo, wgu, wd, perm, xbuf, gbuf, e1s, e1r, e2s, e2r, pipe_out,
    n1, n2, qb, kb, vb, pmat, mix, middle, dgate, dup, hidden, lt, part, gmid, cs, allow, gqkv,
    lt_n, mb_ref, gdown, gout, gqkv_w,
    r1, r2, h2, q1, q2, h3, q3, cx, c1, c2, hc, d1, d2, small_in,
    load_sem, send_sem, recv_sem, sum_send, sum_recv, small_send, small_recv,
):
    pipe = lax.axis_index("pipe")
    t = lax.axis_index("tensor")
    rank = lax.axis_index("dp")
    other = 1 - t
    x_hi, z, y = rank // 16, (rank // 4) % 4, rank % 4
    pos = (y, z)

    loads = [
        pltpu.make_async_copy(wq_hbm, wq.at[pl.ds(0, QW)], load_sem.at[0]),
        pltpu.make_async_copy(wkv_hbm, wkv, load_sem.at[1]),
        pltpu.make_async_copy(wo_hbm, wo.at[pl.ds(0, QW)], load_sem.at[2]),
        pltpu.make_async_copy(wgu_hbm, wgu, load_sem.at[3]),
        pltpu.make_async_copy(wd_hbm, wd, load_sem.at[4]),
        pltpu.make_async_copy(perm_hbm, perm, load_sem.at[5]),
    ]
    for c in loads:
        c.start()

    def to_core(src, dst, i):
        return pltpu.make_async_remote_copy(
            src_ref=src, dst_ref=dst, send_sem=send_sem.at[i], recv_sem=recv_sem.at[i],
            device_id={"tensor": other}, device_id_type=MESH)

    def to_pipe(src, dst, i):
        return pltpu.make_async_remote_copy(
            src_ref=src, dst_ref=dst, send_sem=send_sem.at[i], recv_sem=recv_sem.at[i],
            device_id={"pipe": 1 - pipe}, device_id_type=MESH)

    share_x = to_core(xbuf.at[:, t], xbuf.at[:, t], 0)
    share_g = to_core(gbuf.at[:, t], gbuf.at[:, t], 1)
    pass_x = to_pipe(pipe_out, xbuf.at[:, t], 2)
    pass_g = to_pipe(pipe_out, gbuf.at[:, t], 3)
    swap_1 = to_core(e1s, e1r, 4)
    swap_2 = to_core(e2s, e2r, 5)
    swap_3 = to_core(e1s, e1r, 6)
    swap_4 = to_core(e2s, e2r, 7)

    def at(yy, zz, xx):
        return {"dp": xx * 16 + zz * 4 + yy}

    def along(axis, step):
        if axis == 0:
            return at((y + step) % 4, z, x_hi)
        return at(y, (z + step) % 4, x_hi)

    x_peer = at(y, z, 1 - x_hi)
    peers = [along(0, 1), along(0, 3), along(1, 1), along(1, 3), x_peer, {"tensor": other}, {"pipe": 1 - pipe}]
    barrier = pltpu.get_barrier_semaphore()
    for peer in peers:
        pl.semaphore_signal(barrier, inc=1, device_id=peer, device_id_type=MESH)
    pl.semaphore_wait(barrier, len(peers))

    def remote(src, dst, peer, *sem):
        return pltpu.make_async_remote_copy(
            src_ref=src, dst_ref=dst, send_sem=sum_send.at[sem], recv_sem=sum_recv.at[sem],
            device_id=peer, device_id_type=MESH)

    bufs = {"down": gdown, "gate": wgu.at[0], "up": wgu.at[1], "out": gout, "qkv": gqkv_w}

    def columns(name, half=None):
        _, _, w, c = PIECES[name]
        if half is None:
            return pl.ds(c, w)
        cutoff = SPLIT[name]
        return pl.ds(c, cutoff) if half == 0 else pl.ds(c + cutoff, w - cutoff)

    def held(name, start, count):
        buf, c, w, _ = PIECES[name]
        return bufs[buf].at[pl.ds(pl.multiple_of(start, 16), count), pl.ds(c, w)]

    def ring(name, stage):
        if name[0] == "c":
            here = lambda half: columns(name, half)
            if stage == 0:
                return (1, lambda q, half: cx.at[pl.ds(pl.multiple_of(q * 112, 16), 112), here(half)],
                        lambda half: c1.at[:, here(half)], lambda k, half: c2.at[k, :, here(half)])
            return (0, lambda q, half: hc.at[q, :, here(half)],
                    lambda half: d1.at[:, here(half)], lambda k, half: d2.at[k, :, here(half)])
        axis = "ab".index(name[0])
        cols = columns(name)
        if stage == 0:
            return (axis, lambda q, half: held(name, q * 224 + 112 * half, 112),
                    lambda half: r1.at[half, :, cols], lambda k, half: r2.at[k, half, :, cols])
        return (1 - axis, lambda q, half: h2.at[q, pl.ds(32 * half, 32), cols],
                lambda half: q1.at[half, :, cols], lambda k, half: q2.at[k, half, :, cols])

    def ring_copy(name, stage, k):
        axis, block, first, last = ring(name, stage)
        f = pos[axis]
        ahead, behind = along(axis, 1), along(axis, 3)
        src, dst, peer = (
            lambda: (block((f + 2) % 4, 0), first(0), ahead),
            lambda: (block((f + 2) % 4, 1), first(1), behind),
            lambda: (block((f + 1) % 4, 1), last(0, 1), ahead),
            lambda: (block((f + 3) % 4, 0), last(1, 0), behind),
            lambda: (first(0), last(0, 0), ahead),
            lambda: (first(1), last(1, 1), behind),
        )[k]()
        return remote(src, dst, peer, NAMES.index(name), 6 * stage + k)

    def ring_begin(name, stage):
        for k in range(4):
            ring_copy(name, stage, k).start()

    def ring_middle(name, stage):
        axis, block, first, _ = ring(name, stage)
        f = pos[axis]
        for k, q in enumerate(((f + 1) % 4, (f + 3) % 4)):
            ring_copy(name, stage, k).wait_recv()
            own = block(q, k)[...]
            slot = first(k)
            slot[...] = (own.astype(F32) + slot[...].astype(F32)).astype(BF)
            ring_copy(name, stage, 4 + k).start()

    def ring_total(name, stage):
        axis, block, _, last = ring(name, stage)
        for k in range(2, 6):
            ring_copy(name, stage, k).wait_recv()
        return [
            block(pos[axis], half)[...].astype(F32) + last(0, half)[...].astype(F32) + last(1, half)[...].astype(F32)
            for half in range(2)]

    def x_copy(name):
        if name[0] == "c":
            return remote(held(name, (1 - x_hi) * 448, 448), cx.at[:, columns(name)], x_peer, NAMES.index(name), 12)
        cols = columns(name)
        return remote(h3.at[:, cols], q3.at[:, cols], x_peer, NAMES.index(name), 12)

    def begin(name):
        if name[0] == "c":
            x_copy(name).start()
        else:
            ring_begin(name, 0)

    def serve(event, name):
        cols = columns(name)
        if event == "cx":
            x_copy(name).wait_recv()
            own = held(name, x_hi * 448, 448)[...]
            cx[:, cols] = (own.astype(F32) + cx[:, cols].astype(F32)).astype(BF)
            ring_begin(name, 0)
        elif event == "m0":
            ring_middle(name, 0)
        elif event == "s":
            sums = ring_total(name, 0)
            for k in range(4):
                if name[0] == "c":
                    for half in range(2):
                        block = sums[half][28 * k:28 * k + 28]
                        zeros = jnp.zeros((4, block.shape[1]), F32)
                        hc[k, :, columns(name, half)] = jnp.concatenate([block, zeros], axis=0).astype(BF)
                else:
                    block = sums[k // 2][(k % 2) * 56:(k % 2 + 1) * 56]
                    zeros = jnp.zeros((8, block.shape[1]), F32)
                    h2[k, :, cols] = jnp.concatenate([block, zeros], axis=0).astype(BF)
            ring_begin(name, 1)
        elif event == "m1":
            ring_middle(name, 1)
        elif event == "t":
            sums = ring_total(name, 1)
            if name[0] == "c":
                for half in range(2):
                    at = columns(name, half)
                    sums_ref[:28, pl.ds(COLS_AB + at.start, at.size)] = sums[half][:28]
            else:
                whole = jnp.concatenate(sums, axis=0)
                first, last = whole[:32], whole[28:60]
                upper = x_hi == 1
                h3[:, cols] = jnp.where(upper, first, last).astype(BF)
                sums_ref[:28, cols] = jnp.where(upper, last, first)[:28]
                x_copy(name).start()
        else:
            x_copy(name).wait_recv()
            sums_ref[:28, cols] = sums_ref[:28, cols] + q3[:, cols].astype(F32)[:28]

    small_peers = [
        along(0, 1 + 2 * (y % 2)), along(0, 3 - 2 * (y % 2)),
        along(1, 1 + 2 * (z % 2)), along(1, 3 - 2 * (z % 2)), x_peer, {"tensor": other},
    ]

    def small_copy(k):
        return pltpu.make_async_remote_copy(
            src_ref=small_in.at[0, k], dst_ref=small_in.at[1, k], send_sem=small_send.at[k], recv_sem=small_recv.at[k],
            device_id=small_peers[k], device_id_type=MESH)

    def small_step(k):
        if k > 0:
            small_copy(k - 1).wait_recv()
            total = small_in[0, k - 1] + small_in[1, k - 1]
            if k < 6:
                small_in[0, k] = total
            else:
                sums_ref[32:40, :D] = total
        if k < 6:
            small_copy(k).start()

    @pl.when(pipe == 0)
    def _():
        xbuf[:, t] = x_ref[...]

    @pl.when(pipe == 1)
    def _():
        gbuf[:, t] = cot_ref[...]
        share_g.start()

    wq[pl.ds(QW, 64), :] = jnp.zeros((64, D), BF)
    wo[pl.ds(QW, 64), :] = jnp.zeros((64, D), BF)
    slot = lax.broadcasted_iota(jnp.int32, (CAP, CAP), 0)
    lane = lax.broadcasted_iota(jnp.int32, (CAP, CAP), 1)
    for m in range(MICRO):
        end = 0
        seg_row = jnp.zeros((CAP, CAP), jnp.int32)
        seg_col = jnp.zeros((CAP, CAP), jnp.int32)
        start = jnp.zeros((CAP, CAP), jnp.int32)
        for s in range(SEQS):
            end = end + len_ref[m, s]
            passed = slot >= end
            seg_row = seg_row + passed.astype(jnp.int32)
            seg_col = seg_col + (lane >= end).astype(jnp.int32)
            start = jnp.where(passed, end, start)
        allow[m] = jnp.where((seg_row == seg_col) & (lane <= slot), 1.0, 0.0)
        cs[m, 2] = jnp.where((seg_row < SEQS) | (pipe == 0), 1.0, 0.0)
        one_hot = jnp.where(slot - start == lane, 1.0, 0.0).astype(BF)
        table = nn(one_hot, tab_ref[...])
        cs[m, 0] = table[:, :128] + table[:, 128:256] + table[:, 256:384]
        cs[m, 1] = table[:, 384:512] + table[:, 512:640] + table[:, 640:768]
    bias_q = jnp.concatenate([bq_ref[...].astype(F32), jnp.zeros((1, 64), F32)], axis=1)
    bias_kv = bkv_ref[...].astype(F32)
    gain_1 = g1_ref[...].astype(F32)
    gain_2 = g2_ref[...].astype(F32)

    @pl.when(pipe == 1)
    def _():
        pass_x.wait_recv()

    share_x.start()
    share_x.wait()
    stream = xbuf[...].astype(F32).reshape(ROWS, D)
    inv = lax.rsqrt(jnp.mean(stream * stream, axis=-1, keepdims=True) + EPS)
    n1[...] = (stream * inv * gain_1).astype(BF)
    loads[0].wait()
    loads[1].wait()
    half_lane = lax.broadcasted_iota(jnp.int32, (CAP, 128), 1)
    for m in range(MICRO):
        rows = pl.ds(m * CAP, CAP)
        qs = nt(n1[rows, :], wq[...]) + bias_q
        vk = pltpu.roll(nn(n1[rows, :], wkv[...]) + bias_kv, 64, 1)
        for j in range(4):
            block = qs[:, j * 128:(j + 1) * 128]
            if j == 3:
                block = jnp.where(half_lane < 64, block, vk)
            block = block * cs[m, 0] + turn(block, half_lane) * cs[m, 1]
            qb[m, j] = block.astype(BF)
            if j == 3:
                odd = jnp.where(half_lane >= 64, block, 0.0)
                kb[m, 1] = odd.astype(BF)
                kb[m, 0] = pltpu.roll(odd, 64, 1).astype(BF)
        even = jnp.where(half_lane < 64, vk, 0.0)
        vb[m, 0] = even.astype(BF)
        vb[m, 1] = pltpu.roll(even, 64, 1).astype(BF)
    for m in range(MICRO):
        q_even = qb[m].reshape(4 * CAP, 128)
        q_odd = qb[m, :3].reshape(3 * CAP, 128)
        seen = allow[m] > 0.0
        mixed = []
        for parity, queries, count in ((0, q_even, 4), (1, q_odd, 3)):
            scores = nt(queries, kb[m, parity]).reshape(count, CAP, CAP) * HEAD ** (-0.5)
            scores = jnp.where(seen[None], scores, -1e30)
            top = jnp.max(scores, axis=-1, keepdims=True)
            grown = jnp.exp(scores - top)
            p = grown * (1.0 / jnp.sum(grown, axis=-1, keepdims=True))
            pmat[m, pl.ds(4 * parity, count)] = p
            mixed.append(nn(p.reshape(count * CAP, CAP).astype(BF), vb[m, parity]))
        for j in range(4):
            block = mixed[0][j * CAP:(j + 1) * CAP]
            if j < 3:
                block = block + mixed[1][j * CAP:(j + 1) * CAP]
            mix[pl.ds(m * CAP, CAP), j * 128:(j + 1) * 128] = block.astype(BF)
    loads[2].wait()
    for c, w in WIDE:
        e1s[:, c:c + w] = nn(mix[...], wo[:, c:c + w]).astype(BF)
    swap_1.start()
    swap_1.wait()
    mid = stream + (e1s[...].astype(F32) + e1r[...].astype(F32))
    middle[...] = mid.reshape(MICRO, 2, OWN, D)
    inv = lax.rsqrt(jnp.mean(mid * mid, axis=-1, keepdims=True) + EPS)
    n2[...] = (mid * inv * gain_2).astype(BF)
    loads[3].wait()
    for c, w in TILES:
        g = nn(n2[...], wgu[0, :, c:c + w])
        u = nn(n2[...], wgu[1, :, c:c + w])
        sig = jax.nn.sigmoid(g)
        silu = g * sig
        hidden[:, c:c + w] = (silu * u).astype(BF)
        dup[:, c:c + w] = silu.astype(BF)
        dgate[:, c:c + w] = (u * sig * (1.0 + g * (1.0 - sig))).astype(BF)
    loads[4].wait()
    for c, w in WIDE:
        part[:, :, :, c:c + w] = nn(hidden[...], wd[:, c:c + w]).reshape(MICRO, 2, OWN, w)
    e2s[...] = part[:, other].astype(BF)
    swap_2.start()
    swap_2.wait()
    pipe_out[...] = (middle[:, t] + (part[:, t] + e2r[...].astype(F32))).astype(BF)
    rows_ref[0] = pipe_out[...].astype(F32)

    def reordered(turned):
        return jnp.concatenate(
            [turned[(4 * b + a) * 56:(4 * b + a + 1) * 56] for a in range(4) for b in range(4)], axis=0).astype(BF)

    def weights_down():
        rows = gbuf[...].reshape(ROWS, D)
        turned = nt(perm[...], rows)
        for name, order in (("a0", 0), ("b0", 1), ("c0", 2), ("c1", 2)):
            if name != "c1":
                lt[order] = (
                    turned.astype(BF) if order == 0 else reordered(turned) if order == 1 else rows.astype(F32).T.astype(BF))
            _, c, w, _ = PIECES[name]
            gdown[:, c:c + w] = nn(lt[order], hidden[:, c:c + w]).astype(BF)
            begin(name)

    def weights_gate_up():
        for name, order in (("a1", 0), ("b1", 1), ("c2", 2), ("a2", 0), ("b2", 1), ("c3", 2)):
            buf, c, w, _ = PIECES[name]
            which, rhs = ((0, dgate), (1, dup))[buf == "up"]
            wgu[which, :, c:c + w] = nn(lt_n[order], rhs[:, c:c + w]).astype(BF)
            begin(name)

    def weights_out():
        lt[0] = nt(perm[...], mb_ref[...]).astype(BF)
        gout[...] = nn(lt[0], mix[...]).astype(BF)
        begin("a3")

    def norm_back(grads, values, gain):
        inverse = lax.rsqrt(jnp.mean(values * values, axis=-1, keepdims=True) + EPS)
        scaled = values * inverse
        weighted = grads * gain
        back = inverse * (weighted - scaled * jnp.mean(weighted * scaled, axis=-1, keepdims=True))
        return back, grads * scaled

    loads[5].wait()

    def backward(turn_now, _):
        chain = pl.when(turn_now == 0)
        weights = pl.when(turn_now == pipe)

        @chain
        def _():
            @pl.when(pipe == 0)
            def _():
                pass_x.start()

        @weights
        def _():
            turned = nt(perm[...], n2[...])
            lt_n[0] = turned.astype(BF)
            lt_n[1] = reordered(turned)
            lt_n[2] = n2[...].astype(F32).T.astype(BF)

        @chain
        def _():
            @pl.when(pipe == 0)
            def _():
                pass_g.wait_recv()
                share_g.start()

            share_g.wait()
            for m in range(MICRO):
                live = cs[m, 2][:, :1].astype(BF).reshape(2, OWN, 1)
                gbuf[m] = gbuf[m] * live

        weights(weights_down)

        @chain
        def _():
            grad = gbuf[...].reshape(ROWS, D)
            for c, w in TILES:
                gh = nt(grad, wd[c:c + w, :])
                dgate[:, c:c + w] = (gh * dgate[:, c:c + w].astype(F32)).astype(BF)
                dup[:, c:c + w] = (gh * dup[:, c:c + w].astype(F32)).astype(BF)
            for c, w in WIDE:
                e1s[:, c:c + w] = (nt(dgate[...], wgu[0, c:c + w, :]) + nt(dup[...], wgu[1, c:c + w, :])).astype(BF)
            swap_3.start()

        weights(weights_gate_up)

        @chain
        def _():
            swap_3.wait()
            grads = e1s[...].astype(F32) + e1r[...].astype(F32)
            back, terms = norm_back(grads, middle[...].reshape(ROWS, D), gain_2)
            row = lax.broadcasted_iota(jnp.int32, (ROWS, 1), 0)
            mine = ((row >> 6) & 1) == t
            small_in[0, 0] = jnp.zeros((8, D), F32)
            small_in[0, 0, 1:2, :] = jnp.sum(jnp.where(mine, terms, 0.0), axis=0, keepdims=True)
            grad_mid = gbuf[...].reshape(ROWS, D).astype(F32) + back
            gmid[...] = grad_mid.reshape(MICRO, 2, OWN, D)
            mb_ref[...] = grad_mid.astype(BF)

        weights(weights_out)
        chain(attention_back)
        return 0

    def attention_back():
        gmix = nt(mb_ref[...], wo[...]).astype(BF)
        for m in range(MICRO):
            blocks = [gmix[m * CAP:(m + 1) * CAP, j * 128:(j + 1) * 128] for j in range(4)]
            q_even = qb[m].reshape(4 * CAP, 128)
            q_odd = qb[m, :3].reshape(3 * CAP, 128)
            out = []
            for parity, queries, count in ((0, q_even, 4), (1, q_odd, 3)):
                gm = jnp.concatenate(blocks[:count], axis=0)
                p = pmat[m, pl.ds(4 * parity, count)].reshape(count * CAP, CAP)
                gp = nt(gm, vb[m, parity])
                ds = (p * (gp - jnp.sum(p * gp, axis=-1, keepdims=True))).astype(BF)
                out.append((nn(ds, kb[m, parity]), tn(ds, queries), tn(p.astype(BF), gm)))
            keys = pltpu.roll(out[0][1], 64, 1) + out[1][1]
            values = out[0][2] + pltpu.roll(out[1][2], 64, 1)
            rows = pl.ds(m * CAP, CAP)
            for j in range(4):
                block = out[0][0][j * CAP:(j + 1) * CAP]
                if j < 3:
                    block = block + out[1][0][j * CAP:(j + 1) * CAP]
                else:
                    block = jnp.where(half_lane < 64, block, keys)
                block = block * HEAD ** (-0.5)
                block = block * cs[m, 0] - turn(block, half_lane) * cs[m, 1]
                if j == 3:
                    gqkv[rows, 512:640] = pltpu.roll(jnp.where(half_lane < 64, values, block), 64, 1).astype(BF)
                    block = jnp.where(half_lane < 64, block, 0.0)
                gqkv[rows, j * 128:(j + 1) * 128] = block.astype(BF)
        for c, w in WIDE:
            part[:, :, :, c:c + w] = (
                nn(gqkv[:, :512], wq[:, c:c + w]) + nt(gqkv[:, 512:], wkv[c:c + w, :])).reshape(MICRO, 2, OWN, w)
        e2s[...] = part[:, other].astype(BF)
        swap_4.start()
        swap_4.wait()
        grads = (part[:, t] + e2r[...].astype(F32)).reshape(MICRO * OWN, D)
        back, terms = norm_back(grads, xbuf[:, t].astype(F32).reshape(MICRO * OWN, D), gain_1)
        total = gmid[:, t] + back.reshape(MICRO, OWN, D)
        rows_ref[1] = total

        @pl.when(pipe == 0)
        def _():
            pass_x.wait_send()

        pipe_out[...] = total.astype(BF)

        @pl.when(pipe == 1)
        def _():
            pass_g.start()

        small_in[0, 0, 0:1, :] = jnp.sum(terms, axis=0, keepdims=True)
        bias = jnp.sum(gqkv[...].astype(F32), axis=0, keepdims=True)
        wide = jnp.concatenate([bias[:, :512], jnp.zeros((1, D - 512), F32)], axis=1)
        small_in[0, 0, 2:3, :] = jnp.where(t == 0, wide, pltpu.roll(wide, QW, 1))
        for c in range(2):
            small_in[0, 0, 3 + c:4 + c, :128] = jnp.where(t == c, bias[:, 512:], 0.0)

    lax.fori_loop(0, 2, backward, 0)
    lt[1] = nt(perm[...], n1[...]).astype(BF)
    gqkv_w[...] = nn(lt[1], gqkv[...]).astype(BF)
    begin("a4")

    for step, event in enumerate(SERVICE):
        if step % 4 == 0 and step < 28:
            small_step(step // 4)
        serve(*event.split(":"))
    for name in NAMES:
        for stage in range(2):
            for k in range(6):
                ring_copy(name, stage, k).wait_send()
        x_copy(name).wait_send()
    for k in range(6):
        small_copy(k).wait_send()

    @pl.when(pipe == 1)
    def _():
        pass_g.wait_send()


def run_train(lens, x, cot, g1, g2, bq, bkv, wq, wkv, wo, wgu, wd):
    vmem = pl.BlockSpec(memory_space=VMEM)
    hbm = pl.BlockSpec(memory_space=pl.ANY)
    dma = pltpu.SemaphoreType.DMA
    return pl.pallas_call(
        train_kernel,
        out_shape=(
            jax.ShapeDtypeStruct((40, COLS_AB + COLS_C), F32),
            jax.ShapeDtypeStruct((2, MICRO, OWN, D), F32),
        ),
        in_specs=[pl.BlockSpec(memory_space=pltpu.SMEM)] + [vmem] * 7 + [hbm] * 6,
        out_specs=(vmem,) * 2,
        scratch_shapes=[
            VMEM((512, D), BF), VMEM((D, 128), BF), VMEM((512, D), BF), VMEM((2, D, FH), BF), VMEM((FH, D), BF), VMEM((D, D), BF),
            VMEM((MICRO, 2, OWN, D), BF), VMEM((MICRO, 2, OWN, D), BF),
            VMEM((ROWS, D), BF), VMEM((ROWS, D), BF),
            VMEM((MICRO, OWN, D), BF), VMEM((MICRO, OWN, D), BF), VMEM((MICRO, OWN, D), BF),
            VMEM((ROWS, D), BF), VMEM((ROWS, D), BF),
            VMEM((MICRO, 4, CAP, 128), BF), VMEM((MICRO, 2, CAP, 128), BF), VMEM((MICRO, 2, CAP, 128), BF),
            VMEM((MICRO, 7, CAP, CAP), F32), VMEM((ROWS, 512), BF), VMEM((MICRO, 2, OWN, D), F32),
            VMEM((ROWS, FH), BF), VMEM((ROWS, FH), BF), VMEM((ROWS, FH), BF),
            VMEM((3, D, ROWS), BF), VMEM((MICRO, 2, OWN, D), F32), VMEM((MICRO, 2, OWN, D), F32),
            VMEM((MICRO, 3, CAP, 128), F32), VMEM((MICRO, CAP, CAP), F32), VMEM((ROWS, 640), BF),
            VMEM((3, D, ROWS), BF), VMEM((ROWS, D), BF), VMEM((D, FH), BF), VMEM((D, 512), BF), VMEM((D, 640), BF),
            VMEM((2, 112, COLS_AB), BF), VMEM((2, 2, 112, COLS_AB), BF),
            VMEM((4, 64, COLS_AB), BF), VMEM((2, 32, COLS_AB), BF), VMEM((2, 2, 32, COLS_AB), BF),
            VMEM((32, COLS_AB), BF), VMEM((32, COLS_AB), BF),
            VMEM((448, COLS_C), BF), VMEM((112, COLS_C), BF), VMEM((2, 112, COLS_C), BF),
            VMEM((4, 32, COLS_C), BF), VMEM((32, COLS_C), BF), VMEM((2, 32, COLS_C), BF),
            VMEM((2, 6, 8, D), F32),
            dma((6,)), dma((8,)), dma((8,)), dma((len(NAMES), 13)), dma((len(NAMES), 13)), dma((6,)), dma((6,)),
        ],
        compiler_params=pltpu.CompilerParams(collective_id=0, has_side_effects=True, vmem_limit_bytes=63 * MIB),
        name="train",
    )(lens, x, cot, g1, g2, bq, bkv, jnp.asarray(rope_table()), wq, wkv, wo, wgu, wd, jnp.asarray(row_order()))


def place_kernel(
    sums_ref, rows_ref,
    so_ref, ig_ref, gain1_ref, gq_ref, bq_ref, gkv_ref, bkv_ref, go_ref, gain2_ref, ggu_ref, gd_ref,
):
    so_ref[...] = rows_ref[0].astype(BF)
    ig_ref[...] = rows_ref[1]
    gain1_ref[...] = sums_ref[32:33, :D]
    gain2_ref[...] = sums_ref[33:34, :D]
    bq_ref[...] = sums_ref[34:35, :D]
    bkv_ref[...] = sums_ref[35:37, :128]
    gq_ref[:, 0, :] = sums_ref[:28, 3200:3200 + QW]
    gkv_ref[:, 0, :] = sums_ref[:28, 3712:3840]
    go_ref[:, 0, :] = sums_ref[:28, 2688:2688 + QW]
    for ref, names in ((gd_ref.at[:, 0], "a0 b0 c0 c1"), (ggu_ref.at[:, 0], "a1 a2 c2"), (ggu_ref.at[:, 1], "b1 b2 c3")):
        for name in names.split():
            _, c, w, at = PIECES[name]
            at = at + COLS_AB * (name[0] == "c")
            ref[:, c:c + w] = sums_ref[:28, at:at + w]


def run_place(*arrays):
    vmem = pl.BlockSpec(memory_space=VMEM)
    shapes = (
        (MICRO, OWN, D), (MICRO, OWN, D), (1, D), (28, 1, QW), (1, D), (28, 1, 128), (2, 128),
        (28, 1, QW), (1, D), (28, 2, FH), (28, 1, FH),
    )
    return pl.pallas_call(
        place_kernel,
        out_shape=tuple(jax.ShapeDtypeStruct(s, F32 if i else BF) for i, s in enumerate(shapes)),
        in_specs=[vmem] * 2,
        out_specs=(vmem,) * 11,
        compiler_params=pltpu.CompilerParams(vmem_limit_bytes=32 * MIB),
        name="place",
    )(*arrays)


def body(
    inputs, cotangent, lengths, gain_attn, w_query, b_query, w_keyval, b_keyval, w_out, gain_mlp, w_gate_up, w_down,
):
    outs = run_train(
        lengths[:, 0], inputs, cotangent, gain_attn, gain_mlp, b_query, b_keyval[0],
        jnp.swapaxes(w_query[0], 0, 1), w_keyval[0, :, 0], w_out[0],
        jnp.swapaxes(w_gate_up[0], 0, 1), w_down[0],
    )
    so, ig, gain1, gq, bq, gkv, bkv, go, gain2, ggu, gd = run_place(*outs)
    return (
        so[None], ig[None], gain1, jnp.swapaxes(gq, 0, 1), bq, gkv[None], bkv[None],
        jnp.transpose(go, (1, 2, 0)), gain2, ggu[None], jnp.transpose(gd, (1, 2, 0)),
    )


def solution(mesh):
    placed = (
        P(None, ("dp", "tensor"), None),
        P(None, ("dp", "tensor"), None),
        P(None, "dp", None),
        P("pipe", None),
        P("pipe", None, "tensor"),
        P("pipe", "tensor"),
        P("pipe", None, "tensor", None),
        P("pipe", "tensor", None),
        P("pipe", "tensor", None),
        P("pipe", None),
        P("pipe", None, None, "tensor"),
        P("pipe", "tensor", None),
    )
    return jax.shard_map(
        body,
        mesh=mesh,
        in_specs=placed,
        out_specs=(
            P("pipe", None, ("dp", "tensor"), None),
            P("pipe", None, ("dp", "tensor"), None),
            P("pipe", None),
            P("pipe", "dp", "tensor"),
            P("pipe", None),
            P("pipe", "dp", "tensor", None),
            P("pipe", None, None),
            P("pipe", "tensor", "dp"),
            P("pipe", None),
            P("pipe", "dp", None, "tensor"),
            P("pipe", "tensor", "dp"),
        ),
        check_vma=False,
    )
```

```python
import functools

import jax
import jax.numpy as jnp
import numpy as np
from jax import lax
from jax.experimental import pallas as pl
from jax.experimental.pallas import tpu as pltpu
from jax.sharding import PartitionSpec as P

D = 896
HEADS = 14
HEAD = 64
CAP = 128
SEQS = 4
MICRO = 2
ROWS = MICRO * CAP
OWN = CAP // 2
FH = 2432
QW = 448
EPS = 1e-06
THETA = 1000000.0
MIB = 1024 * 1024

BF = jnp.bfloat16
F32 = jnp.float32
MESH = pl.DeviceIdType.MESH
VMEM = pltpu.VMEM

PIECES = {
    "a0": ("down", 0, 640, 0), "a1": ("gate", 0, 896, 640), "a2": ("gate", 896, 1152, 1536),
    "a3": ("out", 0, 512, 2688), "a4": ("qkv", 0, 640, 3200),
    "b0": ("down", 640, 640, 3840), "b1": ("up", 0, 896, 4480), "b2": ("up", 896, 1280, 5376),
    "c0": ("down", 1280, 512, 0), "c1": ("down", 1792, 640, 512), "c2": ("gate", 2048, 384, 1152), "c3": ("up", 2176, 256, 1536),
}
NAMES = tuple(PIECES)
COLS_AB = 6656
COLS_C = 1792
SPLIT = {"c0": 256, "c1": 256, "c2": 256, "c3": 128}
SERVICE = (
    "cx:c0 m0:a0 m0:a1 m0:b0",
    "m0:b1 m0:a2 m0:b2 m0:a3",
    "m0:c0 cx:c1 s:b0 m0:a4",
    "s:b1 cx:c2 s:a0 s:b2",
    "s:a1 s:c0 cx:c3 m0:c1",
    "m0:c2 s:a2 m1:a0 s:a3",
    "m1:a1 m1:b0 m0:c3 s:c1",
    "s:a4 s:c2 m1:b1 m1:a2",
    "m1:b2 t:a0 m1:a3 m1:c0",
    "t:a1 t:b0 e:a0 s:c3",
    "m1:c1 m1:a4 m1:c2 t:b1",
    "e:a1 t:a2 t:a3 e:b0",
    "t:b2 t:c0 m1:c3 t:a4",
    "t:c1 t:c2 e:b1 t:c3",
    "e:a2 e:a3 e:b2 e:a4",
)
SERVICE = tuple(event for line in SERVICE for event in line.split())
TILES = ((0, 512), (512, 512), (1024, 512), (1536, 512), (2048, 384))
WIDE = ((0, 256), (256, 256), (512, 256), (768, 128))


def nn(a, b):
    return lax.dot_general(a, b, (((1,), (0,)), ((), ())), preferred_element_type=F32)


def nt(a, b):
    return lax.dot_general(a, b, (((1,), (1,)), ((), ())), preferred_element_type=F32)


def tn(a, b):
    return lax.dot_general(a, b, (((0,), (0,)), ((), ())), preferred_element_type=F32)


def rope_table():
    half = HEAD // 2
    frequency = np.power(np.float32(THETA), -(np.arange(half, dtype=np.float32) * np.float32(2.0 / HEAD)))
    phases = (np.arange(CAP, dtype=np.float32)[:, None] * frequency[None, :].astype(np.float32)).astype(np.float32)
    phases = phases.astype(np.float64)
    cosine = np.concatenate([np.cos(phases)] * 4, axis=1).astype(np.float32)
    sine = np.concatenate([-np.sin(phases), np.sin(phases)] * 2, axis=1).astype(np.float32)
    parts = []
    for table in (cosine, sine):
        rest = table
        for _ in range(3):
            piece = rest.astype(jnp.bfloat16)
            parts.append(piece)
            rest = rest - piece.astype(np.float32)
    return np.concatenate(parts, axis=1)


def row_order():
    index = np.arange(D)
    y, z, x_hi, k = index // 224, index // 56 % 4, index // 28 % 2, index % 28
    source = (x_hi * 16 + z * 4 + y) * 28 + k
    return (source[:, None] == np.arange(D)[None, :]).astype(jnp.bfloat16)


def turn(block, lane):
    low = (lane & 63) < 32
    return jnp.where(low, pltpu.roll(block, 96, 1), pltpu.roll(block, 32, 1))


def train_kernel(
    len_ref, x_ref, cot_ref, g1_ref, g2_ref, bq_ref, bkv_ref, tab_ref,
    wq_hbm, wkv_hbm, wo_hbm, wgu_hbm, wd_hbm, perm_hbm,
    sums_ref, rows_ref,
    wq, wkv, wo, wgu, wd, perm, xbuf, gbuf, e1s, e1r, e2s, e2r, pipe_out,
    n1, n2, qb, kb, vb, pmat, mix, middle, dgate, dup, hidden, lt, part, gmid, cs, allow, gqkv,
    lt_n, mb_ref, gdown, gout, gqkv_w,
    r1, r2, h2, q1, q2, h3, q3, cx, c1, c2, hc, d1, d2, small_in,
    load_sem, send_sem, recv_sem, sum_send, sum_recv, small_send, small_recv,
):
    pipe = lax.axis_index("pipe")
    t = lax.axis_index("tensor")
    rank = lax.axis_index("dp")
    other = 1 - t
    x_hi, z, y = rank // 16, (rank // 4) % 4, rank % 4
    pos = (y, z)

    loads = [
        pltpu.make_async_copy(wq_hbm, wq.at[pl.ds(0, QW)], load_sem.at[0]),
        pltpu.make_async_copy(wkv_hbm, wkv, load_sem.at[1]),
        pltpu.make_async_copy(wo_hbm, wo.at[pl.ds(0, QW)], load_sem.at[2]),
        pltpu.make_async_copy(wgu_hbm, wgu, load_sem.at[3]),
        pltpu.make_async_copy(wd_hbm, wd, load_sem.at[4]),
        pltpu.make_async_copy(perm_hbm, perm, load_sem.at[5]),
    ]
    for c in loads:
        c.start()

    def to_core(src, dst, i):
        return pltpu.make_async_remote_copy(
            src_ref=src, dst_ref=dst, send_sem=send_sem.at[i], recv_sem=recv_sem.at[i],
            device_id={"tensor": other}, device_id_type=MESH)

    def to_pipe(src, dst, i):
        return pltpu.make_async_remote_copy(
            src_ref=src, dst_ref=dst, send_sem=send_sem.at[i], recv_sem=recv_sem.at[i],
            device_id={"pipe": 1 - pipe}, device_id_type=MESH)

    share_x = [to_core(xbuf.at[m, t], xbuf.at[m, t], 8 * m) for m in range(MICRO)]
    share_g = to_core(gbuf.at[:, t], gbuf.at[:, t], 1)
    pass_x = [to_pipe(pipe_out.at[m], xbuf.at[m, t], 2 + 7 * m) for m in range(MICRO)]
    pass_g = to_pipe(pipe_out, gbuf.at[:, t], 3)
    swap_1 = to_core(e1s, e1r, 4)
    swap_2 = to_core(e2s, e2r, 5)
    swap_3 = to_core(e1s, e1r, 6)
    swap_4 = to_core(e2s, e2r, 7)

    def at(yy, zz, xx):
        return {"dp": xx * 16 + zz * 4 + yy}

    def along(axis, step):
        if axis == 0:
            return at((y + step) % 4, z, x_hi)
        return at(y, (z + step) % 4, x_hi)

    x_peer = at(y, z, 1 - x_hi)
    peers = [along(0, 1), along(0, 3), along(1, 1), along(1, 3), x_peer, {"tensor": other}, {"pipe": 1 - pipe}]
    barrier = pltpu.get_barrier_semaphore()
    for peer in peers:
        pl.semaphore_signal(barrier, inc=1, device_id=peer, device_id_type=MESH)
    pl.semaphore_wait(barrier, len(peers))

    def remote(src, dst, peer, *sem):
        return pltpu.make_async_remote_copy(
            src_ref=src, dst_ref=dst, send_sem=sum_send.at[sem], recv_sem=sum_recv.at[sem],
            device_id=peer, device_id_type=MESH)

    bufs = {"down": gdown, "gate": wgu.at[0], "up": wgu.at[1], "out": gout, "qkv": gqkv_w}

    def columns(name, half=None):
        _, _, w, c = PIECES[name]
        if half is None:
            return pl.ds(c, w)
        cutoff = SPLIT[name]
        return pl.ds(c, cutoff) if half == 0 else pl.ds(c + cutoff, w - cutoff)

    def held(name, start, count):
        buf, c, w, _ = PIECES[name]
        return bufs[buf].at[pl.ds(pl.multiple_of(start, 16), count), pl.ds(c, w)]

    def ring(name, stage):
        if name[0] == "c":
            here = lambda half: columns(name, half)
            if stage == 0:
                return (1, lambda q, half: cx.at[pl.ds(pl.multiple_of(q * 112, 16), 112), here(half)],
                        lambda half: c1.at[:, here(half)], lambda k, half: c2.at[k, :, here(half)])
            return (0, lambda q, half: hc.at[q, :, here(half)],
                    lambda half: d1.at[:, here(half)], lambda k, half: d2.at[k, :, here(half)])
        axis = "ab".index(name[0])
        cols = columns(name)
        if stage == 0:
            return (axis, lambda q, half: held(name, q * 224 + 112 * half, 112),
                    lambda half: r1.at[half, :, cols], lambda k, half: r2.at[k, half, :, cols])
        return (1 - axis, lambda q, half: h2.at[q, pl.ds(32 * half, 32), cols],
                lambda half: q1.at[half, :, cols], lambda k, half: q2.at[k, half, :, cols])

    def ring_copy(name, stage, k):
        axis, block, first, last = ring(name, stage)
        f = pos[axis]
        ahead, behind = along(axis, 1), along(axis, 3)
        src, dst, peer = (
            lambda: (block((f + 2) % 4, 0), first(0), ahead),
            lambda: (block((f + 2) % 4, 1), first(1), behind),
            lambda: (block((f + 1) % 4, 1), last(0, 1), ahead),
            lambda: (block((f + 3) % 4, 0), last(1, 0), behind),
            lambda: (first(0), last(0, 0), ahead),
            lambda: (first(1), last(1, 1), behind),
        )[k]()
        return remote(src, dst, peer, NAMES.index(name), 6 * stage + k)

    def ring_begin(name, stage):
        for k in range(4):
            ring_copy(name, stage, k).start()

    def ring_middle(name, stage):
        axis, block, first, _ = ring(name, stage)
        f = pos[axis]
        for k, q in enumerate(((f + 1) % 4, (f + 3) % 4)):
            ring_copy(name, stage, k).wait_recv()
            own = block(q, k)[...]
            slot = first(k)
            slot[...] = (own.astype(F32) + slot[...].astype(F32)).astype(BF)
            ring_copy(name, stage, 4 + k).start()

    def ring_total(name, stage):
        axis, block, _, last = ring(name, stage)
        for k in range(2, 6):
            ring_copy(name, stage, k).wait_recv()
        return [
            block(pos[axis], half)[...].astype(F32) + last(0, half)[...].astype(F32) + last(1, half)[...].astype(F32)
            for half in range(2)]

    def x_copy(name):
        if name[0] == "c":
            return remote(held(name, (1 - x_hi) * 448, 448), cx.at[:, columns(name)], x_peer, NAMES.index(name), 12)
        cols = columns(name)
        return remote(h3.at[:, cols], q3.at[:, cols], x_peer, NAMES.index(name), 12)

    def begin(name):
        if name[0] == "c":
            x_copy(name).start()
        else:
            ring_begin(name, 0)

    def serve(event, name):
        cols = columns(name)
        if event == "cx":
            x_copy(name).wait_recv()
            own = held(name, x_hi * 448, 448)[...]
            cx[:, cols] = (own.astype(F32) + cx[:, cols].astype(F32)).astype(BF)
            ring_begin(name, 0)
        elif event == "m0":
            ring_middle(name, 0)
        elif event == "s":
            sums = ring_total(name, 0)
            for k in range(4):
                if name[0] == "c":
                    for half in range(2):
                        block = sums[half][28 * k:28 * k + 28]
                        zeros = jnp.zeros((4, block.shape[1]), F32)
                        hc[k, :, columns(name, half)] = jnp.concatenate([block, zeros], axis=0).astype(BF)
                else:
                    block = sums[k // 2][(k % 2) * 56:(k % 2 + 1) * 56]
                    zeros = jnp.zeros((8, block.shape[1]), F32)
                    h2[k, :, cols] = jnp.concatenate([block, zeros], axis=0).astype(BF)
            ring_begin(name, 1)
        elif event == "m1":
            ring_middle(name, 1)
        elif event == "t":
            sums = ring_total(name, 1)
            if name[0] == "c":
                for half in range(2):
                    at = columns(name, half)
                    sums_ref[:28, pl.ds(COLS_AB + at.start, at.size)] = sums[half][:28]
            else:
                whole = jnp.concatenate(sums, axis=0)
                first, last = whole[:32], whole[28:60]
                upper = x_hi == 1
                h3[:, cols] = jnp.where(upper, first, last).astype(BF)
                sums_ref[:28, cols] = jnp.where(upper, last, first)[:28]
                x_copy(name).start()
        else:
            x_copy(name).wait_recv()
            sums_ref[:28, cols] = sums_ref[:28, cols] + q3[:, cols].astype(F32)[:28]

    small_peers = [
        along(0, 1 + 2 * (y % 2)), along(0, 3 - 2 * (y % 2)),
        along(1, 1 + 2 * (z % 2)), along(1, 3 - 2 * (z % 2)), x_peer, {"tensor": other},
    ]

    def small_copy(k):
        return pltpu.make_async_remote_copy(
            src_ref=small_in.at[0, k], dst_ref=small_in.at[1, k], send_sem=small_send.at[k], recv_sem=small_recv.at[k],
            device_id=small_peers[k], device_id_type=MESH)

    def small_step(k):
        if k > 0:
            small_copy(k - 1).wait_recv()
            total = small_in[0, k - 1] + small_in[1, k - 1]
            if k < 6:
                small_in[0, k] = total
            else:
                sums_ref[32:40, :D] = total
        if k < 6:
            small_copy(k).start()

    @pl.when(pipe == 0)
    def _():
        xbuf[:, t] = x_ref[...]

    @pl.when(pipe == 1)
    def _():
        gbuf[:, t] = cot_ref[...]
        share_g.start()

    wq[pl.ds(QW, 64), :] = jnp.zeros((64, D), BF)
    wo[pl.ds(QW, 64), :] = jnp.zeros((64, D), BF)
    slot = lax.broadcasted_iota(jnp.int32, (CAP, CAP), 0)
    lane = lax.broadcasted_iota(jnp.int32, (CAP, CAP), 1)
    for m in range(MICRO):
        end = 0
        seg_row = jnp.zeros((CAP, CAP), jnp.int32)
        seg_col = jnp.zeros((CAP, CAP), jnp.int32)
        start = jnp.zeros((CAP, CAP), jnp.int32)
        for s in range(SEQS):
            end = end + len_ref[m, s]
            passed = slot >= end
            seg_row = seg_row + passed.astype(jnp.int32)
            seg_col = seg_col + (lane >= end).astype(jnp.int32)
            start = jnp.where(passed, end, start)
        allow[m] = jnp.where((seg_row == seg_col) & (lane <= slot), 1.0, 0.0)
        cs[m, 2] = jnp.where(seg_row < SEQS, 1.0, 0.0)
        one_hot = jnp.where(slot - start == lane, 1.0, 0.0).astype(BF)
        table = nn(one_hot, tab_ref[...])
        cs[m, 0] = table[:, :128] + table[:, 128:256] + table[:, 256:384]
        cs[m, 1] = table[:, 384:512] + table[:, 512:640] + table[:, 640:768]
    bias_q = jnp.concatenate([bq_ref[...].astype(F32), jnp.zeros((1, 64), F32)], axis=1)
    bias_kv = bkv_ref[...].astype(F32)
    gain_1 = g1_ref[...].astype(F32)
    gain_2 = g2_ref[...].astype(F32)

    @pl.when(pipe == 1)
    def _():
        share_g.wait()
        for m in range(MICRO):
            gbuf[m] = gbuf[m] * cs[m, 2][:, :1].astype(BF).reshape(2, OWN, 1)
        loads[4].wait()
        for c, w in TILES:
            gdown[:ROWS, c:c + w] = nt(gbuf[...].reshape(ROWS, D), wd[c:c + w, :]).astype(BF)

    half_lane = lax.broadcasted_iota(jnp.int32, (CAP, 128), 1)

    def arrived(m):
        @pl.when(pipe == 1)
        def _():
            pass_x[m].wait_recv()
            share_x[m].start()

    def projections(m):
        share_x[m].wait()
        rows = pl.ds(m * CAP, CAP)
        stream = xbuf[m].astype(F32).reshape(CAP, D)
        inv = lax.rsqrt(jnp.mean(stream * stream, axis=-1, keepdims=True) + EPS)
        n1[rows, :] = (stream * inv * gain_1).astype(BF)
        qs = nt(n1[rows, :], wq[...]) + bias_q
        vk = pltpu.roll(nn(n1[rows, :], wkv[...]) + bias_kv, 64, 1)
        for j in range(4):
            block = qs[:, j * 128:(j + 1) * 128]
            if j == 3:
                block = jnp.where(half_lane < 64, block, vk)
            block = block * cs[m, 0] + turn(block, half_lane) * cs[m, 1]
            qb[m, j] = block.astype(BF)
            if j == 3:
                odd = jnp.where(half_lane >= 64, block, 0.0)
                kb[m, 1] = odd.astype(BF)
                kb[m, 0] = pltpu.roll(odd, 64, 1).astype(BF)
        even = jnp.where(half_lane < 64, vk, 0.0)
        vb[m, 0] = even.astype(BF)
        vb[m, 1] = pltpu.roll(even, 64, 1).astype(BF)

    def attention(m):
        q_even = qb[m].reshape(4 * CAP, 128)
        q_odd = qb[m, :3].reshape(3 * CAP, 128)
        seen = allow[m] > 0.0
        mixed = []
        for parity, queries, count in ((0, q_even, 4), (1, q_odd, 3)):
            scores = nt(queries, kb[m, parity]).reshape(count, CAP, CAP) * HEAD ** (-0.5)
            scores = jnp.where(seen[None], scores, -1e30)
            top = jnp.max(scores, axis=-1, keepdims=True)
            grown = jnp.exp(scores - top)
            p = grown * (1.0 / jnp.sum(grown, axis=-1, keepdims=True))
            pmat[m, pl.ds(4 * parity, count)] = p
            mixed.append(nn(p.reshape(count * CAP, CAP).astype(BF), vb[m, parity]))
        for j in range(4):
            block = mixed[0][j * CAP:(j + 1) * CAP]
            if j < 3:
                block = block + mixed[1][j * CAP:(j + 1) * CAP]
            mix[pl.ds(m * CAP, CAP), j * 128:(j + 1) * 128] = block.astype(BF)

    @pl.when(pipe == 0)
    def _():
        share_x[0].start()
        share_x[1].start()

    loads[0].wait()
    loads[1].wait()
    arrived(0)
    projections(0)
    arrived(1)
    attention(0)
    projections(1)
    attention(1)
    loads[2].wait()
    for c, w in WIDE:
        e1s[:, c:c + w] = nn(mix[...], wo[:, c:c + w]).astype(BF)
    swap_1.start()
    swap_1.wait()
    mid = xbuf[...].astype(F32).reshape(ROWS, D) + (e1s[...].astype(F32) + e1r[...].astype(F32))
    middle[...] = mid.reshape(MICRO, 2, OWN, D)
    inv = lax.rsqrt(jnp.mean(mid * mid, axis=-1, keepdims=True) + EPS)
    n2[...] = (mid * inv * gain_2).astype(BF)
    loads[3].wait()
    for c, w in TILES:
        g = nn(n2[...], wgu[0, :, c:c + w])
        u = nn(n2[...], wgu[1, :, c:c + w])
        sig = jax.nn.sigmoid(g)
        silu = g * sig
        hidden[:, c:c + w] = (silu * u).astype(BF)
        dup[:, c:c + w] = silu.astype(BF)
        dgate[:, c:c + w] = (u * sig * (1.0 + g * (1.0 - sig))).astype(BF)

    @pl.when(pipe == 0)
    def _():
        loads[4].wait()

    for c, w in WIDE:
        part[:, :, :, c:c + w] = nn(hidden[...], wd[:, c:c + w]).reshape(MICRO, 2, OWN, w)
    e2s[...] = part[:, other].astype(BF)
    swap_2.start()
    swap_2.wait()
    pipe_out[...] = (middle[:, t] + (part[:, t] + e2r[...].astype(F32))).astype(BF)
    rows_ref[0] = pipe_out[...].astype(F32)

    def reordered(turned):
        return jnp.concatenate(
            [turned[(4 * b + a) * 56:(4 * b + a + 1) * 56] for a in range(4) for b in range(4)], axis=0).astype(BF)

    def weights_down():
        rows = gbuf[...].reshape(ROWS, D)
        turned = nt(perm[...], rows)
        for name, order in (("a0", 0), ("b0", 1), ("c0", 2), ("c1", 2)):
            if name != "c1":
                lt[order] = (
                    turned.astype(BF) if order == 0 else reordered(turned) if order == 1 else rows.astype(F32).T.astype(BF))
            _, c, w, _ = PIECES[name]
            gdown[:, c:c + w] = nn(lt[order], hidden[:, c:c + w]).astype(BF)
            begin(name)

    def weights_gate_up():
        for name, order in (("a1", 0), ("b1", 1), ("c2", 2), ("a2", 0), ("b2", 1), ("c3", 2)):
            buf, c, w, _ = PIECES[name]
            which, rhs = ((0, dgate), (1, dup))[buf == "up"]
            wgu[which, :, c:c + w] = nn(lt_n[order], rhs[:, c:c + w]).astype(BF)
            begin(name)

    def weights_out():
        lt[0] = nt(perm[...], mb_ref[...]).astype(BF)
        gout[...] = nn(lt[0], mix[...]).astype(BF)
        begin("a3")

    def norm_back(grads, values, gain):
        inverse = lax.rsqrt(jnp.mean(values * values, axis=-1, keepdims=True) + EPS)
        scaled = values * inverse
        weighted = grads * gain
        back = inverse * (weighted - scaled * jnp.mean(weighted * scaled, axis=-1, keepdims=True))
        return back, grads * scaled

    loads[5].wait()

    def backward(turn_now, _):
        chain = pl.when(turn_now == 0)
        weights = pl.when(turn_now == pipe)

        @chain
        def _():
            @pl.when(pipe == 0)
            def _():
                pass_x[0].start()
                pass_x[1].start()

        @weights
        def _():
            turned = nt(perm[...], n2[...])
            lt_n[0] = turned.astype(BF)
            lt_n[1] = reordered(turned)
            lt_n[2] = n2[...].astype(F32).T.astype(BF)

        @chain
        def _():
            @pl.when(pipe == 0)
            def _():
                pass_g.wait_recv()
                share_g.start()
                share_g.wait()

        weights(weights_down)

        @chain
        def _():
            def scale(c, w, gh):
                dgate[:, c:c + w] = (gh * dgate[:, c:c + w].astype(F32)).astype(BF)
                dup[:, c:c + w] = (gh * dup[:, c:c + w].astype(F32)).astype(BF)

            @pl.when(pipe == 0)
            def _():
                for c, w in TILES:
                    scale(c, w, nt(gbuf[...].reshape(ROWS, D), wd[c:c + w, :]))

            @pl.when(pipe == 1)
            def _():
                for c, w in TILES:
                    scale(c, w, gdown[:ROWS, c:c + w].astype(F32))

            for c, w in WIDE:
                e1s[:, c:c + w] = (nt(dgate[...], wgu[0, c:c + w, :]) + nt(dup[...], wgu[1, c:c + w, :])).astype(BF)
            swap_3.start()

        weights(weights_gate_up)

        @chain
        def _():
            swap_3.wait()
            grads = e1s[...].astype(F32) + e1r[...].astype(F32)
            back, terms = norm_back(grads, middle[...].reshape(ROWS, D), gain_2)
            row = lax.broadcasted_iota(jnp.int32, (ROWS, 1), 0)
            mine = ((row >> 6) & 1) == t
            small_in[0, 0] = jnp.zeros((8, D), F32)
            small_in[0, 0, 1:2, :] = jnp.sum(jnp.where(mine, terms, 0.0), axis=0, keepdims=True)
            grad_mid = gbuf[...].reshape(ROWS, D).astype(F32) + back
            gmid[...] = grad_mid.reshape(MICRO, 2, OWN, D)
            mb_ref[...] = grad_mid.astype(BF)

        weights(weights_out)
        chain(attention_back)
        return 0

    def attention_back():
        gmix = nt(mb_ref[...], wo[...]).astype(BF)
        for m in range(MICRO):
            blocks = [gmix[m * CAP:(m + 1) * CAP, j * 128:(j + 1) * 128] for j in range(4)]
            q_even = qb[m].reshape(4 * CAP, 128)
            q_odd = qb[m, :3].reshape(3 * CAP, 128)
            out = []
            for parity, queries, count in ((0, q_even, 4), (1, q_odd, 3)):
                gm = jnp.concatenate(blocks[:count], axis=0)
                p = pmat[m, pl.ds(4 * parity, count)].reshape(count * CAP, CAP)
                gp = nt(gm, vb[m, parity])
                ds = (p * (gp - jnp.sum(p * gp, axis=-1, keepdims=True))).astype(BF)
                out.append((nn(ds, kb[m, parity]), tn(ds, queries), tn(p.astype(BF), gm)))
            keys = pltpu.roll(out[0][1], 64, 1) + out[1][1]
            values = out[0][2] + pltpu.roll(out[1][2], 64, 1)
            rows = pl.ds(m * CAP, CAP)
            for j in range(4):
                block = out[0][0][j * CAP:(j + 1) * CAP]
                if j < 3:
                    block = block + out[1][0][j * CAP:(j + 1) * CAP]
                else:
                    block = jnp.where(half_lane < 64, block, keys)
                block = block * HEAD ** (-0.5)
                block = block * cs[m, 0] - turn(block, half_lane) * cs[m, 1]
                if j == 3:
                    gqkv[rows, 512:640] = pltpu.roll(jnp.where(half_lane < 64, values, block), 64, 1).astype(BF)
                    block = jnp.where(half_lane < 64, block, 0.0)
                gqkv[rows, j * 128:(j + 1) * 128] = block.astype(BF)
        for c, w in WIDE:
            part[:, :, :, c:c + w] = (
                nn(gqkv[:, :512], wq[:, c:c + w]) + nt(gqkv[:, 512:], wkv[c:c + w, :])).reshape(MICRO, 2, OWN, w)
        e2s[...] = part[:, other].astype(BF)
        swap_4.start()
        swap_4.wait()
        grads = (part[:, t] + e2r[...].astype(F32)).reshape(MICRO * OWN, D)
        back, terms = norm_back(grads, xbuf[:, t].astype(F32).reshape(MICRO * OWN, D), gain_1)
        total = gmid[:, t] + back.reshape(MICRO, OWN, D)
        rows_ref[1] = total

        @pl.when(pipe == 0)
        def _():
            pass_x[0].wait_send()
            pass_x[1].wait_send()

        pipe_out[...] = total.astype(BF)

        @pl.when(pipe == 1)
        def _():
            pass_g.start()

        small_in[0, 0, 0:1, :] = jnp.sum(terms, axis=0, keepdims=True)
        bias = jnp.sum(gqkv[...].astype(F32), axis=0, keepdims=True)
        wide = jnp.concatenate([bias[:, :512], jnp.zeros((1, D - 512), F32)], axis=1)
        small_in[0, 0, 2:3, :] = jnp.where(t == 0, wide, pltpu.roll(wide, QW, 1))
        for c in range(2):
            small_in[0, 0, 3 + c:4 + c, :128] = jnp.where(t == c, bias[:, 512:], 0.0)

    lax.fori_loop(0, 2, backward, 0)
    lt[1] = nt(perm[...], n1[...]).astype(BF)
    gqkv_w[...] = nn(lt[1], gqkv[...]).astype(BF)
    begin("a4")

    for step, event in enumerate(SERVICE):
        if step % 4 == 0 and step < 28:
            small_step(step // 4)
        serve(*event.split(":"))
    for name in NAMES:
        for stage in range(2):
            for k in range(6):
                ring_copy(name, stage, k).wait_send()
        x_copy(name).wait_send()
    for k in range(6):
        small_copy(k).wait_send()

    @pl.when(pipe == 1)
    def _():
        pass_g.wait_send()


def run_train(lens, x, cot, g1, g2, bq, bkv, wq, wkv, wo, wgu, wd):
    vmem = pl.BlockSpec(memory_space=VMEM)
    hbm = pl.BlockSpec(memory_space=pl.ANY)
    dma = pltpu.SemaphoreType.DMA
    return pl.pallas_call(
        train_kernel,
        out_shape=(
            jax.ShapeDtypeStruct((40, COLS_AB + COLS_C), F32),
            jax.ShapeDtypeStruct((2, MICRO, OWN, D), F32),
        ),
        in_specs=[pl.BlockSpec(memory_space=pltpu.SMEM)] + [vmem] * 7 + [hbm] * 6,
        out_specs=(vmem,) * 2,
        scratch_shapes=[
            VMEM((512, D), BF), VMEM((D, 128), BF), VMEM((512, D), BF), VMEM((2, D, FH), BF), VMEM((FH, D), BF), VMEM((D, D), BF),
            VMEM((MICRO, 2, OWN, D), BF), VMEM((MICRO, 2, OWN, D), BF),
            VMEM((ROWS, D), BF), VMEM((ROWS, D), BF),
            VMEM((MICRO, OWN, D), BF), VMEM((MICRO, OWN, D), BF), VMEM((MICRO, OWN, D), BF),
            VMEM((ROWS, D), BF), VMEM((ROWS, D), BF),
            VMEM((MICRO, 4, CAP, 128), BF), VMEM((MICRO, 2, CAP, 128), BF), VMEM((MICRO, 2, CAP, 128), BF),
            VMEM((MICRO, 7, CAP, CAP), F32), VMEM((ROWS, 512), BF), VMEM((MICRO, 2, OWN, D), F32),
            VMEM((ROWS, FH), BF), VMEM((ROWS, FH), BF), VMEM((ROWS, FH), BF),
            VMEM((3, D, ROWS), BF), VMEM((MICRO, 2, OWN, D), F32), VMEM((MICRO, 2, OWN, D), F32),
            VMEM((MICRO, 3, CAP, 128), F32), VMEM((MICRO, CAP, CAP), F32), VMEM((ROWS, 640), BF),
            VMEM((3, D, ROWS), BF), VMEM((ROWS, D), BF), VMEM((D, FH), BF), VMEM((D, 512), BF), VMEM((D, 640), BF),
            VMEM((2, 112, COLS_AB), BF), VMEM((2, 2, 112, COLS_AB), BF),
            VMEM((4, 64, COLS_AB), BF), VMEM((2, 32, COLS_AB), BF), VMEM((2, 2, 32, COLS_AB), BF),
            VMEM((32, COLS_AB), BF), VMEM((32, COLS_AB), BF),
            VMEM((448, COLS_C), BF), VMEM((112, COLS_C), BF), VMEM((2, 112, COLS_C), BF),
            VMEM((4, 32, COLS_C), BF), VMEM((32, COLS_C), BF), VMEM((2, 32, COLS_C), BF),
            VMEM((2, 6, 8, D), F32),
            dma((6,)), dma((10,)), dma((10,)), dma((len(NAMES), 13)), dma((len(NAMES), 13)), dma((6,)), dma((6,)),
        ],
        compiler_params=pltpu.CompilerParams(collective_id=0, has_side_effects=True, vmem_limit_bytes=63 * MIB),
        name="train",
    )(lens, x, cot, g1, g2, bq, bkv, jnp.asarray(rope_table()), wq, wkv, wo, wgu, wd, jnp.asarray(row_order()))


def place_kernel(
    sums_ref, rows_ref,
    so_ref, ig_ref, gain1_ref, gq_ref, bq_ref, gkv_ref, bkv_ref, go_ref, gain2_ref, ggu_ref, gd_ref,
):
    so_ref[...] = rows_ref[0].astype(BF)
    ig_ref[...] = rows_ref[1]
    gain1_ref[...] = sums_ref[32:33, :D]
    gain2_ref[...] = sums_ref[33:34, :D]
    bq_ref[...] = sums_ref[34:35, :D]
    bkv_ref[...] = sums_ref[35:37, :128]
    gq_ref[:, 0, :] = sums_ref[:28, 3200:3200 + QW]
    gkv_ref[:, 0, :] = sums_ref[:28, 3712:3840]
    go_ref[:, 0, :] = sums_ref[:28, 2688:2688 + QW]
    for ref, names in ((gd_ref.at[:, 0], "a0 b0 c0 c1"), (ggu_ref.at[:, 0], "a1 a2 c2"), (ggu_ref.at[:, 1], "b1 b2 c3")):
        for name in names.split():
            _, c, w, at = PIECES[name]
            at = at + COLS_AB * (name[0] == "c")
            ref[:, c:c + w] = sums_ref[:28, at:at + w]


def run_place(*arrays):
    vmem = pl.BlockSpec(memory_space=VMEM)
    shapes = (
        (MICRO, OWN, D), (MICRO, OWN, D), (1, D), (28, 1, QW), (1, D), (28, 1, 128), (2, 128),
        (28, 1, QW), (1, D), (28, 2, FH), (28, 1, FH),
    )
    return pl.pallas_call(
        place_kernel,
        out_shape=tuple(jax.ShapeDtypeStruct(s, F32 if i else BF) for i, s in enumerate(shapes)),
        in_specs=[vmem] * 2,
        out_specs=(vmem,) * 11,
        compiler_params=pltpu.CompilerParams(vmem_limit_bytes=60 * MIB),
        name="place",
    )(*arrays)


def body(
    inputs, cotangent, lengths, gain_attn, w_query, b_query, w_keyval, b_keyval, w_out, gain_mlp, w_gate_up, w_down,
):
    outs = run_train(
        lengths[:, 0], inputs, cotangent, gain_attn, gain_mlp, b_query, b_keyval[0],
        jnp.swapaxes(w_query[0], 0, 1), w_keyval[0, :, 0], w_out[0],
        jnp.swapaxes(w_gate_up[0], 0, 1), w_down[0],
    )
    so, ig, gain1, gq, bq, gkv, bkv, go, gain2, ggu, gd = run_place(*outs)
    return (
        so[None], ig[None], gain1, jnp.swapaxes(gq, 0, 1), bq, gkv[None], bkv[None],
        jnp.transpose(go, (1, 2, 0)), gain2, ggu[None], jnp.transpose(gd, (1, 2, 0)),
    )


def solution(mesh):
    placed = (
        P(None, ("dp", "tensor"), None),
        P(None, ("dp", "tensor"), None),
        P(None, "dp", None),
        P("pipe", None),
        P("pipe", None, "tensor"),
        P("pipe", "tensor"),
        P("pipe", None, "tensor", None),
        P("pipe", "tensor", None),
        P("pipe", "tensor", None),
        P("pipe", None),
        P("pipe", None, None, "tensor"),
        P("pipe", "tensor", None),
    )
    return jax.shard_map(
        body,
        mesh=mesh,
        in_specs=placed,
        out_specs=(
            P("pipe", None, ("dp", "tensor"), None),
            P("pipe", None, ("dp", "tensor"), None),
            P("pipe", None),
            P("pipe", "dp", "tensor"),
            P("pipe", None),
            P("pipe", "dp", "tensor", None),
            P("pipe", None, None),
            P("pipe", "tensor", "dp"),
            P("pipe", None),
            P("pipe", "dp", None, "tensor"),
            P("pipe", "tensor", "dp"),
        ),
        check_vma=False,
    )
```

```python
import functools

import jax
import jax.numpy as jnp
import numpy as np
from jax import lax
from jax.experimental import pallas as pl
from jax.experimental.pallas import tpu as pltpu
from jax.sharding import PartitionSpec as P

D = 896
HEADS = 14
HEAD = 64
CAP = 128
SEQS = 4
MICRO = 2
ROWS = MICRO * CAP
OWN = CAP // 2
FH = 2432
QW = 448
EPS = 1e-06
THETA = 1000000.0
MIB = 1024 * 1024

BF = jnp.bfloat16
F32 = jnp.float32
MESH = pl.DeviceIdType.MESH
VMEM = pltpu.VMEM

PIECES = {
    "a0": ("down", 0, 640, 0), "a1": ("gate", 0, 896, 640), "a2": ("gate", 896, 1152, 1536),
    "a3": ("out", 0, 512, 2688), "a4": ("qkv", 0, 640, 3200),
    "b0": ("down", 640, 640, 3840), "b1": ("up", 0, 896, 4480), "b2": ("up", 896, 1280, 5376),
    "c0": ("down", 1280, 512, 0), "c1": ("down", 1792, 640, 512), "c2": ("gate", 2048, 384, 1152), "c3": ("up", 2176, 256, 1536),
}
NAMES = tuple(PIECES)
COLS_AB = 6656
COLS_C = 1792
SPLIT = {"c0": 256, "c1": 256, "c2": 256, "c3": 128}
SERVICE = (
    "cx:c0 m0:a0 m0:a1 m0:b0",
    "m0:b1 m0:a2 m0:b2 m0:a3",
    "m0:c0 s:b0 cx:c1 m0:a4",
    "s:b1 s:a0 s:b2 s:a1",
    "s:c0 cx:c2 m0:c1 m1:a0",
    "s:a2 m1:a1 s:a3 cx:c3",
    "m0:c2 m1:b0 s:c1 t:a0",
    "s:a4 m1:a2 m1:b1 t:a1",
    "m1:b2 m1:a3 e:a0 m0:c3",
    "m1:c0 s:c2 t:b0 m1:c1",
    "m1:a4 e:a1 t:b1 t:a2",
    "t:a3 t:b2 t:c0 s:c3",
    "m1:c2 t:c1 e:b0 t:a4",
    "e:b1 m1:c3 t:c2 e:a2",
    "e:a3 t:c3 e:b2 e:a4",
)
SERVICE = tuple(event for line in SERVICE for event in line.split())
TILES = ((0, 512), (512, 512), (1024, 512), (1536, 512), (2048, 384))
WIDE = ((0, 256), (256, 256), (512, 256), (768, 128))


def nn(a, b):
    return lax.dot_general(a, b, (((1,), (0,)), ((), ())), preferred_element_type=F32)


def nt(a, b):
    return lax.dot_general(a, b, (((1,), (1,)), ((), ())), preferred_element_type=F32)


def tn(a, b):
    return lax.dot_general(a, b, (((0,), (0,)), ((), ())), preferred_element_type=F32)


def rope_table():
    half = HEAD // 2
    frequency = np.power(np.float32(THETA), -(np.arange(half, dtype=np.float32) * np.float32(2.0 / HEAD)))
    phases = (np.arange(CAP, dtype=np.float32)[:, None] * frequency[None, :].astype(np.float32)).astype(np.float32)
    phases = phases.astype(np.float64)
    cosine = np.concatenate([np.cos(phases)] * 4, axis=1).astype(np.float32)
    sine = np.concatenate([-np.sin(phases), np.sin(phases)] * 2, axis=1).astype(np.float32)
    parts = []
    for table in (cosine, sine):
        rest = table
        for _ in range(3):
            piece = rest.astype(jnp.bfloat16)
            parts.append(piece)
            rest = rest - piece.astype(np.float32)
    return np.concatenate(parts, axis=1)


def row_order():
    index = np.arange(D)
    y, z, x_hi, k = index // 224, index // 56 % 4, index // 28 % 2, index % 28
    source = (x_hi * 16 + z * 4 + y) * 28 + k
    return (source[:, None] == np.arange(D)[None, :]).astype(jnp.bfloat16)


def turn(block, lane):
    low = (lane & 63) < 32
    return jnp.where(low, pltpu.roll(block, 96, 1), pltpu.roll(block, 32, 1))


def train_kernel(
    len_ref, x_ref, cot_ref, g1_ref, g2_ref, bq_ref, bkv_ref, tab_ref,
    wq_hbm, wkv_hbm, wo_hbm, wgu_hbm, wd_hbm, perm_hbm,
    sums_ref, rows_ref,
    wq, wkv, wo, wgu, wd, perm, xbuf, gbuf, e1s, e1r, e2s, e2r, pipe_out,
    n1, n2, qb, kb, vb, pmat, mix, middle, dgate, dup, hidden, lt, part, gmid, cs, allow, gqkv,
    lt_n, mb_ref, gdown, gout, gqkv_w,
    r1, r2, h2, q1, q2, h3, q3, cx, c1, c2, hc, d1, d2, small_in,
    load_sem, send_sem, recv_sem, sum_send, sum_recv, small_send, small_recv,
):
    pipe = lax.axis_index("pipe")
    t = lax.axis_index("tensor")
    rank = lax.axis_index("dp")
    other = 1 - t
    x_hi, z, y = rank // 16, (rank // 4) % 4, rank % 4
    pos = (y, z)

    loads = [
        pltpu.make_async_copy(wq_hbm, wq.at[pl.ds(0, QW)], load_sem.at[0]),
        pltpu.make_async_copy(wkv_hbm, wkv, load_sem.at[1]),
        pltpu.make_async_copy(wo_hbm, wo.at[pl.ds(0, QW)], load_sem.at[2]),
        pltpu.make_async_copy(wgu_hbm, wgu, load_sem.at[3]),
        pltpu.make_async_copy(wd_hbm, wd, load_sem.at[4]),
        pltpu.make_async_copy(perm_hbm, perm, load_sem.at[5]),
    ]
    for c in loads:
        c.start()

    def to_core(src, dst, i):
        return pltpu.make_async_remote_copy(
            src_ref=src, dst_ref=dst, send_sem=send_sem.at[i], recv_sem=recv_sem.at[i],
            device_id={"tensor": other}, device_id_type=MESH)

    def to_pipe(src, dst, i):
        return pltpu.make_async_remote_copy(
            src_ref=src, dst_ref=dst, send_sem=send_sem.at[i], recv_sem=recv_sem.at[i],
            device_id={"pipe": 1 - pipe}, device_id_type=MESH)

    share_x = [to_core(xbuf.at[m, t], xbuf.at[m, t], 8 * m) for m in range(MICRO)]
    share_g = to_core(gbuf.at[:, t], gbuf.at[:, t], 1)
    pass_x = [to_pipe(pipe_out.at[m], xbuf.at[m, t], 2 + 7 * m) for m in range(MICRO)]
    pass_g = to_pipe(pipe_out, gbuf.at[:, t], 3)
    swap_1 = to_core(e1s, e1r, 4)
    swap_2 = to_core(e2s, e2r, 5)
    swap_3 = to_core(e1s, e1r, 6)
    swap_4 = to_core(e2s, e2r, 7)

    def at(yy, zz, xx):
        return {"dp": xx * 16 + zz * 4 + yy}

    def along(axis, step):
        if axis == 0:
            return at((y + step) % 4, z, x_hi)
        return at(y, (z + step) % 4, x_hi)

    x_peer = at(y, z, 1 - x_hi)
    peers = [along(0, 1), along(0, 3), along(1, 1), along(1, 3), x_peer, {"tensor": other}, {"pipe": 1 - pipe}]
    barrier = pltpu.get_barrier_semaphore()
    for peer in peers:
        pl.semaphore_signal(barrier, inc=1, device_id=peer, device_id_type=MESH)
    pl.semaphore_wait(barrier, len(peers))

    def remote(src, dst, peer, *sem):
        return pltpu.make_async_remote_copy(
            src_ref=src, dst_ref=dst, send_sem=sum_send.at[sem], recv_sem=sum_recv.at[sem],
            device_id=peer, device_id_type=MESH)

    bufs = {"down": gdown, "gate": wgu.at[0], "up": wgu.at[1], "out": gout, "qkv": gqkv_w}

    def columns(name, half=None):
        _, _, w, c = PIECES[name]
        if half is None:
            return pl.ds(c, w)
        cutoff = SPLIT[name]
        return pl.ds(c, cutoff) if half == 0 else pl.ds(c + cutoff, w - cutoff)

    def held(name, start, count):
        buf, c, w, _ = PIECES[name]
        return bufs[buf].at[pl.ds(pl.multiple_of(start, 16), count), pl.ds(c, w)]

    def ring(name, stage):
        if name[0] == "c":
            here = lambda half: columns(name, half)
            if stage == 0:
                return (1, lambda q, half: cx.at[pl.ds(pl.multiple_of(q * 112, 16), 112), here(half)],
                        lambda half: c1.at[:, here(half)], lambda k, half: c2.at[k, :, here(half)])
            return (0, lambda q, half: hc.at[q, :, here(half)],
                    lambda half: d1.at[:, here(half)], lambda k, half: d2.at[k, :, here(half)])
        axis = "ab".index(name[0])
        cols = columns(name)
        if stage == 0:
            return (axis, lambda q, half: held(name, q * 224 + 112 * half, 112),
                    lambda half: r1.at[half, :, cols], lambda k, half: r2.at[k, half, :, cols])
        return (1 - axis, lambda q, half: h2.at[q, pl.ds(32 * half, 32), cols],
                lambda half: q1.at[half, :, cols], lambda k, half: q2.at[k, half, :, cols])

    def ring_copy(name, stage, k):
        axis, block, first, last = ring(name, stage)
        f = pos[axis]
        ahead, behind = along(axis, 1), along(axis, 3)
        src, dst, peer = (
            lambda: (block((f + 2) % 4, 0), first(0), ahead),
            lambda: (block((f + 2) % 4, 1), first(1), behind),
            lambda: (block((f + 1) % 4, 1), last(0, 1), ahead),
            lambda: (block((f + 3) % 4, 0), last(1, 0), behind),
            lambda: (first(0), last(0, 0), ahead),
            lambda: (first(1), last(1, 1), behind),
        )[k]()
        return remote(src, dst, peer, NAMES.index(name), 6 * stage + k)

    def ring_begin(name, stage):
        for k in range(4):
            ring_copy(name, stage, k).start()

    def ring_middle(name, stage):
        axis, block, first, _ = ring(name, stage)
        f = pos[axis]
        for k, q in enumerate(((f + 1) % 4, (f + 3) % 4)):
            ring_copy(name, stage, k).wait_recv()
            own = block(q, k)[...]
            slot = first(k)
            slot[...] = (own.astype(F32) + slot[...].astype(F32)).astype(BF)
            ring_copy(name, stage, 4 + k).start()

    def ring_total(name, stage):
        axis, block, _, last = ring(name, stage)
        for k in range(2, 6):
            ring_copy(name, stage, k).wait_recv()
        return [
            block(pos[axis], half)[...].astype(F32) + last(0, half)[...].astype(F32) + last(1, half)[...].astype(F32)
            for half in range(2)]

    def x_copy(name):
        if name[0] == "c":
            return remote(held(name, (1 - x_hi) * 448, 448), cx.at[:, columns(name)], x_peer, NAMES.index(name), 12)
        cols = columns(name)
        return remote(h3.at[:, cols], q3.at[:, cols], x_peer, NAMES.index(name), 12)

    def begin(name):
        if name[0] == "c":
            x_copy(name).start()
        else:
            ring_begin(name, 0)

    def serve(event, name):
        cols = columns(name)
        if event == "cx":
            x_copy(name).wait_recv()
            own = held(name, x_hi * 448, 448)[...]
            cx[:, cols] = (own.astype(F32) + cx[:, cols].astype(F32)).astype(BF)
            ring_begin(name, 0)
        elif event == "m0":
            ring_middle(name, 0)
        elif event == "s":
            sums = ring_total(name, 0)
            for k in range(4):
                if name[0] == "c":
                    for half in range(2):
                        block = sums[half][28 * k:28 * k + 28]
                        zeros = jnp.zeros((4, block.shape[1]), F32)
                        hc[k, :, columns(name, half)] = jnp.concatenate([block, zeros], axis=0).astype(BF)
                else:
                    block = sums[k // 2][(k % 2) * 56:(k % 2 + 1) * 56]
                    zeros = jnp.zeros((8, block.shape[1]), F32)
                    h2[k, :, cols] = jnp.concatenate([block, zeros], axis=0).astype(BF)
            ring_begin(name, 1)
        elif event == "m1":
            ring_middle(name, 1)
        elif event == "t":
            sums = ring_total(name, 1)
            if name[0] == "c":
                for half in range(2):
                    at = columns(name, half)
                    sums_ref[:28, pl.ds(COLS_AB + at.start, at.size)] = sums[half][:28]
            else:
                whole = jnp.concatenate(sums, axis=0)
                first, last = whole[:32], whole[28:60]
                upper = x_hi == 1
                h3[:, cols] = jnp.where(upper, first, last).astype(BF)
                sums_ref[:28, cols] = jnp.where(upper, last, first)[:28]
                x_copy(name).start()
        else:
            x_copy(name).wait_recv()
            sums_ref[:28, cols] = sums_ref[:28, cols] + q3[:, cols].astype(F32)[:28]

    small_peers = [
        along(0, 1 + 2 * (y % 2)), along(0, 3 - 2 * (y % 2)),
        along(1, 1 + 2 * (z % 2)), along(1, 3 - 2 * (z % 2)), x_peer, {"tensor": other},
    ]

    def small_copy(k):
        return pltpu.make_async_remote_copy(
            src_ref=small_in.at[0, k], dst_ref=small_in.at[1, k], send_sem=small_send.at[k], recv_sem=small_recv.at[k],
            device_id=small_peers[k], device_id_type=MESH)

    def small_step(k):
        if k > 0:
            small_copy(k - 1).wait_recv()
            total = small_in[0, k - 1] + small_in[1, k - 1]
            if k < 6:
                small_in[0, k] = total
            else:
                sums_ref[32:40, :D] = total
        if k < 6:
            small_copy(k).start()

    @pl.when(pipe == 0)
    def _():
        xbuf[:, t] = x_ref[...]

    @pl.when(pipe == 1)
    def _():
        gbuf[:, t] = cot_ref[...]
        share_g.start()

    wq[pl.ds(QW, 64), :] = jnp.zeros((64, D), BF)
    wo[pl.ds(QW, 64), :] = jnp.zeros((64, D), BF)
    slot = lax.broadcasted_iota(jnp.int32, (CAP, CAP), 0)
    lane = lax.broadcasted_iota(jnp.int32, (CAP, CAP), 1)
    for m in range(MICRO):
        end = 0
        seg_row = jnp.zeros((CAP, CAP), jnp.int32)
        seg_col = jnp.zeros((CAP, CAP), jnp.int32)
        start = jnp.zeros((CAP, CAP), jnp.int32)
        for s in range(SEQS):
            end = end + len_ref[m, s]
            passed = slot >= end
            seg_row = seg_row + passed.astype(jnp.int32)
            seg_col = seg_col + (lane >= end).astype(jnp.int32)
            start = jnp.where(passed, end, start)
        allow[m] = jnp.where((seg_row == seg_col) & (lane <= slot), 1.0, 0.0)
        cs[m, 2] = jnp.where(seg_row < SEQS, 1.0, 0.0)
        one_hot = jnp.where(slot - start == lane, 1.0, 0.0).astype(BF)
        table = nn(one_hot, tab_ref[...])
        cs[m, 0] = table[:, :128] + table[:, 128:256] + table[:, 256:384]
        cs[m, 1] = table[:, 384:512] + table[:, 512:640] + table[:, 640:768]
    bias_q = jnp.concatenate([bq_ref[...].astype(F32), jnp.zeros((1, 64), F32)], axis=1)
    bias_kv = bkv_ref[...].astype(F32)
    gain_1 = g1_ref[...].astype(F32)
    gain_2 = g2_ref[...].astype(F32)

    @pl.when(pipe == 1)
    def _():
        share_g.wait()
        for m in range(MICRO):
            gbuf[m] = gbuf[m] * cs[m, 2][:, :1].astype(BF).reshape(2, OWN, 1)
        loads[4].wait()
        for c, w in TILES:
            gdown[:ROWS, c:c + w] = nt(gbuf[...].reshape(ROWS, D), wd[c:c + w, :]).astype(BF)

    half_lane = lax.broadcasted_iota(jnp.int32, (CAP, 128), 1)

    def arrived(m):
        @pl.when(pipe == 1)
        def _():
            pass_x[m].wait_recv()
            share_x[m].start()

    def projections(m):
        share_x[m].wait()
        rows = pl.ds(m * CAP, CAP)
        stream = xbuf[m].astype(F32).reshape(CAP, D)
        inv = lax.rsqrt(jnp.mean(stream * stream, axis=-1, keepdims=True) + EPS)
        n1[rows, :] = (stream * inv * gain_1).astype(BF)
        qs = nt(n1[rows, :], wq[...]) + bias_q
        vk = pltpu.roll(nn(n1[rows, :], wkv[...]) + bias_kv, 64, 1)
        for j in range(4):
            block = qs[:, j * 128:(j + 1) * 128]
            if j == 3:
                block = jnp.where(half_lane < 64, block, vk)
            block = block * cs[m, 0] + turn(block, half_lane) * cs[m, 1]
            qb[m, j] = block.astype(BF)
            if j == 3:
                odd = jnp.where(half_lane >= 64, block, 0.0)
                kb[m, 1] = odd.astype(BF)
                kb[m, 0] = pltpu.roll(odd, 64, 1).astype(BF)
        even = jnp.where(half_lane < 64, vk, 0.0)
        vb[m, 0] = even.astype(BF)
        vb[m, 1] = pltpu.roll(even, 64, 1).astype(BF)

    def attention(m):
        q_even = qb[m].reshape(4 * CAP, 128)
        q_odd = qb[m, :3].reshape(3 * CAP, 128)
        seen = allow[m] > 0.0
        mixed = []
        for parity, queries, count in ((0, q_even, 4), (1, q_odd, 3)):
            scores = nt(queries, kb[m, parity]).reshape(count, CAP, CAP) * HEAD ** (-0.5)
            scores = jnp.where(seen[None], scores, -1e30)
            top = jnp.max(scores, axis=-1, keepdims=True)
            grown = jnp.exp(scores - top)
            p = grown * (1.0 / jnp.sum(grown, axis=-1, keepdims=True))
            pmat[m, pl.ds(4 * parity, count)] = p
            mixed.append(nn(p.reshape(count * CAP, CAP).astype(BF), vb[m, parity]))
        for j in range(4):
            block = mixed[0][j * CAP:(j + 1) * CAP]
            if j < 3:
                block = block + mixed[1][j * CAP:(j + 1) * CAP]
            mix[pl.ds(m * CAP, CAP), j * 128:(j + 1) * 128] = block.astype(BF)

    @pl.when(pipe == 0)
    def _():
        share_x[0].start()
        share_x[1].start()

    loads[0].wait()
    loads[1].wait()
    arrived(0)
    projections(0)
    arrived(1)
    attention(0)
    projections(1)
    attention(1)
    loads[2].wait()
    for c, w in WIDE:
        e1s[:, c:c + w] = nn(mix[...], wo[:, c:c + w]).astype(BF)
    swap_1.start()
    swap_1.wait()
    mid = xbuf[...].astype(F32).reshape(ROWS, D) + (e1s[...].astype(F32) + e1r[...].astype(F32))
    middle[...] = mid.reshape(MICRO, 2, OWN, D)
    inv = lax.rsqrt(jnp.mean(mid * mid, axis=-1, keepdims=True) + EPS)
    n2[...] = (mid * inv * gain_2).astype(BF)
    loads[3].wait()
    for c, w in TILES:
        g = nn(n2[...], wgu[0, :, c:c + w])
        u = nn(n2[...], wgu[1, :, c:c + w])
        sig = jax.nn.sigmoid(g)
        silu = g * sig
        hidden[:, c:c + w] = (silu * u).astype(BF)
        dup[:, c:c + w] = silu.astype(BF)
        dgate[:, c:c + w] = (u * sig * (1.0 + g * (1.0 - sig))).astype(BF)

    @pl.when(pipe == 0)
    def _():
        loads[4].wait()

    for c, w in WIDE:
        part[:, :, :, c:c + w] = nn(hidden[...], wd[:, c:c + w]).reshape(MICRO, 2, OWN, w)
    e2s[...] = part[:, other].astype(BF)
    swap_2.start()
    swap_2.wait()
    pipe_out[...] = (middle[:, t] + (part[:, t] + e2r[...].astype(F32))).astype(BF)
    rows_ref[0] = pipe_out[...].astype(F32)

    def reordered(turned):
        return jnp.concatenate(
            [turned[(4 * b + a) * 56:(4 * b + a + 1) * 56] for a in range(4) for b in range(4)], axis=0).astype(BF)

    def weights_down():
        rows = gbuf[...].reshape(ROWS, D)
        turned = nt(perm[...], rows)
        for name, order in (("a0", 0), ("b0", 1), ("c0", 2), ("c1", 2)):
            if name != "c1":
                lt[order] = (
                    turned.astype(BF) if order == 0 else reordered(turned) if order == 1 else rows.astype(F32).T.astype(BF))
            _, c, w, _ = PIECES[name]
            gdown[:, c:c + w] = nn(lt[order], hidden[:, c:c + w]).astype(BF)
            begin(name)

    def weights_gate_up():
        for name, order in (("a1", 0), ("b1", 1), ("c2", 2), ("a2", 0), ("b2", 1), ("c3", 2)):
            buf, c, w, _ = PIECES[name]
            which, rhs = ((0, dgate), (1, dup))[buf == "up"]
            wgu[which, :, c:c + w] = nn(lt_n[order], rhs[:, c:c + w]).astype(BF)
            begin(name)

    def weights_out():
        lt[0] = nt(perm[...], mb_ref[...]).astype(BF)
        gout[...] = nn(lt[0], mix[...]).astype(BF)
        begin("a3")

    def norm_back(grads, values, gain):
        inverse = lax.rsqrt(jnp.mean(values * values, axis=-1, keepdims=True) + EPS)
        scaled = values * inverse
        weighted = grads * gain
        back = inverse * (weighted - scaled * jnp.mean(weighted * scaled, axis=-1, keepdims=True))
        return back, grads * scaled

    loads[5].wait()

    def backward(turn_now, _):
        chain = pl.when(turn_now == 0)
        weights = pl.when(turn_now == pipe)

        @chain
        def _():
            @pl.when(pipe == 0)
            def _():
                pass_x[0].start()
                pass_x[1].start()

        @weights
        def _():
            turned = nt(perm[...], n2[...])
            lt_n[0] = turned.astype(BF)
            lt_n[1] = reordered(turned)
            lt_n[2] = n2[...].astype(F32).T.astype(BF)

        @chain
        def _():
            @pl.when(pipe == 0)
            def _():
                pass_g.wait_recv()
                share_g.start()
                share_g.wait()

        weights(weights_down)

        @chain
        def _():
            def scale(c, w, gh):
                dgate[:, c:c + w] = (gh * dgate[:, c:c + w].astype(F32)).astype(BF)
                dup[:, c:c + w] = (gh * dup[:, c:c + w].astype(F32)).astype(BF)

            @pl.when(pipe == 0)
            def _():
                for c, w in TILES:
                    scale(c, w, nt(gbuf[...].reshape(ROWS, D), wd[c:c + w, :]))

            @pl.when(pipe == 1)
            def _():
                for c, w in TILES:
                    scale(c, w, gdown[:ROWS, c:c + w].astype(F32))

            for c, w in WIDE:
                e1s[:, c:c + w] = (nt(dgate[...], wgu[0, c:c + w, :]) + nt(dup[...], wgu[1, c:c + w, :])).astype(BF)
            swap_3.start()

        weights(weights_gate_up)

        @chain
        def _():
            swap_3.wait()
            grads = e1s[...].astype(F32) + e1r[...].astype(F32)
            back, terms = norm_back(grads, middle[...].reshape(ROWS, D), gain_2)
            row = lax.broadcasted_iota(jnp.int32, (ROWS, 1), 0)
            mine = ((row >> 6) & 1) == t
            small_in[0, 0] = jnp.zeros((8, D), F32)
            small_in[0, 0, 1:2, :] = jnp.sum(jnp.where(mine, terms, 0.0), axis=0, keepdims=True)
            grad_mid = gbuf[...].reshape(ROWS, D).astype(F32) + back
            gmid[...] = grad_mid.reshape(MICRO, 2, OWN, D)
            mb_ref[...] = grad_mid.astype(BF)

        weights(weights_out)
        chain(attention_back)
        return 0

    def attention_back():
        gmix = nt(mb_ref[...], wo[...]).astype(BF)
        for m in range(MICRO):
            blocks = [gmix[m * CAP:(m + 1) * CAP, j * 128:(j + 1) * 128] for j in range(4)]
            q_even = qb[m].reshape(4 * CAP, 128)
            q_odd = qb[m, :3].reshape(3 * CAP, 128)
            out = []
            for parity, queries, count in ((0, q_even, 4), (1, q_odd, 3)):
                gm = jnp.concatenate(blocks[:count], axis=0)
                p = pmat[m, pl.ds(4 * parity, count)].reshape(count * CAP, CAP)
                gp = nt(gm, vb[m, parity])
                ds = (p * (gp - jnp.sum(p * gp, axis=-1, keepdims=True))).astype(BF)
                out.append((nn(ds, kb[m, parity]), tn(ds, queries), tn(p.astype(BF), gm)))
            keys = pltpu.roll(out[0][1], 64, 1) + out[1][1]
            values = out[0][2] + pltpu.roll(out[1][2], 64, 1)
            rows = pl.ds(m * CAP, CAP)
            for j in range(4):
                block = out[0][0][j * CAP:(j + 1) * CAP]
                if j < 3:
                    block = block + out[1][0][j * CAP:(j + 1) * CAP]
                else:
                    block = jnp.where(half_lane < 64, block, keys)
                block = block * HEAD ** (-0.5)
                block = block * cs[m, 0] - turn(block, half_lane) * cs[m, 1]
                if j == 3:
                    gqkv[rows, 512:640] = pltpu.roll(jnp.where(half_lane < 64, values, block), 64, 1).astype(BF)
                    block = jnp.where(half_lane < 64, block, 0.0)
                gqkv[rows, j * 128:(j + 1) * 128] = block.astype(BF)
        for c, w in WIDE:
            part[:, :, :, c:c + w] = (
                nn(gqkv[:, :512], wq[:, c:c + w]) + nt(gqkv[:, 512:], wkv[c:c + w, :])).reshape(MICRO, 2, OWN, w)
        e2s[...] = part[:, other].astype(BF)
        swap_4.start()
        swap_4.wait()
        grads = (part[:, t] + e2r[...].astype(F32)).reshape(MICRO * OWN, D)
        back, terms = norm_back(grads, xbuf[:, t].astype(F32).reshape(MICRO * OWN, D), gain_1)
        total = gmid[:, t] + back.reshape(MICRO, OWN, D)
        rows_ref[1] = total

        @pl.when(pipe == 0)
        def _():
            pass_x[0].wait_send()
            pass_x[1].wait_send()

        pipe_out[...] = total.astype(BF)

        @pl.when(pipe == 1)
        def _():
            pass_g.start()

        small_in[0, 0, 0:1, :] = jnp.sum(terms, axis=0, keepdims=True)
        bias = jnp.sum(gqkv[...].astype(F32), axis=0, keepdims=True)
        wide = jnp.concatenate([bias[:, :512], jnp.zeros((1, D - 512), F32)], axis=1)
        small_in[0, 0, 2:3, :] = jnp.where(t == 0, wide, pltpu.roll(wide, QW, 1))
        for c in range(2):
            small_in[0, 0, 3 + c:4 + c, :128] = jnp.where(t == c, bias[:, 512:], 0.0)

    lax.fori_loop(0, 2, backward, 0)
    lt[1] = nt(perm[...], n1[...]).astype(BF)
    gqkv_w[...] = nn(lt[1], gqkv[...]).astype(BF)
    begin("a4")

    for step, event in enumerate(SERVICE):
        if step % 4 == 0 and step < 28:
            small_step(step // 4)
        serve(*event.split(":"))
    for name in NAMES:
        for stage in range(2):
            for k in range(6):
                ring_copy(name, stage, k).wait_send()
        x_copy(name).wait_send()
    for k in range(6):
        small_copy(k).wait_send()

    @pl.when(pipe == 1)
    def _():
        pass_g.wait_send()


def run_train(lens, x, cot, g1, g2, bq, bkv, wq, wkv, wo, wgu, wd):
    vmem = pl.BlockSpec(memory_space=VMEM)
    hbm = pl.BlockSpec(memory_space=pl.ANY)
    dma = pltpu.SemaphoreType.DMA
    return pl.pallas_call(
        train_kernel,
        out_shape=(
            jax.ShapeDtypeStruct((40, COLS_AB + COLS_C), F32),
            jax.ShapeDtypeStruct((2, MICRO, OWN, D), F32),
        ),
        in_specs=[pl.BlockSpec(memory_space=pltpu.SMEM)] + [vmem] * 7 + [hbm] * 6,
        out_specs=(vmem,) * 2,
        scratch_shapes=[
            VMEM((512, D), BF), VMEM((D, 128), BF), VMEM((512, D), BF), VMEM((2, D, FH), BF), VMEM((FH, D), BF), VMEM((D, D), BF),
            VMEM((MICRO, 2, OWN, D), BF), VMEM((MICRO, 2, OWN, D), BF),
            VMEM((ROWS, D), BF), VMEM((ROWS, D), BF),
            VMEM((MICRO, OWN, D), BF), VMEM((MICRO, OWN, D), BF), VMEM((MICRO, OWN, D), BF),
            VMEM((ROWS, D), BF), VMEM((ROWS, D), BF),
            VMEM((MICRO, 4, CAP, 128), BF), VMEM((MICRO, 2, CAP, 128), BF), VMEM((MICRO, 2, CAP, 128), BF),
            VMEM((MICRO, 7, CAP, CAP), F32), VMEM((ROWS, 512), BF), VMEM((MICRO, 2, OWN, D), F32),
            VMEM((ROWS, FH), BF), VMEM((ROWS, FH), BF), VMEM((ROWS, FH), BF),
            VMEM((3, D, ROWS), BF), VMEM((MICRO, 2, OWN, D), F32), VMEM((MICRO, 2, OWN, D), F32),
            VMEM((MICRO, 3, CAP, 128), F32), VMEM((MICRO, CAP, CAP), F32), VMEM((ROWS, 640), BF),
            VMEM((3, D, ROWS), BF), VMEM((ROWS, D), BF), VMEM((D, FH), BF), VMEM((D, 512), BF), VMEM((D, 640), BF),
            VMEM((2, 112, COLS_AB), BF), VMEM((2, 2, 112, COLS_AB), BF),
            VMEM((4, 64, COLS_AB), BF), VMEM((2, 32, COLS_AB), BF), VMEM((2, 2, 32, COLS_AB), BF),
            VMEM((32, COLS_AB), BF), VMEM((32, COLS_AB), BF),
            VMEM((448, COLS_C), BF), VMEM((112, COLS_C), BF), VMEM((2, 112, COLS_C), BF),
            VMEM((4, 32, COLS_C), BF), VMEM((32, COLS_C), BF), VMEM((2, 32, COLS_C), BF),
            VMEM((2, 6, 8, D), F32),
            dma((6,)), dma((10,)), dma((10,)), dma((len(NAMES), 13)), dma((len(NAMES), 13)), dma((6,)), dma((6,)),
        ],
        compiler_params=pltpu.CompilerParams(collective_id=0, has_side_effects=True, vmem_limit_bytes=63 * MIB),
        name="train",
    )(lens, x, cot, g1, g2, bq, bkv, jnp.asarray(rope_table()), wq, wkv, wo, wgu, wd, jnp.asarray(row_order()))


def place_kernel(
    sums_ref, rows_ref,
    so_ref, ig_ref, gain1_ref, gq_ref, bq_ref, gkv_ref, bkv_ref, go_ref, gain2_ref, ggu_ref, gd_ref,
):
    so_ref[...] = rows_ref[0].astype(BF)
    ig_ref[...] = rows_ref[1]
    gain1_ref[...] = sums_ref[32:33, :D]
    gain2_ref[...] = sums_ref[33:34, :D]
    bq_ref[...] = sums_ref[34:35, :D]
    bkv_ref[...] = sums_ref[35:37, :128]
    gq_ref[:, 0, :] = sums_ref[:28, 3200:3200 + QW]
    gkv_ref[:, 0, :] = sums_ref[:28, 3712:3840]
    go_ref[:, 0, :] = sums_ref[:28, 2688:2688 + QW]
    for ref, names in ((gd_ref.at[:, 0], "a0 b0 c0 c1"), (ggu_ref.at[:, 0], "a1 a2 c2"), (ggu_ref.at[:, 1], "b1 b2 c3")):
        for name in names.split():
            _, c, w, at = PIECES[name]
            at = at + COLS_AB * (name[0] == "c")
            ref[:, c:c + w] = sums_ref[:28, at:at + w]


def run_place(*arrays):
    vmem = pl.BlockSpec(memory_space=VMEM)
    shapes = (
        (MICRO, OWN, D), (MICRO, OWN, D), (1, D), (28, 1, QW), (1, D), (28, 1, 128), (2, 128),
        (28, 1, QW), (1, D), (28, 2, FH), (28, 1, FH),
    )
    return pl.pallas_call(
        place_kernel,
        out_shape=tuple(jax.ShapeDtypeStruct(s, F32 if i else BF) for i, s in enumerate(shapes)),
        in_specs=[vmem] * 2,
        out_specs=(vmem,) * 11,
        compiler_params=pltpu.CompilerParams(vmem_limit_bytes=60 * MIB),
        name="place",
    )(*arrays)


def body(
    inputs, cotangent, lengths, gain_attn, w_query, b_query, w_keyval, b_keyval, w_out, gain_mlp, w_gate_up, w_down,
):
    outs = run_train(
        lengths[:, 0], inputs, cotangent, gain_attn, gain_mlp, b_query, b_keyval[0],
        jnp.swapaxes(w_query[0], 0, 1), w_keyval[0, :, 0], w_out[0],
        jnp.swapaxes(w_gate_up[0], 0, 1), w_down[0],
    )
    so, ig, gain1, gq, bq, gkv, bkv, go, gain2, ggu, gd = run_place(*outs)
    return (
        so[None], ig[None], gain1, jnp.swapaxes(gq, 0, 1), bq, gkv[None], bkv[None],
        jnp.transpose(go, (1, 2, 0)), gain2, ggu[None], jnp.transpose(gd, (1, 2, 0)),
    )


def solution(mesh):
    placed = (
        P(None, ("dp", "tensor"), None),
        P(None, ("dp", "tensor"), None),
        P(None, "dp", None),
        P("pipe", None),
        P("pipe", None, "tensor"),
        P("pipe", "tensor"),
        P("pipe", None, "tensor", None),
        P("pipe", "tensor", None),
        P("pipe", "tensor", None),
        P("pipe", None),
        P("pipe", None, None, "tensor"),
        P("pipe", "tensor", None),
    )
    return jax.shard_map(
        body,
        mesh=mesh,
        in_specs=placed,
        out_specs=(
            P("pipe", None, ("dp", "tensor"), None),
            P("pipe", None, ("dp", "tensor"), None),
            P("pipe", None),
            P("pipe", "dp", "tensor"),
            P("pipe", None),
            P("pipe", "dp", "tensor", None),
            P("pipe", None, None),
            P("pipe", "tensor", "dp"),
            P("pipe", None),
            P("pipe", "dp", None, "tensor"),
            P("pipe", "tensor", "dp"),
        ),
        check_vma=False,
    )
```
